32 devices in a mesh: stream: 2 (over x), frames: 16 (over z, y, core).
Axes of the slice: x: 2, y: 2, z: 4, core: 2. Of those that a mesh axis runs over, the one named last changes fastest.
Arguments:
- tokens: bfloat16 [2, 2048, 8, 1024], P('stream', 'frames'), may hold values from -6 to 6
- context: bfloat16 [2048, 1024], P('frames', 'stream'), may hold values from -6 to 6
- ctx_weight: bfloat16 [1024, 1024], P(('stream', 'frames')), may hold values from -0.1875 to 0.1875
- delay: int32 [8], replicated, may hold values from 0 to 2, as said below
- lengths: int32 [3], replicated, may hold values from 1 to 1024, 2048 in all
- attn_gain: bfloat16 [2, 8, 1024], P('stream'), may hold values from 0.5 to 1.5
- ffn_gain: bfloat16 [2, 8, 1024], P('stream'), may hold values from 0.5 to 1.5
- qkv_weight: bfloat16 [2, 1024, 3072], P('stream', 'frames'), may hold values from -0.1875 to 0.1875
- out_weight: bfloat16 [2, 1024, 1024], P('stream', 'frames'), may hold values from -0.375 to 0.375
- gate_weight: bfloat16 [2, 1024, 2816], P('stream', 'frames'), may hold values from -0.1875 to 0.1875
- up_weight: bfloat16 [2, 1024, 2816], P('stream', 'frames'), may hold values from -0.1875 to 0.1875
- down_weight: bfloat16 [2, 2816, 1024], P('stream', 'frames'), may hold values from -0.1875 to 0.1875
- cotangent: bfloat16 [2, 2048, 8, 1024], P('stream', 'frames'), may hold values from -6 to 6
Outputs:
- mixed_out: bfloat16 [2, 2048, 8, 1024], P('stream', 'frames')
- d_tokens: float32 [2, 2048, 8, 1024], P('stream', 'frames')
- d_context: float32 [2048, 1024], P('frames', 'stream')
- d_ctx_weight: float32 [1024, 1024], P(('stream', 'frames'))
- d_attn_gain: float32 [2, 8, 1024], P('stream')
- d_ffn_gain: float32 [2, 8, 1024], P('stream')
- d_qkv: float32 [2, 1024, 3072], P('stream', 'frames')
- d_out: float32 [2, 1024, 1024], P('stream', 'frames')
- d_gate: float32 [2, 1024, 2816], P('stream', 'frames')
- d_up: float32 [2, 1024, 2816], P('stream', 'frames')
- d_down: float32 [2, 2816, 1024], P('stream', 'frames')
The draws below stay inside these ranges and needn't reach their ends.
Inputs may be any that keep to these rules, and one draw needn't show every extreme that they name: Position 0 has delay 0, position 7 has delay 2, every other position 1 or 2. Item lengths in frames, in order, summing to 2048; the longest has 1024.
All inputs are finite; a program needn't handle non-finite values.
Results may differ from the reference program's by a relative error of at most 0.014.
Values may be sent and summed in bfloat16 or wider, within the bound.
A program may use at most 256 MiB of HBM per device.

```python
import math
import jax
import jax.numpy as jnp
import numpy as np
from jax import lax

D = 1024
HEADS = 16
HEAD = 64
FF = 2816
POS = 8
FRAMES = 2048
ITEM_MAX = 1024
ITEMS = 3


def draw_delay(key, part):
    key = jax.random.fold_in(key, 11)
    shifts = jax.random.randint(key, (POS,), 1, 3)
    shifts = shifts.at[0].set(0)
    shifts = shifts.at[POS - 1].set(2)
    return shifts.astype(jnp.int32)


def level_of(key, extent, split, least, high):
    factor_of, own = 1.0, jax.random.fold_in(key, 6)
    for dim, shards_of in split:
        draws = jnp.exp(jax.random.uniform(jax.random.fold_in(own, dim), (shards_of,), jnp.float32, least / len(split), high / len(split)))
        factor_of = factor_of * jnp.repeat(draws, extent[dim] // shards_of).reshape([-1 if axis == dim else 1 for axis in range(len(extent))])
    return factor_of


def length_profile(count, total, bound, skew):
    weights = [(1 << 20) // math.isqrt(rank ** skew) + 1 for rank in range(2, count + 1)]
    spare, given = total - bound - (count - 1), [1] * (count - 1)
    while spare > 0:
        movable = [i for i in range(count - 1) if given[i] < bound]
        whole, budget = sum([weights[i] for i in movable]), spare
        for i in movable:
            extra = min(bound - given[i], max(1, budget * weights[i] // whole), spare)
            given[i] = given[i] + extra
            spare = spare - extra
    return np.array([bound] + given)


def ragged(rng, count, total, most, slope):
    if count == 2:
        one = jax.random.randint(rng, (), max(1, total - most), min(most, total - 1) + 1)
        return jnp.stack([one, total - one])
    sizes = jnp.asarray(length_profile(count, total, most, slope), jnp.int32)
    twos = (count - 1) // 2
    source_of, receiver = sizes[1:1 + 2 * twos:2], sizes[2:2 + 2 * twos:2]
    room = jnp.minimum(source_of - 1, most - receiver)
    shifted = jax.random.randint(jax.random.fold_in(rng, 1), (twos,), 0, 1 << 20) % (room + 1)
    sizes = sizes.at[1:1 + 2 * twos:2].set(source_of - shifted).at[2:2 + 2 * twos:2].set(receiver + shifted)
    return sizes[jax.random.permutation(jax.random.fold_in(rng, 2), count)]


def scatter_about(own_key, extent, width, most, pieces=(), kind=jnp.bfloat16):
    drawn = jax.random.normal(own_key, extent, jnp.float32) * width
    if len(pieces) > 0:
        drawn = level_of(own_key, extent, pieces, -0.22, 0.18) * drawn
    return jnp.clip(drawn, min=-most, max=most).astype(kind)


def setup_inputs(seed: int = 0) -> dict:
    splits = jax.random.split(jax.random.key(seed), 14)
    tokens = scatter_about(splits[0], (2, FRAMES, POS, D), 1.0, 6.0, ((0, 2), (1, 16)))
    context = scatter_about(splits[1], (FRAMES, D), 1.0, 6.0, ((0, 16), (1, 2)))
    ctx_weight = scatter_about(splits[2], (D, D), D ** -0.5, 0.1875, ((0, 32),))
    delay = draw_delay(jax.random.fold_in(splits[13], 71), 0)
    lengths = ragged(splits[4], ITEMS, FRAMES, ITEM_MAX, 0).astype(jnp.int32)
    attn_gain = jnp.clip(1.0 + 0.1 * jax.random.normal(splits[5], (2, POS, D), jnp.float32), 0.5, 1.5).astype(jnp.bfloat16)
    ffn_gain = jnp.clip(1.0 + 0.1 * jax.random.normal(splits[6], (2, POS, D), jnp.float32), 0.5, 1.5).astype(jnp.bfloat16)
    qkv_weight = scatter_about(splits[7], (2, D, 3 * D), D ** -0.5, 0.1875, ((0, 2), (1, 16)))
    out_weight = scatter_about(splits[8], (2, D, D), (D // 4) ** -0.5, 0.375, ((0, 2), (1, 16)))
    gate_weight = scatter_about(splits[9], (2, D, FF), D ** -0.5, 0.1875, ((0, 2), (1, 16)))
    up_weight = scatter_about(splits[10], (2, D, FF), D ** -0.5, 0.1875, ((0, 2), (1, 16)))
    down_weight = scatter_about(splits[11], (2, FF, D), (FF // 3) ** -0.5, 0.1875, ((0, 2), (1, 16)))
    cotangent = scatter_about(splits[12], (2, FRAMES, POS, D), 1.0, 6.0, ((0, 2), (1, 16)))
    return {"tokens": tokens, "context": context, "ctx_weight": ctx_weight, "delay": delay, "lengths": lengths, "attn_gain": attn_gain, "ffn_gain": ffn_gain, "qkv_weight": qkv_weight, "out_weight": out_weight, "gate_weight": gate_weight, "up_weight": up_weight, "down_weight": down_weight, "cotangent": cotangent}


@jax.custom_vjp
def low(v):
    return lax.optimization_barrier(v.astype(jnp.bfloat16)).astype(jnp.float32)

@jax.custom_vjp
def low_back(v):
    return v

def low_keep(v):
    return (low(v), None)

def low_pass(kept, grad):
    return (grad,)

def back_keep(v):
    return (v, None)

def back_low(kept, grad):
    return (low(grad),)
low.defvjp(low_keep, low_pass)
low_back.defvjp(back_keep, back_low)
epsilon = 1e-05

def matmul_high(left, right):
    return jnp.dot(left, right, precision=lax.Precision.HIGHEST, preferred_element_type=jnp.float32)

def norm_rows(rows, gain):
    return rows * lax.rsqrt(lax.optimization_barrier(jnp.mean(rows * rows, axis=-1, keepdims=True)) + epsilon) * gain

def shift_tables(delay, lengths, frame_ids):
    starts = (jnp.cumsum(lengths) - lengths).astype(jnp.int32)
    at_start = jnp.any(frame_ids[:, None] == starts[None, :], axis=1)
    after_start = jnp.any(frame_ids[:, None] - 1 == starts[None, :], axis=1)
    keep_one = jnp.logical_not(at_start)
    keep_two = jnp.logical_and(keep_one, jnp.logical_not(after_start))
    valid_rows = jnp.stack([jnp.ones_like(keep_one), keep_one, keep_two]).astype(jnp.float32)
    chosen = (delay[None, :] == jnp.arange(3, dtype=jnp.int32)[:, None]).astype(jnp.float32)
    return (chosen, valid_rows)

def delay_input(rows, chosen, valid_rows):
    frame_count = rows.shape[0]
    padded = jnp.pad(rows, ((2, 0), (0, 0), (0, 0)))
    summed = jnp.zeros_like(rows)
    for offset in range(3):
        piece = padded[2 - offset:2 - offset + frame_count]
        summed = summed + chosen[offset][None, :, None] * valid_rows[offset][:, None, None] * piece
    return summed

def block_layer(layer_in, weights):
    qkv_weight, out_weight, gate_weight, up_weight, down_weight, attn_gain, ffn_gain = weights
    frame_count = layer_in.shape[0]
    token_rows = frame_count * POS
    normed = low(norm_rows(layer_in, attn_gain)).reshape(token_rows, D)
    qkv = low_back(low(matmul_high(normed, qkv_weight))).reshape(frame_count, POS, 3, HEADS, HEAD)
    queries = qkv[:, :, 0]
    key_part = qkv[:, :, 1]
    values = qkv[:, :, 2]
    scores = jnp.einsum('fqhd,fkhd->fhqk', queries, key_part, precision=lax.Precision.HIGHEST)
    scores = low_back(scores * HEAD ** (-0.5))
    causal = jnp.arange(POS)[:, None] >= jnp.arange(POS)[None, :]
    scores = jnp.where(causal[None, None], scores, -1e+30)
    probs = low(jax.nn.softmax(scores, axis=-1))
    mixed = jnp.einsum('fhqk,fkhd->fqhd', probs, values, precision=lax.Precision.HIGHEST)
    mixed = low_back(low(mixed)).reshape(token_rows, D)
    after_attn = layer_in + low_back(matmul_high(mixed, out_weight)).reshape(frame_count, POS, D)
    normed_two = low(norm_rows(after_attn, ffn_gain)).reshape(token_rows, D)
    gate_pre = low_back(matmul_high(normed_two, gate_weight))
    up_pre = low_back(matmul_high(normed_two, up_weight))
    hidden = low(jax.nn.silu(gate_pre) * up_pre)
    return after_attn + low_back(matmul_high(hidden, down_weight)).reshape(frame_count, POS, D)

def forward(tokens, context, ctx_weight, attn_gain, ffn_gain, qkv_weight, out_weight, gate_weight, up_weight, down_weight, chosen, valid_rows):
    shift_term = low_back(matmul_high(context, ctx_weight))
    block_frames = min(512, FRAMES)
    results = []
    for stream_index in range(2):
        layer_in = delay_input(tokens[stream_index], chosen, valid_rows) + shift_term[:, None, :]
        blocks = layer_in.reshape(FRAMES // block_frames, block_frames, POS, D)
        weights = (qkv_weight[stream_index], out_weight[stream_index], gate_weight[stream_index], up_weight[stream_index], down_weight[stream_index], attn_gain[stream_index], ffn_gain[stream_index])

        def run_block(frame_block, weights=weights):
            return block_layer(frame_block, weights)
        outputs = lax.map(jax.checkpoint(run_block), blocks)
        results.append(outputs.reshape(FRAMES, POS, D))
    return jnp.stack(results)

def reference(tokens, context, ctx_weight, delay, lengths, attn_gain, ffn_gain, qkv_weight, out_weight, gate_weight, up_weight, down_weight, cotangent):
    floats = [array.astype(jnp.float32) for array in (tokens, context, ctx_weight, attn_gain, ffn_gain, qkv_weight, out_weight, gate_weight, up_weight, down_weight)]
    frame_ids = jnp.arange(FRAMES, dtype=jnp.int32)
    chosen, valid_rows = shift_tables(delay, lengths, frame_ids)

    def wrapped(*arrays):
        return forward(*arrays, chosen, valid_rows)
    mixed_out, pullback = jax.vjp(wrapped, *floats)
    grads = pullback(cotangent.astype(jnp.float32))
    return (mixed_out.astype(jnp.bfloat16), grads[0], grads[1], grads[2], grads[3], grads[4], grads[5], grads[6], grads[7], grads[8], grads[9])
```

```python
import jax
import jax.numpy as jnp
from jax import lax
from jax.experimental import pallas as pl
from jax.experimental.pallas import tpu as pltpu
from jax.sharding import PartitionSpec as P

HEADS = 16
HEAD = 64


epsilon = 1e-05


def shifted(x, axis, by):
    length = lax.axis_size(axis)
    pairs = [(i, i + by) for i in range(length) if 0 <= i + by < length]
    return lax.ppermute(x, axis, pairs)


def flat_dot(left, right):
    return jnp.dot(left, right, preferred_element_type=jnp.float32)


def trans_dot(left, right):
    return lax.dot_general(
        left, right, (((0,), (0,)), ((), ())), preferred_element_type=jnp.float32
    )


def back_dot(left, right):
    return lax.dot_general(
        left, right, (((1,), (1,)), ((), ())), preferred_element_type=jnp.float32
    )


def norm_rows(rows, gain):
    return rows * lax.rsqrt(jnp.mean(rows * rows, axis=-1, keepdims=True) + epsilon) * gain


def norm_back(grad_normed, rows, gain):
    scale = lax.rsqrt(jnp.mean(rows * rows, axis=-1, keepdims=True) + epsilon)
    unit = rows * scale
    grad_gain = jnp.sum(grad_normed * unit, axis=0)
    grad_unit = grad_normed * gain
    grad_rows = scale * (grad_unit - unit * jnp.mean(grad_unit * unit, axis=-1, keepdims=True))
    return (grad_rows, grad_gain)


def shift_tables(delay, lengths, frame_ids):
    starts = jnp.cumsum(lengths) - lengths
    at_start = jnp.any(frame_ids[:, None] == starts[None, :], axis=1)
    after_start = jnp.any(frame_ids[:, None] - 1 == starts[None, :], axis=1)
    keep_one = jnp.logical_not(at_start)
    keep_two = jnp.logical_and(keep_one, jnp.logical_not(after_start))
    valid_rows = jnp.stack([jnp.ones_like(keep_one), keep_one, keep_two]).astype(jnp.float32)
    chosen = (delay[None, :] == jnp.arange(3, dtype=jnp.int32)[:, None]).astype(jnp.float32)
    return (chosen, valid_rows)


MESH = pl.DeviceIdType.MESH
CHUNKS = 17
FEED = 11
WIDE = 768
ROUNDS = 4


def mm(a, b):
    return jnp.dot(a, b, preferred_element_type=jnp.float32)


def nt(a, b):
    return lax.dot_general(a, b, (((1,), (1,)), ((), ())), preferred_element_type=jnp.float32)


def tn(a, b):
    return lax.dot_general(a, b, (((0,), (0,)), ((), ())), preferred_element_type=jnp.float32)


def either(cond, fn):
    if isinstance(cond, bool):
        if cond:
            fn()
    else:
        pl.when(cond)(fn)


def within(t, low, high):
    if isinstance(t, int):
        return low <= t < high
    return jnp.logical_and(t >= low, t < high)


def layer_kernel(
    tok,
    ctx,
    gains,
    cot,
    w_own,
    mixed_hbm,
    gin_hbm,
    dctx,
    gain_out,
    dw_hbm,
    gathered,
    lin,
    n1,
    n1t,
    qkv,
    mixed,
    mixt,
    aft,
    n2,
    n2t,
    oacc,
    gn,
    wbuf,
    part,
    gg,
    hidt,
    shift,
    bias,
    gacc,
    gsend,
    grecv,
    xsend,
    xrecv,
    r_c,
    r_y,
    r_zl,
    r_zh,
    t_keep,
    t_send,
    u_keep,
    u_send,
    v_keep,
    v_send,
    fin,
    ag_ss,
    ag_rs,
    rs_ss,
    rs_rs,
    x_ss,
    x_rs,
    g_ss,
    g_rs,
    own_sem,
    load_sem,
    fin_sem,
    out_sem,
):
    s = lax.axis_index("stream")
    f = lax.axis_index("frames")
    c = f % 2
    y = (f // 2) % 2
    zl = (f // 4) % 2
    zh = f // 8
    d_c = (s, f + 1 - 2 * c)
    d_y = (s, f + 2 - 4 * y)
    d_zl = (s, f + 4 - 8 * zl)
    d_zh = (s, f + 8 - 16 * zh)
    d_x = (1 - s, f)
    partners = (d_zh, d_zl, d_y, d_c)

    own_copy = pltpu.make_async_copy(w_own, gathered.at[:, zh, zl, y, c], own_sem)
    own_copy.start()

    barrier = pltpu.get_barrier_semaphore()
    for device in partners + (d_x,):
        pl.semaphore_signal(barrier, inc=1, device_id=device, device_id_type=MESH)
    pl.semaphore_wait(barrier, 5)

    def remote(src, dst, ss, rs, device):
        return pltpu.make_async_remote_copy(
            src_ref=src, dst_ref=dst, send_sem=ss, recv_sem=rs, device_id=device, device_id_type=MESH
        )

    def ag_copy(stage, k):
        if stage == 0:
            src = dst = gathered.at[k, zh, zl, y, c]
        elif stage == 1:
            src = dst = gathered.at[k, :, zl, y, c]
        elif stage == 2:
            src = dst = gathered.at[k, :, :, y, c]
        else:
            src = dst = gathered.at[k, :, :, :, c]
        return remote(src, dst, ag_ss.at[stage, k], ag_rs.at[stage, k], partners[stage])

    def ag_tick(t):
        for stage in range(4):
            def step(stage=stage):
                k = t - stage
                if stage > 0:
                    ag_copy(stage - 1, k).wait_recv()
                ag_copy(stage, k).start()
            either(within(t, stage, stage + CHUNKS), step)
        def ready():
            ag_copy(3, t - 4).wait_recv()
        either(within(t, 4, 4 + CHUNKS), ready)

    def load(k, slot):
        cp = pltpu.make_async_copy(gathered.at[k], wbuf.at[slot], load_sem.at[slot])
        cp.start()
        cp.wait()

    def rs_copy(stage, r):
        two, four = r % 2, r % ROUNDS
        if stage == 0:
            src, dst = part.at[two, :, :, :, 1 - c], r_c.at[four]
        elif stage == 1:
            src, dst = t_send.at[two], r_y.at[four]
        elif stage == 2:
            src, dst = u_send.at[two], r_zl.at[four]
        else:
            src, dst = v_send.at[two], r_zh.at[four]
        return remote(src, dst, rs_ss.at[stage, two], rs_rs.at[stage, four], partners[3 - stage])

    def add(a, b):
        return a.astype(jnp.float32) + b.astype(jnp.float32)

    def fin_copy(r):
        return pltpu.make_async_copy(fin.at[r % 2], dw_hbm.at[r], fin_sem.at[r % 2])

    def rs_tick(r, static_first=False):
        def start_c():
            rs_copy(0, r).start()
        either(within(r, 0, CHUNKS), start_c)

        def stage_y():
            k = r - 1
            rs_copy(0, k).wait_recv()
            either(within(k, 2, CHUNKS), lambda: rs_copy(1, k - 2).wait_send())
            two, four = k % 2, k % ROUNDS
            def piece(i, _):
                a, b = i // 2, i % 2
                t_send[two, i] = add(part[two, a, b, 1 - y, c], r_c[four, a, b, 1 - y]).astype(jnp.bfloat16)
                t_keep[two, i] = add(part[two, a, b, y, c], r_c[four, a, b, y]).astype(jnp.bfloat16)
                return 0
            lax.fori_loop(0, 4, piece, 0)
            rs_copy(1, k).start()
        either(within(r, 1, CHUNKS + 1), stage_y)

        def stage_zl():
            k = r - 2
            rs_copy(1, k).wait_recv()
            either(within(k, 2, CHUNKS), lambda: rs_copy(2, k - 2).wait_send())
            two, four = k % 2, k % ROUNDS
            for a in range(2):
                far, near = a * 2 + 1 - zl, a * 2 + zl
                u_send[two, a] = add(t_keep[two, far], r_y[four, far]).astype(jnp.bfloat16)
                u_keep[two, a] = add(t_keep[two, near], r_y[four, near]).astype(jnp.bfloat16)
            rs_copy(2, k).start()
        either(within(r, 2, CHUNKS + 2), stage_zl)

        def stage_zh():
            k = r - 3
            rs_copy(2, k).wait_recv()
            either(within(k, 2, CHUNKS), lambda: rs_copy(3, k - 2).wait_send())
            two, four = k % 2, k % ROUNDS
            v_send[two] = add(u_keep[two, 1 - zh], r_zl[four, 1 - zh]).astype(jnp.bfloat16)
            v_keep[two] = add(u_keep[two, zh], r_zl[four, zh]).astype(jnp.bfloat16)
            rs_copy(3, k).start()
        either(within(r, 3, CHUNKS + 3), stage_zh)

        def last():
            k = r - 4
            rs_copy(3, k).wait_recv()
            either(within(k, 2, CHUNKS), lambda: fin_copy(k - 2).wait())
            fin[k % 2] = add(v_keep[k % 2], r_zh[k % ROUNDS])
            fin_copy(k).start()
        either(within(r, 4, CHUNKS + 4), last)

    def part_free(r):
        either(within(r, 2, CHUNKS), lambda: rs_copy(0, r - 2).wait_send())

    row_id = lax.broadcasted_iota(jnp.int32, (128, 256), 0)
    col_id = lax.broadcasted_iota(jnp.int32, (128, 256), 1) % 128
    seen = jnp.logical_and(row_id // 8 == col_id // 8, col_id <= row_id)
    bias[...] = jnp.where(seen, 0.0, -1e30)

    def zero_gain(i, _):
        gacc[...] = jnp.zeros_like(gacc)
        return 0
    lax.fori_loop(0, 1, zero_gain, 0)

    ag_tick_first(ag_tick, own_copy)

    load(0, 0)
    half = shift.shape[1] // 2
    for h in range(2):
        w_half = wbuf[0, :, :, :, :, h * 32 : h * 32 + 32, 0:512].reshape(512, 512)
        shift[:, h * half : (h + 1) * half] = mm(ctx[...], w_half)
    xsend[0] = shift[...].astype(jnp.bfloat16)

    def x_copy(i):
        return remote(xsend.at[i], xrecv.at[i], x_ss.at[i], x_rs.at[i], d_x)

    x_copy(0).start()
    ag_tick(5)
    x_copy(0).wait_recv()
    shift[...] = shift[...] + xrecv[0].astype(jnp.float32)

    def rows_of(i, size):
        return pl.ds(pl.multiple_of(i * size, size), size)

    def norm1(i, _):
        rows = rows_of(i, 128)
        sh = shift[rows_of(i, 16), :]
        x = tok[rows, :].astype(jnp.float32).reshape(16, 8, 1024) + sh[:, None, :]
        r = lax.rsqrt(jnp.mean(x * x, axis=-1, keepdims=True) + epsilon)
        n = (x * r * gains[0][None]).reshape(128, 1024).astype(jnp.bfloat16)
        lin[rows, :] = x.reshape(128, 1024)
        n1[rows, :] = n
        n1t[:, rows] = n.T
        return 0

    lax.fori_loop(0, 8, norm1, 0)

    lane_low = lax.broadcasted_iota(jnp.int32, (128, 128), 1) < 64
    head_scale = HEAD ** (-0.5)

    def both(v):
        zero = jnp.zeros_like(v)
        return jnp.concatenate([jnp.where(lane_low, v, zero), jnp.where(lane_low, zero, v)], axis=0)

    def softmax(sc):
        parts = []
        for h in range(2):
            p = sc[:, h * 128 : h * 128 + 128]
            e = jnp.exp(p - jnp.max(p, axis=-1, keepdims=True))
            parts.append(e / jnp.sum(e, axis=-1, keepdims=True))
        return parts

    def attn_fwd(g):
        def rows_step(i, _):
            rows = rows_of(i, 256)
            for u in range(2):
                sub = rows_of(i * 2 + u, 128)
                for p in range(2):
                    lo = p * 128
                    q = qkv[g, sub, lo : lo + 128]
                    k = qkv[g, sub, 256 + lo : 384 + lo]
                    v = qkv[g, sub, 512 + lo : 640 + lo]
                    sc = nt(q, both(k)) * head_scale + bias[...]
                    pr = jnp.concatenate([x.astype(jnp.bfloat16) for x in softmax(sc)], axis=1)
                    out = mm(pr, both(v)).astype(jnp.bfloat16)
                    mixed[sub, pl.ds(pl.multiple_of(g * 256 + lo, 128), 128)] = out
            return 0
        lax.fori_loop(0, 4, rows_step, 0)

    def attn_bwd(g):
        def rows_step(i, _):
            for u in range(2):
                sub = rows_of(i * 2 + u, 128)
                for p in range(2):
                    lo = p * 128
                    q = qkv[g, sub, lo : lo + 128]
                    k = qkv[g, sub, 256 + lo : 384 + lo]
                    v = qkv[g, sub, 512 + lo : 640 + lo]
                    do = mixed[sub, pl.ds(pl.multiple_of(g * 256 + lo, 128), 128)]
                    kk = both(k)
                    sc = nt(q, kk) * head_scale + bias[...]
                    pr = softmax(sc)
                    dp = nt(do, both(v))
                    ds = []
                    for h in range(2):
                        d = dp[:, h * 128 : h * 128 + 128]
                        ds.append((pr[h] * (d - jnp.sum(d * pr[h], axis=-1, keepdims=True))).astype(jnp.bfloat16))
                    ds = jnp.concatenate(ds, axis=1)
                    pl_low = jnp.concatenate([x.astype(jnp.bfloat16) for x in pr], axis=1)
                    dq = mm(ds, kk) * head_scale
                    dk = tn(ds, q)
                    dv = tn(pl_low, do)
                    qkv[g, sub, lo : lo + 128] = dq.astype(jnp.bfloat16)
                    qkv[g, sub, 256 + lo : 384 + lo] = (
                        jnp.where(lane_low, dk[:128], dk[128:]) * head_scale
                    ).astype(jnp.bfloat16)
                    qkv[g, sub, 512 + lo : 640 + lo] = jnp.where(lane_low, dv[:128], dv[128:]).astype(jnp.bfloat16)
            return 0
        lax.fori_loop(0, 4, rows_step, 0)

    def qkv_group(g, _):
        either(g > 0, lambda: ag_tick(5 + g))
        load(1 + g, 0)
        def rows_step(i, _):
            rows = rows_of(i, 256)
            qkv[g, rows, :] = mm(n1[rows, :], wbuf[0].reshape(1024, WIDE)).astype(jnp.bfloat16)
            return 0
        lax.fori_loop(0, 4, rows_step, 0)
        attn_fwd(g)
        return 0

    lax.fori_loop(0, 4, qkv_group, 0)

    ag_tick(9)
    load(5, 0)
    load(0, 1)

    def after(i, _):
        rows = rows_of(i, 256)
        m = mixed[rows, :]
        a = lin[rows, 0:WIDE] + mm(m, wbuf[0].reshape(1024, WIDE))
        b = lin[rows, WIDE:1024] + mm(m, wbuf[1, :, :, :, :, :, 512:768].reshape(1024, 256))
        x = jnp.concatenate([a, b], axis=1)
        aft[rows, :] = x
        oacc[rows, :] = x
        x3 = x.reshape(32, 8, 1024)
        r = lax.rsqrt(jnp.mean(x3 * x3, axis=-1, keepdims=True) + epsilon)
        n = (x3 * r * gains[1][None]).reshape(256, 1024).astype(jnp.bfloat16)
        n2[rows, :] = n
        n2t[:, rows] = n.T
        mixt[:, rows] = m.T
        return 0

    lax.fori_loop(0, 4, after, 0)

    def feed(j, _):
        ag_tick(10 + j)
        load(6 + j, 0)
        part_free(j)
        two = j % 2

        def rows_step(i, _):
            rows = rows_of(i, 256)
            w_gu = wbuf[0, :, :, :, :, :, 0:512].reshape(1024, 512)
            pre = mm(n2[rows, :], w_gu)
            gate, up = pre[:, :256], pre[:, 256:]
            g_hid = jnp.zeros((256, 256), jnp.float32)
            for q in range(4):
                w_q = wbuf[0, :, :, :, :, q * 16 : q * 16 + 16, 512:768].reshape(256, 256)
                g_hid = g_hid + nt(cot[rows, q * 256 : q * 256 + 256], w_q)
            sig = jax.nn.sigmoid(gate)
            silu = gate * sig
            hid = (silu * up).astype(jnp.bfloat16)
            g_gate = (g_hid * up * sig * (1.0 + gate * (1.0 - sig))).astype(jnp.bfloat16)
            g_up = (g_hid * silu).astype(jnp.bfloat16)
            for q in range(4):
                w_q = wbuf[0, :, :, :, :, q * 16 : q * 16 + 16, 512:768].reshape(256, 256)
                oacc[rows, q * 256 : q * 256 + 256] += mm(hid, w_q)
            both_g = jnp.concatenate([g_gate, g_up], axis=1)
            gg[rows, :] = both_g
            hidt[:, rows] = hid.T
            back = nt(both_g, w_gu)
            @pl.when(j == 0)
            def _():
                gn[rows, :] = back
            @pl.when(j > 0)
            def _():
                gn[rows, :] += back
            return 0

        lax.fori_loop(0, 4, rows_step, 0)

        def weight_step(m, _):
            res = mm(n2t[rows_of(m, 256), :], gg[...]).astype(jnp.bfloat16).reshape(2, 2, 64, 512)
            part[two, m // 2, m % 2, :, :, :, 0:512] = res
            return 0

        lax.fori_loop(0, 4, weight_step, 0)
        for q in range(4):
            res = mm(hidt[...], cot[:, q * 256 : q * 256 + 256]).astype(jnp.bfloat16)
            part[two, :, :, :, :, q * 16 : q * 16 + 16, 512:768] = res.reshape(2, 2, 2, 2, 16, 256)
        rs_tick(j)
        return 0

    lax.fori_loop(0, FEED, feed, 0)

    def norm2_back(i, _):
        rows = rows_of(i, 128)
        n1[rows, :] = oacc[rows, :].astype(jnp.bfloat16)
        x = aft[rows, :].reshape(16, 8, 1024)
        g = gn[rows, :].reshape(16, 8, 1024)
        r = lax.rsqrt(jnp.mean(x * x, axis=-1, keepdims=True) + epsilon)
        unit = x * r
        gacc[8:16, :] += jnp.sum(g * unit, axis=0)
        gu = g * gains[1][None]
        back = r * (gu - unit * jnp.mean(gu * unit, axis=-1, keepdims=True))
        total = cot[rows, :].astype(jnp.float32) + back.reshape(128, 1024)
        oacc[rows, :] = total
        n2[rows, :] = total.astype(jnp.bfloat16)
        return 0

    lax.fori_loop(0, 8, norm2_back, 0)
    mixed_copy = pltpu.make_async_copy(n1, mixed_hbm, out_sem.at[0])
    mixed_copy.start()

    load(5, 0)
    load(0, 1)
    part_free(11)

    def out_weight_step(m, _):
        res = mm(mixt[rows_of(m, 256), :], n2[:, 0:WIDE]).astype(jnp.bfloat16)
        part[1, m // 2, m % 2] = res.reshape(2, 2, 64, WIDE)
        return 0

    lax.fori_loop(0, 4, out_weight_step, 0)
    rs_tick(11)

    def mixed_back(i, _):
        rows = rows_of(i, 256)
        g = n2[rows, :]
        res = nt(g[:, 0:WIDE], wbuf[0].reshape(1024, WIDE)) + nt(
            g[:, WIDE:1024], wbuf[1, :, :, :, :, :, 512:768].reshape(1024, 256)
        )
        mixed[rows, :] = res.astype(jnp.bfloat16)
        return 0

    lax.fori_loop(0, 4, mixed_back, 0)

    def qkv_back(g, _):
        load(1 + g, 0)
        attn_bwd(g)
        part_free(12 + g)
        two = g % 2

        def weight_step(m, _):
            res = mm(n1t[rows_of(m, 256), :], qkv[g]).astype(jnp.bfloat16)
            part[two, m // 2, m % 2] = res.reshape(2, 2, 64, WIDE)
            return 0

        lax.fori_loop(0, 4, weight_step, 0)
        rs_tick(12 + g)

        def rows_step(i, _):
            rows = rows_of(i, 256)
            back = nt(qkv[g, rows, :], wbuf[0].reshape(1024, WIDE))
            @pl.when(g == 0)
            def _():
                gn[rows, :] = back
            @pl.when(g > 0)
            def _():
                gn[rows, :] += back
            return 0

        lax.fori_loop(0, 4, rows_step, 0)
        return 0

    lax.fori_loop(0, 4, qkv_back, 0)

    def norm1_back(i, _):
        rows = rows_of(i, 128)
        x = lin[rows, :].reshape(16, 8, 1024)
        g = gn[rows, :].reshape(16, 8, 1024)
        r = lax.rsqrt(jnp.mean(x * x, axis=-1, keepdims=True) + epsilon)
        unit = x * r
        gacc[0:8, :] += jnp.sum(g * unit, axis=0)
        gu = g * gains[0][None]
        back = r * (gu - unit * jnp.mean(gu * unit, axis=-1, keepdims=True))
        total = oacc[rows, :].reshape(16, 8, 1024) + back
        oacc[rows, :] = total.reshape(128, 1024)
        shift[rows_of(i, 16), :] = jnp.sum(total, axis=1)
        return 0

    lax.fori_loop(0, 8, norm1_back, 0)
    gin_copy = pltpu.make_async_copy(oacc, gin_hbm, out_sem.at[1])
    gin_copy.start()

    xsend[1] = shift[...].astype(jnp.bfloat16)
    x_copy(1).start()

    def gain_copy(i):
        return remote(gsend.at[i], grecv.at[i], g_ss.at[i], g_rs.at[i], partners[i])

    gsend[0] = gacc[...]
    gain_copy(0).start()

    load(0, 1)
    part_free(16)

    def out_tail_step(m, _):
        res = mm(mixt[rows_of(m, 256), :], n2[:, WIDE:1024]).astype(jnp.bfloat16)
        part[0, m // 2, m % 2, :, :, :, 512:768] = res.reshape(2, 2, 64, 256)
        return 0

    lax.fori_loop(0, 4, out_tail_step, 0)

    x_copy(1).wait_recv()
    g_low = (shift[...] + xrecv[1].astype(jnp.float32)).astype(jnp.bfloat16)
    ctx_t = ctx[...].T
    for h in range(2):
        gh = g_low[:, h * 512 : (h + 1) * 512]
        res = mm(ctx_t, gh).astype(jnp.bfloat16).reshape(2, 2, 2, 2, 32, 512)
        part[0, :, :, :, :, h * 32 : h * 32 + 32, 0:512] = res
    rs_tick(16)
    w0 = wbuf[1, :, :, :, :, 0:32, 0:512].reshape(512, 512)
    w1 = wbuf[1, :, :, :, :, 32:64, 0:512].reshape(512, 512)
    dctx[...] = nt(g_low[:, :512], w0) + nt(g_low[:, 512:], w1)

    for i in range(4):
        gain_copy(i).wait_recv()
        if i < 3:
            gsend[i + 1] = gsend[i] + grecv[i]
            gain_copy(i + 1).start()
        else:
            gain_out[...] = gsend[i] + grecv[i]
        rs_tick(17 + i)

    for i in range(4):
        gain_copy(i).wait_send()
    for i in range(2):
        x_copy(i).wait_send()

    for stage in range(4):
        for k in (CHUNKS - 2, CHUNKS - 1):
            rs_copy(stage, k).wait_send()

    def drain(k, _):
        for stage in range(4):
            ag_copy(stage, k).wait_send()
        return 0

    lax.fori_loop(0, CHUNKS, drain, 0)
    fin_copy(CHUNKS - 2).wait()
    fin_copy(CHUNKS - 1).wait()
    mixed_copy.wait()
    gin_copy.wait()


def ag_tick_first(ag_tick, own_copy):
    own_copy.wait()

    def step(t, _):
        ag_tick(t)
        return 0

    lax.fori_loop(0, 5, step, 0)


def call_layer(tok, ctx, gains, cot, w_own):
    f32, bf16 = jnp.float32, jnp.bfloat16
    vm, dma = pltpu.VMEM, pltpu.SemaphoreType.DMA
    shape = jax.ShapeDtypeStruct
    return pl.pallas_call(
        layer_kernel,
        name="layer",
        out_shape=(
            shape((1024, 1024), bf16),
            shape((1024, 1024), f32),
            shape((128, 512), f32),
            shape((16, 1024), f32),
            shape((CHUNKS, 64, WIDE), f32),
            shape((CHUNKS, 2, 2, 2, 2, 64, WIDE), bf16),
        ),
        in_specs=[pl.BlockSpec(memory_space=pltpu.VMEM)] * 4 + [pl.BlockSpec(memory_space=pltpu.HBM)],
        out_specs=(
            pl.BlockSpec(memory_space=pltpu.HBM),
            pl.BlockSpec(memory_space=pltpu.HBM),
            pl.BlockSpec(memory_space=pltpu.VMEM),
            pl.BlockSpec(memory_space=pltpu.VMEM),
            pl.BlockSpec(memory_space=pltpu.HBM),
            pl.BlockSpec(memory_space=pltpu.HBM),
        ),
        scratch_shapes=[
            vm((1024, 1024), f32),
            vm((1024, 1024), bf16),
            vm((1024, 1024), bf16),
            vm((4, 1024, WIDE), bf16),
            vm((1024, 1024), bf16),
            vm((1024, 1024), bf16),
            vm((1024, 1024), f32),
            vm((1024, 1024), bf16),
            vm((1024, 1024), bf16),
            vm((1024, 1024), f32),
            vm((1024, 1024), f32),
            vm((2, 2, 2, 2, 2, 64, WIDE), bf16),
            vm((2, 2, 2, 2, 2, 64, WIDE), bf16),
            vm((1024, 512), bf16),
            vm((256, 1024), bf16),
            vm((128, 1024), f32),
            vm((128, 256), f32),
            vm((16, 1024), f32),
            vm((4, 16, 1024), f32),
            vm((4, 16, 1024), f32),
            vm((2, 128, 1024), bf16),
            vm((2, 128, 1024), bf16),
            vm((ROUNDS, 2, 2, 2, 64, WIDE), bf16),
            vm((ROUNDS, 4, 64, WIDE), bf16),
            vm((ROUNDS, 2, 64, WIDE), bf16),
            vm((ROUNDS, 64, WIDE), bf16),
            vm((2, 4, 64, WIDE), bf16),
            vm((2, 4, 64, WIDE), bf16),
            vm((2, 2, 64, WIDE), bf16),
            vm((2, 2, 64, WIDE), bf16),
            vm((2, 64, WIDE), bf16),
            vm((2, 64, WIDE), bf16),
            vm((2, 64, WIDE), f32),
            dma((4, CHUNKS)),
            dma((4, CHUNKS)),
            dma((4, 2)),
            dma((4, ROUNDS)),
            dma((2,)),
            dma((2,)),
            dma((4,)),
            dma((4,)),
            dma,
            dma((2,)),
            dma((2,)),
            dma((2,)),
        ],
        compiler_params=pltpu.CompilerParams(
            collective_id=0, has_side_effects=True, vmem_limit_bytes=63 * 1024 * 1024
        ),
    )(tok, ctx, gains, cot, w_own)


def pack_weights(ctx_weight, qkv_weight, out_weight, gate_weight, up_weight, down_weight):
    qkv = qkv_weight.reshape(64, 3, 4, 256).transpose(2, 0, 1, 3).reshape(4, 64, WIDE)
    gate = gate_weight.reshape(64, 16, FEED, 16).transpose(2, 0, 1, 3).reshape(FEED, 64, 256)
    up = up_weight.reshape(64, 16, FEED, 16).transpose(2, 0, 1, 3).reshape(FEED, 64, 256)
    down = down_weight.reshape(FEED, 16, 4, 256).transpose(0, 2, 1, 3).reshape(FEED, 64, 256)
    feed = jnp.concatenate([gate, up, down], axis=-1)
    ctx = ctx_weight.reshape(32, 2, 512).transpose(1, 0, 2).reshape(64, 512)
    first = jnp.concatenate([ctx, out_weight[:, WIDE:]], axis=-1)
    return jnp.concatenate([first[None], qkv, out_weight[None, :, :WIDE], feed], axis=0)


def unpack_grads(dw):
    feed = dw[:FEED]
    gate = feed[:, :, 0:256].reshape(FEED, 64, 16, 16).transpose(1, 2, 0, 3).reshape(64, 2816)
    up = feed[:, :, 256:512].reshape(FEED, 64, 16, 16).transpose(1, 2, 0, 3).reshape(64, 2816)
    down = feed[:, :, 512:768].reshape(FEED, 4, 16, 256).transpose(0, 2, 1, 3).reshape(176, 1024)
    out = jnp.concatenate([dw[11], dw[16][:, 512:]], axis=-1)
    qkv = dw[12:16].reshape(4, 64, 3, 256).transpose(1, 2, 0, 3).reshape(64, 3072)
    ctx = dw[16][:, :512].reshape(2, 32, 512).transpose(1, 0, 2).reshape(32, 1024)
    return (qkv, out, gate, up, down, ctx)


def body_kernel(
    tokens,
    context,
    ctx_weight,
    delay,
    lengths,
    attn_gain,
    ffn_gain,
    qkv_weight,
    out_weight,
    gate_weight,
    up_weight,
    down_weight,
    cotangent,
):
    frame_count, positions, width = tokens.shape[1:]
    inputs = tokens[0]
    rim_rows = shifted(inputs[frame_count - 2 :], "frames", 1)
    extended = jnp.concatenate([rim_rows, inputs], axis=0)
    frame_ids = lax.axis_index("frames") * frame_count + jnp.arange(frame_count, dtype=jnp.int32)
    chosen, valid_rows = shift_tables(delay, lengths, frame_ids)
    tok = jnp.zeros((frame_count, positions, width), jnp.float32)
    for offset in range(3):
        piece = extended[2 - offset : 2 - offset + frame_count].astype(jnp.float32)
        tok = tok + chosen[offset][None, :, None] * valid_rows[offset][:, None, None] * piece
    tok = tok.astype(jnp.bfloat16).reshape(frame_count * positions, width)
    gains = jnp.stack([attn_gain[0], ffn_gain[0]]).astype(jnp.float32)
    w_own = pack_weights(
        ctx_weight, qkv_weight[0], out_weight[0], gate_weight[0], up_weight[0], down_weight[0]
    )
    mixed_out, grad_in, d_context, gain_sums, dw, _ = call_layer(
        tok, context, gains, cotangent[0].reshape(frame_count * positions, width), w_own
    )
    d_qkv, d_out, d_gate, d_up, d_down, d_ctx = unpack_grads(dw)
    grad_in = grad_in.reshape(frame_count, positions, width)
    grad_ext = jnp.zeros((frame_count + 2, positions, width), jnp.float32)
    for offset in range(3):
        term = chosen[offset][None, :, None] * valid_rows[offset][:, None, None] * grad_in
        grad_ext = grad_ext + jnp.pad(term, ((2 - offset, offset), (0, 0), (0, 0)))
    back_rows = shifted(grad_ext[:2].astype(jnp.bfloat16), "frames", -1).astype(jnp.float32)
    grad_tokens = grad_ext[2:].at[frame_count - 2 :].add(back_rows)
    return (
        mixed_out.reshape(frame_count, positions, width)[None],
        grad_tokens[None],
        d_context,
        d_ctx,
        gain_sums[:8][None],
        gain_sums[8:][None],
        d_qkv[None],
        d_out[None],
        d_gate[None],
        d_up[None],
        d_down[None],
    )


def body(
    tokens,
    context,
    ctx_weight,
    delay,
    lengths,
    attn_gain,
    ffn_gain,
    qkv_weight,
    out_weight,
    gate_weight,
    up_weight,
    down_weight,
    cotangent,
):
    frame_count = tokens.shape[1]
    positions = tokens.shape[2]
    model_width = tokens.shape[3]
    token_rows = frame_count * positions
    head_scale = HEAD ** (-0.5)
    ctx_full = lax.all_gather(context, "stream", axis=1, tiled=True)
    ctx_rows = lax.all_gather(ctx_weight, ("stream", "frames"), axis=0, tiled=True)
    shift_term = flat_dot(ctx_full, ctx_rows)
    inputs = tokens[0]
    rim_rows = shifted(inputs[frame_count - 2 :], "frames", 1)
    extended = jnp.concatenate([rim_rows, inputs], axis=0).astype(jnp.float32)
    frame_ids = lax.axis_index("frames") * frame_count + jnp.arange(frame_count, dtype=jnp.int32)
    chosen, valid_rows = shift_tables(delay, lengths, frame_ids)
    layer_in = jnp.broadcast_to(shift_term[:, None, :], (frame_count, positions, model_width))
    for offset in range(3):
        piece = extended[2 - offset : 2 - offset + frame_count]
        layer_in = (
            layer_in + chosen[offset][None, :, None] * valid_rows[offset][:, None, None] * piece
        )
    weights = (
        lax.all_gather(qkv_weight[0], "frames", axis=0, tiled=True),
        lax.all_gather(out_weight[0], "frames", axis=0, tiled=True),
        lax.all_gather(gate_weight[0], "frames", axis=0, tiled=True),
        lax.all_gather(up_weight[0], "frames", axis=0, tiled=True),
        lax.all_gather(down_weight[0], "frames", axis=0, tiled=True),
    )
    w_qkv, w_out, w_gate, w_up, w_down = weights
    gain_one = attn_gain[0].astype(jnp.float32)
    gain_two = ffn_gain[0].astype(jnp.float32)
    normed = norm_rows(layer_in, gain_one).astype(jnp.bfloat16).reshape(token_rows, model_width)
    qkv = (
        flat_dot(normed, w_qkv).astype(jnp.bfloat16).reshape(frame_count, positions, 3, HEADS, HEAD)
    )
    queries = qkv[:, :, 0]
    key_part = qkv[:, :, 1]
    values = qkv[:, :, 2]
    scores = (
        jnp.einsum("fqhd,fkhd->fhqk", queries, key_part, preferred_element_type=jnp.float32)
        * head_scale
    )
    causal = jnp.arange(positions)[:, None] >= jnp.arange(positions)[None, :]
    scores = jnp.where(causal[None, None], scores, -1e30)
    probs = jax.nn.softmax(scores, axis=-1)
    probs_low = probs.astype(jnp.bfloat16)
    mixed = jnp.einsum("fhqk,fkhd->fqhd", probs_low, values, preferred_element_type=jnp.float32)
    mixed = mixed.astype(jnp.bfloat16).reshape(token_rows, model_width)
    after_attn = layer_in + flat_dot(mixed, w_out).reshape(frame_count, positions, model_width)
    normed_two = (
        norm_rows(after_attn, gain_two).astype(jnp.bfloat16).reshape(token_rows, model_width)
    )
    gate_pre = flat_dot(normed_two, w_gate)
    up_pre = flat_dot(normed_two, w_up)
    hidden = (jax.nn.silu(gate_pre) * up_pre).astype(jnp.bfloat16)
    out_full = after_attn + flat_dot(hidden, w_down).reshape(frame_count, positions, model_width)
    b_qkv, b_out, b_gate, b_up, b_down = weights
    grad_out = cotangent[0].astype(jnp.float32)
    grad_ff = grad_out.reshape(token_rows, model_width).astype(jnp.bfloat16)
    grad_down = trans_dot(hidden, grad_ff)
    grad_hidden = back_dot(grad_ff, b_down)
    sigmoid_gate = jax.nn.sigmoid(gate_pre)
    grad_gate = (
        grad_hidden * up_pre * sigmoid_gate * (1.0 + gate_pre * (1.0 - sigmoid_gate))
    ).astype(jnp.bfloat16)
    grad_up = (grad_hidden * gate_pre * sigmoid_gate).astype(jnp.bfloat16)
    grad_gate_w = trans_dot(normed_two, grad_gate)
    grad_up_w = trans_dot(normed_two, grad_up)
    grad_normed_two = (back_dot(grad_gate, b_gate) + back_dot(grad_up, b_up)).reshape(
        frame_count, positions, model_width
    )
    grad_after_norm, grad_gain_two = norm_back(grad_normed_two, after_attn, gain_two)
    grad_after = grad_out + grad_after_norm
    grad_branch = grad_after.reshape(token_rows, model_width).astype(jnp.bfloat16)
    grad_out_w = trans_dot(mixed, grad_branch)
    grad_mixed = (
        back_dot(grad_branch, b_out)
        .astype(jnp.bfloat16)
        .reshape(frame_count, positions, HEADS, HEAD)
    )
    grad_values = jnp.einsum(
        "fhqk,fqhd->fkhd", probs_low, grad_mixed, preferred_element_type=jnp.float32
    )
    grad_probs = jnp.einsum(
        "fqhd,fkhd->fhqk", grad_mixed, values, preferred_element_type=jnp.float32
    )
    grad_scores = (
        probs * (grad_probs - jnp.sum(grad_probs * probs, axis=-1, keepdims=True))
    ).astype(jnp.bfloat16)
    grad_queries = (
        jnp.einsum("fhqk,fkhd->fqhd", grad_scores, key_part, preferred_element_type=jnp.float32)
        * head_scale
    )
    grad_keys = (
        jnp.einsum("fhqk,fqhd->fkhd", grad_scores, queries, preferred_element_type=jnp.float32)
        * head_scale
    )
    grad_qkv = jnp.stack([grad_queries, grad_keys, grad_values], axis=2).astype(jnp.bfloat16)
    grad_qkv = grad_qkv.reshape(token_rows, 3 * model_width)
    grad_qkv_w = trans_dot(normed, grad_qkv)
    all_parts = (
        lax.psum_scatter(grad_qkv_w, "frames", scatter_dimension=0, tiled=True),
        lax.psum_scatter(grad_out_w, "frames", scatter_dimension=0, tiled=True),
        lax.psum_scatter(grad_gate_w, "frames", scatter_dimension=0, tiled=True),
        lax.psum_scatter(grad_up_w, "frames", scatter_dimension=0, tiled=True),
        lax.psum_scatter(grad_down, "frames", scatter_dimension=0, tiled=True),
    )
    d_qkv_rows, d_out_rows, d_gate_rows, d_up_rows, d_down_rows = all_parts
    grad_normed = back_dot(grad_qkv, b_qkv).reshape(frame_count, positions, model_width)
    grad_in_norm, grad_gain_one = norm_back(grad_normed, layer_in, gain_one)
    grad_in = grad_after + grad_in_norm
    gain_sums = lax.psum((grad_gain_one, grad_gain_two), "frames")
    grad_shift = jnp.sum(grad_in, axis=1).astype(jnp.bfloat16)
    grad_ctx_w = trans_dot(ctx_full, grad_shift)
    ctx_w_rows = lax.psum_scatter(grad_ctx_w, ("stream", "frames"), scatter_dimension=0, tiled=True)
    grad_context = back_dot(grad_shift, ctx_rows)
    context_half = lax.psum_scatter(
        grad_context.astype(jnp.bfloat16), "stream", scatter_dimension=1, tiled=True
    ).astype(jnp.float32)
    grad_ext = jnp.zeros((frame_count + 2, positions, model_width), jnp.float32)
    for offset in range(3):
        term = chosen[offset][None, :, None] * valid_rows[offset][:, None, None] * grad_in
        grad_ext = grad_ext + jnp.pad(term, ((2 - offset, offset), (0, 0), (0, 0)))
    back_rows = shifted(grad_ext[:2].astype(jnp.bfloat16), "frames", -1).astype(jnp.float32)
    grad_tokens = grad_ext[2:].at[frame_count - 2 :].add(back_rows)
    return (
        out_full.astype(jnp.bfloat16)[None],
        grad_tokens[None],
        context_half,
        ctx_w_rows,
        gain_sums[0][None],
        gain_sums[1][None],
        d_qkv_rows[None],
        d_out_rows[None],
        d_gate_rows[None],
        d_up_rows[None],
        d_down_rows[None],
    )


def solution(mesh):
    fits = mesh.shape["frames"] == 16 and mesh.shape["stream"] == 2
    return jax.shard_map(
        body_kernel if fits else body,
        mesh=mesh,
        in_specs=(
            P("stream", "frames", None, None),
            P("frames", "stream"),
            P(("stream", "frames"), None),
            P(),
            P(),
            P("stream", None, None),
            P("stream", None, None),
            P("stream", "frames", None),
            P("stream", "frames", None),
            P("stream", "frames", None),
            P("stream", "frames", None),
            P("stream", "frames", None),
            P("stream", "frames", None, None),
        ),
        out_specs=(
            P("stream", "frames", None, None),
            P("stream", "frames", None, None),
            P("frames", "stream"),
            P(("stream", "frames"), None),
            P("stream", None, None),
            P("stream", None, None),
            P("stream", "frames", None),
            P("stream", "frames", None),
            P("stream", "frames", None),
            P("stream", "frames", None),
            P("stream", "frames", None),
        ),
        check_vma=False,
    )
```

```python
import jax
import jax.numpy as jnp
from jax import lax
from jax.experimental import pallas as pl
from jax.experimental.pallas import tpu as pltpu
from jax.sharding import PartitionSpec as P

HEADS = 16
HEAD = 64


epsilon = 1e-05


def shifted(x, axis, by):
    length = lax.axis_size(axis)
    pairs = [(i, i + by) for i in range(length) if 0 <= i + by < length]
    return lax.ppermute(x, axis, pairs)


def flat_dot(left, right):
    return jnp.dot(left, right, preferred_element_type=jnp.float32)


def trans_dot(left, right):
    return lax.dot_general(
        left, right, (((0,), (0,)), ((), ())), preferred_element_type=jnp.float32
    )


def back_dot(left, right):
    return lax.dot_general(
        left, right, (((1,), (1,)), ((), ())), preferred_element_type=jnp.float32
    )


def norm_rows(rows, gain):
    return rows * lax.rsqrt(jnp.mean(rows * rows, axis=-1, keepdims=True) + epsilon) * gain


def norm_back(grad_normed, rows, gain):
    scale = lax.rsqrt(jnp.mean(rows * rows, axis=-1, keepdims=True) + epsilon)
    unit = rows * scale
    grad_gain = jnp.sum(grad_normed * unit, axis=0)
    grad_unit = grad_normed * gain
    grad_rows = scale * (grad_unit - unit * jnp.mean(grad_unit * unit, axis=-1, keepdims=True))
    return (grad_rows, grad_gain)


def shift_tables(delay, lengths, frame_ids):
    starts = jnp.cumsum(lengths) - lengths
    at_start = jnp.any(frame_ids[:, None] == starts[None, :], axis=1)
    after_start = jnp.any(frame_ids[:, None] - 1 == starts[None, :], axis=1)
    keep_one = jnp.logical_not(at_start)
    keep_two = jnp.logical_and(keep_one, jnp.logical_not(after_start))
    valid_rows = jnp.stack([jnp.ones_like(keep_one), keep_one, keep_two]).astype(jnp.float32)
    chosen = (delay[None, :] == jnp.arange(3, dtype=jnp.int32)[:, None]).astype(jnp.float32)
    return (chosen, valid_rows)


MESH = pl.DeviceIdType.MESH
CHUNKS = 17
FEED = 11
WIDE = 768
ROUNDS = 5


def mm(a, b):
    return jnp.dot(a, b, preferred_element_type=jnp.float32)


def nt(a, b):
    return lax.dot_general(a, b, (((1,), (1,)), ((), ())), preferred_element_type=jnp.float32)


def tn(a, b):
    return lax.dot_general(a, b, (((0,), (0,)), ((), ())), preferred_element_type=jnp.float32)


def either(cond, fn):
    if isinstance(cond, bool):
        if cond:
            fn()
    else:
        pl.when(cond)(fn)


def within(t, low, high):
    if isinstance(t, int):
        return low <= t < high
    return jnp.logical_and(t >= low, t < high)


def layer_kernel(
    tok_hbm,
    ctx,
    gain_one,
    gain_two,
    cot,
    ctx_own,
    qkv_own,
    out_own,
    gate_own,
    up_own,
    down_own,
    delay,
    lengths,
    mixed_hbm,
    dtok_hbm,
    dctx,
    dctxw_hbm,
    dgain_one,
    dgain_two,
    dqkv_hbm,
    dout_hbm,
    dgate_hbm,
    dup_hbm,
    ddown_hbm,
    gathered,
    w_own,
    lin,
    n1,
    n1t,
    qkv,
    mixed,
    mixt,
    aft,
    n2,
    n2t,
    oacc,
    gn,
    wbuf,
    wtail,
    part,
    hidt,
    shift,
    bias,
    gacc,
    gsend,
    grecv,
    xsend,
    xrecv,
    r_c,
    r_y,
    r_zl,
    r_zh,
    t_keep,
    t_send,
    u_keep,
    u_send,
    v_keep,
    v_send,
    fin,
    ag_ss,
    ag_rs,
    rs_ss,
    rs_rs,
    x_ss,
    x_rs,
    g_ss,
    g_rs,
    own_sem,
    load_sem,
    tok_sem,
    rim_ss,
    rim_rs,
    out_sem,
):
    s = lax.axis_index("stream")
    f = lax.axis_index("frames")
    c = f % 2
    y = (f // 2) % 2
    zl = (f // 4) % 2
    zh = f // 8
    d_c = (s, f + 1 - 2 * c)
    d_y = (s, f + 2 - 4 * y)
    d_zl = (s, f + 4 - 8 * zl)
    d_zh = (s, f + 8 - 16 * zh)
    d_x = (1 - s, f)
    partners = (d_zh, d_zl, d_y, d_c)

    frames = lax.axis_size("frames")
    has_next, has_prev = f < frames - 1, f > 0
    d_next, d_prev = (s, f + 1), (s, f - 1)

    tokext = n2t
    tok_copy = pltpu.make_async_copy(tok_hbm, tokext.at[16:1040], tok_sem)
    tok_copy.start()

    barrier = pltpu.get_barrier_semaphore()

    def greet(device):
        pl.semaphore_signal(barrier, inc=1, device_id=device, device_id_type=MESH)

    for device in partners + (d_x,):
        greet(device)
    pl.when(has_next)(lambda: greet(d_next))
    pl.when(has_prev)(lambda: greet(d_prev))

    w_own[0, 0:32, 0:512] = ctx_own[:, 0:512]
    w_own[0, 32:64, 0:512] = ctx_own[:, 512:1024]
    w_own[0, :, 512:768] = out_own[:, 768:1024]
    w_own[5] = out_own[:, 0:768]
    for g in range(4):
        for part_id in range(3):
            at = part_id * 1024 + g * 256
            w_own[1 + g, :, part_id * 256 : part_id * 256 + 256] = qkv_own[:, at : at + 256]

    def own_copy(low, high, i):
        return pltpu.make_async_copy(
            w_own.at[low:high], gathered.at[low:high, zh, zl, y, c], own_sem.at[i]
        )

    own_copy(0, 6, 0).start()

    pl.semaphore_wait(barrier, 5 + has_next.astype(jnp.int32) + has_prev.astype(jnp.int32))

    def remote(src, dst, ss, rs, device):
        return pltpu.make_async_remote_copy(
            src_ref=src, dst_ref=dst, send_sem=ss, recv_sem=rs, device_id=device, device_id_type=MESH
        )

    def crossed(k):
        return k % 4 == 2

    def ag_copy(stage, k, cross):
        if stage == 0:
            src = dst = gathered.at[k, zh, zl, y, c]
        elif stage == 1:
            src = dst = gathered.at[k, :, zl, y, c]
        elif stage == 2:
            src = dst = gathered.at[k, :, zl, :, c] if cross else gathered.at[k, :, :, y, c]
        else:
            src = dst = gathered.at[k, :, :, :, c]
        if stage == 0:
            src = w_own.at[k]
        order = (d_zh, d_y, d_zl, d_c) if cross else (d_zh, d_zl, d_y, d_c)
        return remote(src, dst, ag_ss.at[stage, k], ag_rs.at[stage, k], order[stage])

    def ag_start(stage, k):
        if stage in (0, 3):
            ag_copy(stage, k, False).start()
        elif isinstance(k, int):
            ag_copy(stage, k, crossed(k)).start()
        else:
            pl.when(crossed(k))(lambda: ag_copy(stage, k, True).start())
            pl.when(jnp.logical_not(crossed(k)))(lambda: ag_copy(stage, k, False).start())

    def load_copy(k, slot):
        return pltpu.make_async_copy(gathered.at[k], wbuf.at[slot], load_sem.at[slot])

    def ag_tick(t):
        for stage in range(4):
            def step(stage=stage):
                k = t - stage
                if stage > 0:
                    ag_copy(stage - 1, k, False).wait_recv()
                ag_start(stage, k)
            either(within(t, stage, stage + CHUNKS), step)
        def ready():
            ag_copy(3, t - 4, False).wait_recv()
            load_copy(t - 4, t % 2).start()
        either(within(t, 4, 4 + CHUNKS), ready)

    def rs_copy(stage, r):
        two, four = r % 2, r % ROUNDS
        if stage == 0:
            src, dst = part.at[two, :, :, :, 1 - c], r_c.at[two]
        elif stage == 1:
            src, dst = t_send.at[two], r_y.at[four]
        elif stage == 2:
            src, dst = u_send.at[two], r_zl.at[four]
        else:
            src, dst = v_send.at[two], r_zh.at[four]
        cross = flag(r)
        to_y, to_zl = f + 2 - 4 * y, f + 4 - 8 * zl
        if stage == 1:
            device = (s, to_y * (1 - cross) + to_zl * cross)
        elif stage == 2:
            device = (s, to_zl * (1 - cross) + to_y * cross)
        else:
            device = partners[3 - stage]
        return remote(src, dst, rs_ss.at[stage, two], rs_rs.at[stage, four], device)

    def flag(r):
        return int(crossed(r)) if isinstance(r, int) else crossed(r).astype(jnp.int32)

    def add(a, b):
        return a.astype(jnp.float32) + b.astype(jnp.float32)

    def place_result(k, res):
        if not isinstance(k, int):
            @pl.when(k < FEED)
            def _():
                fin[k] = res
            pl.when(k == FEED)(lambda: place_result(FEED, res))
            return
        if k < FEED:
            fin[k] = res
        elif k == FEED:
            aft[384:448, 0:768] = res
        elif k < CHUNKS - 1:
            g = k - FEED - 1
            for p in range(3):
                aft[192 + 64 * p : 256 + 64 * p, g * 256 : g * 256 + 256] = res[:, p * 256 : p * 256 + 256]
        else:
            aft[384:448, 768:1024] = res[:, 512:768]
            aft[448:480, 0:512] = res[0:32, 0:512]
            aft[448:480, 512:1024] = res[32:64, 0:512]

    def out_copies():
        pairs = [(aft.at[384:448], dout_hbm), (aft.at[448:480], dctxw_hbm)]
        for p in range(3):
            pairs.append((aft.at[192 + 64 * p : 256 + 64 * p], dqkv_hbm.at[:, p * 1024 : p * 1024 + 1024]))
        return pairs

    def feed_copies():
        pairs = [(aft.at[512:688], ddown_hbm)]
        for i, hbm in enumerate((dgate_hbm, dup_hbm)):
            at = i * 768
            if i == 1:
                at = 704
            for p in range(3):
                n = 1024 if p < 2 else 768
                pairs.append((aft.at[at + 64 * p : at + 64 * p + 64, 0:n], hbm.at[:, p * 1024 : p * 1024 + n]))
        return pairs

    def out_copy(pair, i):
        return pltpu.make_async_copy(pair[0], pair[1], out_sem.at[i])

    def unpack_feed():
        for j in range(FEED):
            for q in range(4):
                aft[512 + j * 16 : 528 + j * 16, q * 256 : q * 256 + 256] = fin[j, q * 16 : q * 16 + 16, 512:768]
        for i, at in enumerate((0, 704)):
            cols = [
                fin[j, :, i * 256 + d * 16 : i * 256 + d * 16 + 16] for d in range(16) for j in range(FEED)
            ]
            for p in range(22):
                piece = jnp.concatenate(cols[p * 8 : p * 8 + 8], axis=1)
                row, col = at + 64 * (p // 8), (p % 8) * 128
                aft[row : row + 64, col : col + 128] = piece

    def rs_tick(r, static_first=False):
        def stage_y():
            k = r - 1
            rs_copy(0, k).wait_recv()
            either(within(k, 2, CHUNKS), lambda: rs_copy(1, k - 2).wait_send())
            two, four = k % 2, k % ROUNDS
            cross = flag(k)

            def piece(i, _):
                a, b = i // 2, i % 2
                near = b * (1 - cross) + (1 - zl) * cross
                side = (1 - y) * (1 - cross) + b * cross
                t_send[two, i] = add(part[two, a, near, side, c], r_c[two, a, near, side]).astype(jnp.bfloat16)
                near = b * (1 - cross) + zl * cross
                side = y * (1 - cross) + b * cross
                t_keep[two, i] = add(part[two, a, near, side, c], r_c[two, a, near, side]).astype(jnp.bfloat16)
                return 0

            lax.fori_loop(0, 4, piece, 0)
            rs_copy(1, k).start()
        either(within(r, 1, CHUNKS + 1), stage_y)
        either(within(r, 0, CHUNKS), lambda: rs_copy(0, r).start())

        def stage_zl():
            k = r - 2
            rs_copy(1, k).wait_recv()
            either(within(k, 2, CHUNKS), lambda: rs_copy(2, k - 2).wait_send())
            two, four = k % 2, k % ROUNDS
            cross = flag(k)
            mine = zl * (1 - cross) + y * cross
            for a in range(2):
                far, near = a * 2 + 1 - mine, a * 2 + mine
                u_send[two, a] = add(t_keep[two, far], r_y[four, far]).astype(jnp.bfloat16)
                u_keep[two, a] = add(t_keep[two, near], r_y[four, near]).astype(jnp.bfloat16)
            rs_copy(2, k).start()
        either(within(r, 2, CHUNKS + 2), stage_zl)

        def stage_zh():
            k = r - 3
            rs_copy(2, k).wait_recv()
            either(within(k, 2, CHUNKS), lambda: rs_copy(3, k - 2).wait_send())
            two, four = k % 2, k % ROUNDS
            v_send[two] = add(u_keep[two, 1 - zh], r_zl[four, 1 - zh]).astype(jnp.bfloat16)
            v_keep[two] = add(u_keep[two, zh], r_zl[four, zh]).astype(jnp.bfloat16)
            rs_copy(3, k).start()
        either(within(r, 3, CHUNKS + 3), stage_zh)

        def last():
            k = r - 4
            rs_copy(3, k).wait_recv()
            place_result(k, add(v_keep[k % 2], r_zh[k % ROUNDS]))
        either(within(r, 4, CHUNKS + 4), last)

    def part_free(r):
        either(within(r, 2, CHUNKS), lambda: rs_copy(0, r - 2).wait_send())

    rim_copy = remote(tok_hbm.at[1008:1024], tokext.at[0:16], rim_ss.at[0], rim_rs.at[0], d_next)
    halo_copy = remote(oacc.at[0:16], oacc.at[1024:1040], rim_ss.at[1], rim_rs.at[1], d_prev)
    pl.when(has_next)(lambda: rim_copy.start())

    @pl.when(jnp.logical_not(has_prev))
    def _():
        tokext[0:16, :] = jnp.zeros((16, 1024), jnp.bfloat16)

    @pl.when(jnp.logical_not(has_next))
    def _():
        oacc[1024:1040, :] = jnp.zeros((16, 1024), jnp.float32)

    row_id = lax.broadcasted_iota(jnp.int32, (128, 256), 0)
    col_id = lax.broadcasted_iota(jnp.int32, (128, 256), 1) % 128
    seen = jnp.logical_and(row_id // 8 == col_id // 8, col_id <= row_id)
    bias[...] = jnp.where(seen, 0.0, -1e30)

    gacc[...] = jnp.zeros_like(gacc)

    place = lax.broadcasted_iota(jnp.int32, (16, 8, 1), 1)
    wait = jnp.zeros((16, 8, 1), jnp.int32)
    for p in range(8):
        wait = jnp.where(place == p, delay[p], wait)

    def starts_at(frame):
        start = jnp.int32(0)
        hit = frame == start
        for i in range(lengths.shape[0] - 1):
            start = start + lengths[i]
            hit = jnp.logical_or(hit, frame == start)
        return hit

    def same_item(frame, j):
        ok = jnp.logical_not(starts_at(frame))
        if j == 2:
            ok = jnp.logical_and(ok, jnp.logical_not(starts_at(frame - 1)))
        return ok

    def frame_of(i):
        return f * 128 + i * 16 + lax.broadcasted_iota(jnp.int32, (16, 8, 1), 0)

    def pack_feed(own, at):
        for j in range(FEED):
            cols = [own[:, d * 176 + j * 16 : d * 176 + j * 16 + 16] for d in range(16)]
            w_own[6 + j, :, at : at + 256] = jnp.concatenate(cols, axis=1)

    ag_tick(0)
    own_copy(0, 6, 0).wait()
    ag_tick(1)
    for j in range(FEED):
        for q in range(4):
            w_own[6 + j, q * 16 : q * 16 + 16, 512:768] = down_own[
                j * 16 : j * 16 + 16, q * 256 : q * 256 + 256
            ]
    pack_feed(gate_own, 0)
    ag_tick(2)
    pack_feed(up_own, 256)
    own_copy(6, CHUNKS, 1).start()
    ag_tick(3)
    ag_tick(4)
    own_copy(6, CHUNKS, 1).wait()

    load_copy(0, 0).wait()
    wtail[...] = wbuf[0, :, :, :, :, :, 512:768].reshape(1024, 256)
    half = shift.shape[1] // 2
    for h in range(2):
        w_half = wbuf[0, :, :, :, :, h * 32 : h * 32 + 32, 0:512].reshape(512, 512)
        shift[:, h * half : (h + 1) * half] = mm(ctx[...], w_half)
    xsend[0] = shift[...].astype(jnp.bfloat16)

    def x_copy(i):
        return remote(xsend.at[i], xrecv.at[i], x_ss.at[i], x_rs.at[i], d_x)

    x_copy(0).start()
    ag_tick(5)
    x_copy(0).wait_recv()
    shift[...] = shift[...] + xrecv[0].astype(jnp.float32)

    def rows_of(i, size):
        return pl.ds(pl.multiple_of(i * size, size), size)

    def norm1(i, _):
        rows = rows_of(i, 128)
        sh = shift[rows_of(i, 16), :]
        near = tokext[pl.ds(pl.multiple_of(i * 128, 128), 144), :].astype(jnp.float32)
        frame = frame_of(i)
        x = jnp.zeros((16, 8, 1024), jnp.float32)
        for j in range(3):
            keep = wait == j
            if j > 0:
                keep = jnp.logical_and(keep, same_item(frame, j))
            piece = near[16 - 8 * j : 144 - 8 * j].reshape(16, 8, 1024)
            x = jnp.where(keep, piece, x)
        x = x + sh[:, None, :]
        r = lax.rsqrt(jnp.mean(x * x, axis=-1, keepdims=True) + epsilon)
        n = (x * r * gain_one[...].astype(jnp.float32)[None]).reshape(128, 1024).astype(jnp.bfloat16)
        lin[rows, :] = x.reshape(128, 1024)
        n1[rows, :] = n
        n1t[:, rows] = n.T
        return 0

    tok_copy.wait()
    pl.when(has_prev)(lambda: rim_copy.wait_recv())
    lax.fori_loop(0, 8, norm1, 0)

    lane_low = lax.broadcasted_iota(jnp.int32, (128, 128), 1) < 64
    head_scale = HEAD ** (-0.5)

    def both(v):
        zero = jnp.zeros_like(v)
        return jnp.concatenate([jnp.where(lane_low, v, zero), jnp.where(lane_low, zero, v)], axis=0)

    def softmax(sc):
        parts = []
        for h in range(2):
            p = sc[:, h * 128 : h * 128 + 128]
            e = jnp.exp(p - jnp.max(p, axis=-1, keepdims=True))
            parts.append(e / jnp.sum(e, axis=-1, keepdims=True))
        return parts

    def attn_fwd(g):
        def rows_step(i, _):
            rows = rows_of(i, 256)
            for u in range(2):
                sub = rows_of(i * 2 + u, 128)
                for p in range(2):
                    lo = p * 128
                    q = qkv[g, sub, lo : lo + 128]
                    k = qkv[g, sub, 256 + lo : 384 + lo]
                    v = qkv[g, sub, 512 + lo : 640 + lo]
                    sc = nt(q, both(k)) * head_scale + bias[...]
                    pr = jnp.concatenate([x.astype(jnp.bfloat16) for x in softmax(sc)], axis=1)
                    out = mm(pr, both(v)).astype(jnp.bfloat16)
                    mixed[sub, pl.ds(pl.multiple_of(g * 256 + lo, 128), 128)] = out
            return 0
        lax.fori_loop(0, 4, rows_step, 0)

    def attn_bwd(g):
        def rows_step(i, _):
            for u in range(2):
                sub = rows_of(i * 2 + u, 128)
                for p in range(2):
                    lo = p * 128
                    q = qkv[g, sub, lo : lo + 128]
                    k = qkv[g, sub, 256 + lo : 384 + lo]
                    v = qkv[g, sub, 512 + lo : 640 + lo]
                    do = mixed[sub, pl.ds(pl.multiple_of(g * 256 + lo, 128), 128)]
                    kk = both(k)
                    sc = nt(q, kk) * head_scale + bias[...]
                    pr = softmax(sc)
                    dp = nt(do, both(v))
                    ds = []
                    for h in range(2):
                        d = dp[:, h * 128 : h * 128 + 128]
                        ds.append((pr[h] * (d - jnp.sum(d * pr[h], axis=-1, keepdims=True))).astype(jnp.bfloat16))
                    ds = jnp.concatenate(ds, axis=1)
                    pl_low = jnp.concatenate([x.astype(jnp.bfloat16) for x in pr], axis=1)
                    dq = mm(ds, kk) * head_scale
                    dk = tn(ds, q)
                    dv = tn(pl_low, do)
                    qkv[g, sub, lo : lo + 128] = dq.astype(jnp.bfloat16)
                    qkv[g, sub, 256 + lo : 384 + lo] = (
                        jnp.where(lane_low, dk[:128], dk[128:]) * head_scale
                    ).astype(jnp.bfloat16)
                    qkv[g, sub, 512 + lo : 640 + lo] = jnp.where(lane_low, dv[:128], dv[128:]).astype(jnp.bfloat16)
            return 0
        lax.fori_loop(0, 4, rows_step, 0)

    def qkv_group(g, _):
        slot = (1 + g) % 2
        load_copy(1 + g, slot).wait()

        def rows_step(i, _):
            rows = rows_of(i, 256)
            qkv[g, rows, :] = mm(n1[rows, :], wbuf[slot].reshape(1024, WIDE)).astype(jnp.bfloat16)
            return 0

        lax.fori_loop(0, 4, rows_step, 0)
        attn_fwd(g)
        ag_tick(6 + g)
        return 0

    lax.fori_loop(0, 4, qkv_group, 0)

    load_copy(5, 1).wait()

    def after(i, _):
        rows = rows_of(i, 256)
        m = mixed[rows, :]
        a = lin[rows, 0:WIDE] + mm(m, wbuf[1].reshape(1024, WIDE))
        b = lin[rows, WIDE:1024] + mm(m, wtail[...])
        x = jnp.concatenate([a, b], axis=1)
        aft[rows, :] = x
        oacc[rows, :] = x
        x3 = x.reshape(32, 8, 1024)
        r = lax.rsqrt(jnp.mean(x3 * x3, axis=-1, keepdims=True) + epsilon)
        n = (x3 * r * gain_two[...].astype(jnp.float32)[None]).reshape(256, 1024).astype(jnp.bfloat16)
        n2[rows, :] = n
        n2t[0:1024, rows] = n.T
        mixt[:, rows] = m.T
        return 0

    lax.fori_loop(0, 4, after, 0)
    ag_tick(10)

    def feed(j, _):
        slot = j % 2
        load_copy(6 + j, slot).wait()
        part_free(j)
        two = j % 2

        def rows_step(i, _):
            rows = rows_of(i, 256)
            w_gu = wbuf[slot, :, :, :, :, :, 0:512].reshape(1024, 512)
            pre = mm(n2[rows, :], w_gu)
            gate, up = pre[:, :256], pre[:, 256:]
            g_hid = jnp.zeros((256, 256), jnp.float32)
            for q in range(4):
                w_q = wbuf[slot, :, :, :, :, q * 16 : q * 16 + 16, 512:768].reshape(256, 256)
                g_hid = g_hid + nt(cot[rows, q * 256 : q * 256 + 256], w_q)
            sig = jax.nn.sigmoid(gate)
            silu = gate * sig
            hid = (silu * up).astype(jnp.bfloat16)
            g_gate = (g_hid * up * sig * (1.0 + gate * (1.0 - sig))).astype(jnp.bfloat16)
            g_up = (g_hid * silu).astype(jnp.bfloat16)
            for q in range(4):
                w_q = wbuf[slot, :, :, :, :, q * 16 : q * 16 + 16, 512:768].reshape(256, 256)
                oacc[rows, q * 256 : q * 256 + 256] += mm(hid, w_q)
            both_g = jnp.concatenate([g_gate, g_up], axis=1)
            n1[rows, 0:512] = both_g
            hidt[:, rows] = hid.T
            back = nt(both_g, w_gu)
            @pl.when(j == 0)
            def _():
                gn[rows, :] = back
            @pl.when(j > 0)
            def _():
                gn[rows, :] += back
            return 0

        lax.fori_loop(0, 4, rows_step, 0)

        def weight_step(m, _):
            res = mm(n2t[rows_of(m, 256), :], n1[:, 0:512]).astype(jnp.bfloat16).reshape(2, 2, 64, 512)
            part[two, m // 2, m % 2, :, :, :, 0:512] = res
            return 0

        lax.fori_loop(0, 4, weight_step, 0)
        for q in range(4):
            res = mm(hidt[...], cot[:, q * 256 : q * 256 + 256]).astype(jnp.bfloat16)
            part[two, :, :, :, :, q * 16 : q * 16 + 16, 512:768] = res.reshape(2, 2, 2, 2, 16, 256)
        ag_tick(11 + j)
        rs_tick(j)
        return 0

    lax.fori_loop(0, FEED, feed, 0)
    load_copy(5, 1).start()
    load_copy(1, 0).start()

    def norm2_back(i, _):
        rows = rows_of(i, 128)
        n2t[rows, :] = oacc[rows, :].astype(jnp.bfloat16)
        x = aft[rows, :].reshape(16, 8, 1024)
        g = gn[rows, :].reshape(16, 8, 1024)
        r = lax.rsqrt(jnp.mean(x * x, axis=-1, keepdims=True) + epsilon)
        unit = x * r
        gacc[8:16, :] += jnp.sum(g * unit, axis=0)
        gu = g * gain_two[...].astype(jnp.float32)[None]
        back = r * (gu - unit * jnp.mean(gu * unit, axis=-1, keepdims=True))
        total = cot[rows, :].astype(jnp.float32) + back.reshape(128, 1024)
        oacc[rows, :] = total
        n2[rows, :] = total.astype(jnp.bfloat16)
        return 0

    lax.fori_loop(0, 8, norm2_back, 0)
    mixed_copy = pltpu.make_async_copy(n2t.at[0:1024], mixed_hbm, out_sem.at[0])
    mixed_copy.start()

    part_free(11)

    def out_weight_step(m, _):
        res = mm(mixt[rows_of(m, 256), :], n2[:, 0:WIDE]).astype(jnp.bfloat16)
        part[1, m // 2, m % 2] = res.reshape(2, 2, 64, WIDE)
        return 0

    lax.fori_loop(0, 4, out_weight_step, 0)
    rs_tick(11)

    def mixed_back(i, _):
        rows = rows_of(i, 256)
        g = n2[rows, :]
        res = nt(g[:, 0:WIDE], wbuf[1].reshape(1024, WIDE)) + nt(g[:, WIDE:1024], wtail[...])
        mixed[rows, :] = res.astype(jnp.bfloat16)
        return 0

    load_copy(5, 1).wait()
    lax.fori_loop(0, 4, mixed_back, 0)
    load_copy(2, 1).start()

    def qkv_back(g, _):
        slot = g % 2
        attn_bwd(g)
        part_free(12 + g)
        two = g % 2

        def weight_step(m, _):
            res = mm(n1t[rows_of(m, 256), :], qkv[g]).astype(jnp.bfloat16)
            part[two, m // 2, m % 2] = res.reshape(2, 2, 64, WIDE)
            return 0

        lax.fori_loop(0, 4, weight_step, 0)
        rs_tick(12 + g)

        def rows_step(i, _):
            rows = rows_of(i, 256)
            back = nt(qkv[g, rows, :], wbuf[slot].reshape(1024, WIDE))
            @pl.when(g == 0)
            def _():
                gn[rows, :] = back
            @pl.when(g > 0)
            def _():
                gn[rows, :] += back
            return 0

        load_copy(1 + g, slot).wait()
        lax.fori_loop(0, 4, rows_step, 0)
        pl.when(g < 2)(lambda: load_copy(3 + g, slot).start())
        pl.when(g == 2)(lambda: load_copy(0, 0).start())
        return 0

    lax.fori_loop(0, 4, qkv_back, 0)

    def norm1_back(i, _):
        rows = rows_of(i, 128)
        x = lin[rows, :].reshape(16, 8, 1024)
        g = gn[rows, :].reshape(16, 8, 1024)
        r = lax.rsqrt(jnp.mean(x * x, axis=-1, keepdims=True) + epsilon)
        unit = x * r
        gacc[0:8, :] += jnp.sum(g * unit, axis=0)
        gu = g * gain_one[...].astype(jnp.float32)[None]
        back = r * (gu - unit * jnp.mean(gu * unit, axis=-1, keepdims=True))
        total = oacc[rows, :].reshape(16, 8, 1024) + back
        oacc[rows, :] = total.reshape(128, 1024)
        shift[rows_of(i, 16), :] = jnp.sum(total, axis=1)
        return 0

    lax.fori_loop(0, 8, norm1_back, 0)
    pl.when(has_prev)(lambda: halo_copy.start())
    xsend[1] = shift[...].astype(jnp.bfloat16)
    x_copy(1).start()

    def gain_copy(i):
        return remote(gsend.at[i], grecv.at[i], g_ss.at[i], g_rs.at[i], partners[i])

    gsend[0] = gacc[...]
    gain_copy(0).start()

    load_copy(0, 0).wait()
    part_free(16)

    def out_tail_step(m, _):
        res = mm(mixt[rows_of(m, 256), :], n2[:, WIDE:1024]).astype(jnp.bfloat16)
        part[0, m // 2, m % 2, :, :, :, 512:768] = res.reshape(2, 2, 64, 256)
        return 0

    lax.fori_loop(0, 4, out_tail_step, 0)

    x_copy(1).wait_recv()
    g_low = (shift[...] + xrecv[1].astype(jnp.float32)).astype(jnp.bfloat16)
    ctx_t = ctx[...].T
    for h in range(2):
        gh = g_low[:, h * 512 : (h + 1) * 512]
        res = mm(ctx_t, gh).astype(jnp.bfloat16).reshape(2, 2, 2, 2, 32, 512)
        part[0, :, :, :, :, h * 32 : h * 32 + 32, 0:512] = res
    rs_tick(16)
    w0 = wbuf[0, :, :, :, :, 0:32, 0:512].reshape(512, 512)
    w1 = wbuf[0, :, :, :, :, 32:64, 0:512].reshape(512, 512)
    dctx[...] = nt(g_low[:, :512], w0) + nt(g_low[:, 512:], w1)

    def dtok(i, _):
        rows = rows_of(i, 128)
        near = oacc[pl.ds(pl.multiple_of(i * 128, 128), 144), :]
        frame = frame_of(i)
        x = jnp.zeros((16, 8, 1024), jnp.float32)
        for j in range(3):
            keep = wait == j
            if j > 0:
                keep = jnp.logical_and(keep, same_item(frame + j, j))
            x = jnp.where(keep, near[8 * j : 128 + 8 * j].reshape(16, 8, 1024), x)
        gn[rows, :] = x.reshape(128, 1024)
        return 0

    dtok_copy = pltpu.make_async_copy(gn, dtok_hbm, out_sem.at[1])
    feed_out = [out_copy(pair, 2 + i) for i, pair in enumerate(feed_copies())]
    for i in range(4):
        gain_copy(i).wait_recv()
        if i < 3:
            gsend[i + 1] = gsend[i] + grecv[i]
            gain_copy(i + 1).start()
        else:
            total = gsend[i] + grecv[i]
            dgain_one[...] = total[0:8]
            dgain_two[...] = total[8:16]
        rs_tick(17 + i)
        if i == 0:
            unpack_feed()
            for cp in feed_out:
                cp.start()
            pl.when(has_next)(lambda: halo_copy.wait_recv())
            lax.fori_loop(0, 8, dtok, 0)
            dtok_copy.start()

    last_out = [out_copy(pair, 9 + i) for i, pair in enumerate(out_copies())]
    for cp in last_out:
        cp.start()
    pl.when(has_next)(lambda: rim_copy.wait_send())
    pl.when(has_prev)(lambda: halo_copy.wait_send())

    for i in range(4):
        gain_copy(i).wait_send()
    for i in range(2):
        x_copy(i).wait_send()

    for stage in range(4):
        for k in (CHUNKS - 2, CHUNKS - 1):
            rs_copy(stage, k).wait_send()

    def drain(k, _):
        for stage in range(4):
            ag_copy(stage, k, False).wait_send()
        return 0

    lax.fori_loop(0, CHUNKS, drain, 0)
    mixed_copy.wait()
    dtok_copy.wait()
    for cp in feed_out + last_out:
        cp.wait()


def call_layer(tok, ctx, gain_one, gain_two, cot, weights, delay, lengths):
    f32, bf16 = jnp.float32, jnp.bfloat16
    vm, dma = pltpu.VMEM, pltpu.SemaphoreType.DMA
    shape = jax.ShapeDtypeStruct
    in_vmem, in_hbm, in_smem = (pl.BlockSpec(memory_space=m) for m in (pltpu.VMEM, pltpu.HBM, pltpu.SMEM))
    return pl.pallas_call(
        layer_kernel,
        name="layer",
        out_shape=(
            shape((1024, 1024), bf16),
            shape((1024, 1024), f32),
            shape((128, 512), f32),
            shape((32, 1024), f32),
            shape((8, 1024), f32),
            shape((8, 1024), f32),
            shape((64, 3072), f32),
            shape((64, 1024), f32),
            shape((64, 2816), f32),
            shape((64, 2816), f32),
            shape((176, 1024), f32),
            shape((CHUNKS, 2, 2, 2, 2, 64, WIDE), bf16),
        ),
        in_specs=[in_hbm] + [in_vmem] * 10 + [in_smem] * 2,
        out_specs=(in_hbm, in_hbm, in_vmem, in_hbm, in_vmem, in_vmem) + (in_hbm,) * 6,
        scratch_shapes=[
            vm((CHUNKS, 64, WIDE), bf16),
            vm((1024, 1024), f32),
            vm((1024, 1024), bf16),
            vm((1024, 1024), bf16),
            vm((4, 1024, WIDE), bf16),
            vm((1024, 1024), bf16),
            vm((1024, 1024), bf16),
            vm((1024, 1024), f32),
            vm((1024, 1024), bf16),
            vm((1040, 1024), bf16),
            vm((1040, 1024), f32),
            vm((1024, 1024), f32),
            vm((2, 2, 2, 2, 2, 64, WIDE), bf16),
            vm((1024, 256), bf16),
            vm((2, 2, 2, 2, 2, 64, WIDE), bf16),
            vm((256, 1024), bf16),
            vm((128, 1024), f32),
            vm((128, 256), f32),
            vm((16, 1024), f32),
            vm((4, 16, 1024), f32),
            vm((4, 16, 1024), f32),
            vm((2, 128, 1024), bf16),
            vm((2, 128, 1024), bf16),
            vm((2, 2, 2, 2, 64, WIDE), bf16),
            vm((ROUNDS, 4, 64, WIDE), bf16),
            vm((ROUNDS, 2, 64, WIDE), bf16),
            vm((ROUNDS, 64, WIDE), bf16),
            vm((2, 4, 64, WIDE), bf16),
            vm((2, 4, 64, WIDE), bf16),
            vm((2, 2, 64, WIDE), bf16),
            vm((2, 2, 64, WIDE), bf16),
            vm((2, 64, WIDE), bf16),
            vm((2, 64, WIDE), bf16),
            vm((FEED, 64, WIDE), f32),
            dma((4, CHUNKS)),
            dma((4, CHUNKS)),
            dma((4, 2)),
            dma((4, ROUNDS)),
            dma((2,)),
            dma((2,)),
            dma((4,)),
            dma((4,)),
            dma((2,)),
            dma((2,)),
            dma,
            dma((2,)),
            dma((2,)),
            dma((14,)),
        ],
        compiler_params=pltpu.CompilerParams(
            collective_id=0, has_side_effects=True, vmem_limit_bytes=63 * 1024 * 1024
        ),
    )(tok, ctx, gain_one, gain_two, cot, *weights, delay, lengths)


def body_kernel(
    tokens,
    context,
    ctx_weight,
    delay,
    lengths,
    attn_gain,
    ffn_gain,
    qkv_weight,
    out_weight,
    gate_weight,
    up_weight,
    down_weight,
    cotangent,
):
    frame_count, positions, width = tokens.shape[1:]
    rows = frame_count * positions
    weights = (ctx_weight, qkv_weight[0], out_weight[0], gate_weight[0], up_weight[0], down_weight[0])
    mixed_out, d_tokens, d_context, d_ctx, d_gain_one, d_gain_two, *grads = call_layer(
        tokens.reshape(rows, width),
        context,
        attn_gain[0],
        ffn_gain[0],
        cotangent.reshape(rows, width),
        weights,
        delay,
        lengths,
    )
    d_qkv, d_out, d_gate, d_up, d_down, _ = grads
    return (
        mixed_out.reshape(tokens.shape),
        d_tokens.reshape(tokens.shape),
        d_context,
        d_ctx,
        d_gain_one[None],
        d_gain_two[None],
        d_qkv[None],
        d_out[None],
        d_gate[None],
        d_up[None],
        d_down[None],
    )


def body(
    tokens,
    context,
    ctx_weight,
    delay,
    lengths,
    attn_gain,
    ffn_gain,
    qkv_weight,
    out_weight,
    gate_weight,
    up_weight,
    down_weight,
    cotangent,
):
    frame_count = tokens.shape[1]
    positions = tokens.shape[2]
    model_width = tokens.shape[3]
    token_rows = frame_count * positions
    head_scale = HEAD ** (-0.5)
    ctx_full = lax.all_gather(context, "stream", axis=1, tiled=True)
    ctx_rows = lax.all_gather(ctx_weight, ("stream", "frames"), axis=0, tiled=True)
    shift_term = flat_dot(ctx_full, ctx_rows)
    inputs = tokens[0]
    rim_rows = shifted(inputs[frame_count - 2 :], "frames", 1)
    extended = jnp.concatenate([rim_rows, inputs], axis=0).astype(jnp.float32)
    frame_ids = lax.axis_index("frames") * frame_count + jnp.arange(frame_count, dtype=jnp.int32)
    chosen, valid_rows = shift_tables(delay, lengths, frame_ids)
    layer_in = jnp.broadcast_to(shift_term[:, None, :], (frame_count, positions, model_width))
    for offset in range(3):
        piece = extended[2 - offset : 2 - offset + frame_count]
        layer_in = (
            layer_in + chosen[offset][None, :, None] * valid_rows[offset][:, None, None] * piece
        )
    weights = (
        lax.all_gather(qkv_weight[0], "frames", axis=0, tiled=True),
        lax.all_gather(out_weight[0], "frames", axis=0, tiled=True),
        lax.all_gather(gate_weight[0], "frames", axis=0, tiled=True),
        lax.all_gather(up_weight[0], "frames", axis=0, tiled=True),
        lax.all_gather(down_weight[0], "frames", axis=0, tiled=True),
    )
    w_qkv, w_out, w_gate, w_up, w_down = weights
    gain_one = attn_gain[0].astype(jnp.float32)
    gain_two = ffn_gain[0].astype(jnp.float32)
    normed = norm_rows(layer_in, gain_one).astype(jnp.bfloat16).reshape(token_rows, model_width)
    qkv = (
        flat_dot(normed, w_qkv).astype(jnp.bfloat16).reshape(frame_count, positions, 3, HEADS, HEAD)
    )
    queries = qkv[:, :, 0]
    key_part = qkv[:, :, 1]
    values = qkv[:, :, 2]
    scores = (
        jnp.einsum("fqhd,fkhd->fhqk", queries, key_part, preferred_element_type=jnp.float32)
        * head_scale
    )
    causal = jnp.arange(positions)[:, None] >= jnp.arange(positions)[None, :]
    scores = jnp.where(causal[None, None], scores, -1e30)
    probs = jax.nn.softmax(scores, axis=-1)
    probs_low = probs.astype(jnp.bfloat16)
    mixed = jnp.einsum("fhqk,fkhd->fqhd", probs_low, values, preferred_element_type=jnp.float32)
    mixed = mixed.astype(jnp.bfloat16).reshape(token_rows, model_width)
    after_attn = layer_in + flat_dot(mixed, w_out).reshape(frame_count, positions, model_width)
    normed_two = (
        norm_rows(after_attn, gain_two).astype(jnp.bfloat16).reshape(token_rows, model_width)
    )
    gate_pre = flat_dot(normed_two, w_gate)
    up_pre = flat_dot(normed_two, w_up)
    hidden = (jax.nn.silu(gate_pre) * up_pre).astype(jnp.bfloat16)
    out_full = after_attn + flat_dot(hidden, w_down).reshape(frame_count, positions, model_width)
    b_qkv, b_out, b_gate, b_up, b_down = weights
    grad_out = cotangent[0].astype(jnp.float32)
    grad_ff = grad_out.reshape(token_rows, model_width).astype(jnp.bfloat16)
    grad_down = trans_dot(hidden, grad_ff)
    grad_hidden = back_dot(grad_ff, b_down)
    sigmoid_gate = jax.nn.sigmoid(gate_pre)
    grad_gate = (
        grad_hidden * up_pre * sigmoid_gate * (1.0 + gate_pre * (1.0 - sigmoid_gate))
    ).astype(jnp.bfloat16)
    grad_up = (grad_hidden * gate_pre * sigmoid_gate).astype(jnp.bfloat16)
    grad_gate_w = trans_dot(normed_two, grad_gate)
    grad_up_w = trans_dot(normed_two, grad_up)
    grad_normed_two = (back_dot(grad_gate, b_gate) + back_dot(grad_up, b_up)).reshape(
        frame_count, positions, model_width
    )
    grad_after_norm, grad_gain_two = norm_back(grad_normed_two, after_attn, gain_two)
    grad_after = grad_out + grad_after_norm
    grad_branch = grad_after.reshape(token_rows, model_width).astype(jnp.bfloat16)
    grad_out_w = trans_dot(mixed, grad_branch)
    grad_mixed = (
        back_dot(grad_branch, b_out)
        .astype(jnp.bfloat16)
        .reshape(frame_count, positions, HEADS, HEAD)
    )
    grad_values = jnp.einsum(
        "fhqk,fqhd->fkhd", probs_low, grad_mixed, preferred_element_type=jnp.float32
    )
    grad_probs = jnp.einsum(
        "fqhd,fkhd->fhqk", grad_mixed, values, preferred_element_type=jnp.float32
    )
    grad_scores = (
        probs * (grad_probs - jnp.sum(grad_probs * probs, axis=-1, keepdims=True))
    ).astype(jnp.bfloat16)
    grad_queries = (
        jnp.einsum("fhqk,fkhd->fqhd", grad_scores, key_part, preferred_element_type=jnp.float32)
        * head_scale
    )
    grad_keys = (
        jnp.einsum("fhqk,fqhd->fkhd", grad_scores, queries, preferred_element_type=jnp.float32)
        * head_scale
    )
    grad_qkv = jnp.stack([grad_queries, grad_keys, grad_values], axis=2).astype(jnp.bfloat16)
    grad_qkv = grad_qkv.reshape(token_rows, 3 * model_width)
    grad_qkv_w = trans_dot(normed, grad_qkv)
    all_parts = (
        lax.psum_scatter(grad_qkv_w, "frames", scatter_dimension=0, tiled=True),
        lax.psum_scatter(grad_out_w, "frames", scatter_dimension=0, tiled=True),
        lax.psum_scatter(grad_gate_w, "frames", scatter_dimension=0, tiled=True),
        lax.psum_scatter(grad_up_w, "frames", scatter_dimension=0, tiled=True),
        lax.psum_scatter(grad_down, "frames", scatter_dimension=0, tiled=True),
    )
    d_qkv_rows, d_out_rows, d_gate_rows, d_up_rows, d_down_rows = all_parts
    grad_normed = back_dot(grad_qkv, b_qkv).reshape(frame_count, positions, model_width)
    grad_in_norm, grad_gain_one = norm_back(grad_normed, layer_in, gain_one)
    grad_in = grad_after + grad_in_norm
    gain_sums = lax.psum((grad_gain_one, grad_gain_two), "frames")
    grad_shift = jnp.sum(grad_in, axis=1).astype(jnp.bfloat16)
    grad_ctx_w = trans_dot(ctx_full, grad_shift)
    ctx_w_rows = lax.psum_scatter(grad_ctx_w, ("stream", "frames"), scatter_dimension=0, tiled=True)
    grad_context = back_dot(grad_shift, ctx_rows)
    context_half = lax.psum_scatter(
        grad_context.astype(jnp.bfloat16), "stream", scatter_dimension=1, tiled=True
    ).astype(jnp.float32)
    grad_ext = jnp.zeros((frame_count + 2, positions, model_width), jnp.float32)
    for offset in range(3):
        term = chosen[offset][None, :, None] * valid_rows[offset][:, None, None] * grad_in
        grad_ext = grad_ext + jnp.pad(term, ((2 - offset, offset), (0, 0), (0, 0)))
    back_rows = shifted(grad_ext[:2].astype(jnp.bfloat16), "frames", -1).astype(jnp.float32)
    grad_tokens = grad_ext[2:].at[frame_count - 2 :].add(back_rows)
    return (
        out_full.astype(jnp.bfloat16)[None],
        grad_tokens[None],
        context_half,
        ctx_w_rows,
        gain_sums[0][None],
        gain_sums[1][None],
        d_qkv_rows[None],
        d_out_rows[None],
        d_gate_rows[None],
        d_up_rows[None],
        d_down_rows[None],
    )


def solution(mesh):
    fits = mesh.shape["frames"] == 16 and mesh.shape["stream"] == 2
    return jax.shard_map(
        body_kernel if fits else body,
        mesh=mesh,
        in_specs=(
            P("stream", "frames", None, None),
            P("frames", "stream"),
            P(("stream", "frames"), None),
            P(),
            P(),
            P("stream", None, None),
            P("stream", None, None),
            P("stream", "frames", None),
            P("stream", "frames", None),
            P("stream", "frames", None),
            P("stream", "frames", None),
            P("stream", "frames", None),
            P("stream", "frames", None, None),
        ),
        out_specs=(
            P("stream", "frames", None, None),
            P("stream", "frames", None, None),
            P("frames", "stream"),
            P(("stream", "frames"), None),
            P("stream", None, None),
            P("stream", None, None),
            P("stream", "frames", None),
            P("stream", "frames", None),
            P("stream", "frames", None),
            P("stream", "frames", None),
            P("stream", "frames", None),
        ),
        check_vma=False,
    )
```

```python
import jax
import jax.numpy as jnp
from jax import lax
from jax.experimental import pallas as pl
from jax.experimental.pallas import tpu as pltpu
from jax.sharding import PartitionSpec as P

HEADS = 16
HEAD = 64


epsilon = 1e-05


def shifted(x, axis, by):
    length = lax.axis_size(axis)
    pairs = [(i, i + by) for i in range(length) if 0 <= i + by < length]
    return lax.ppermute(x, axis, pairs)


def flat_dot(left, right):
    return jnp.dot(left, right, preferred_element_type=jnp.float32)


def trans_dot(left, right):
    return lax.dot_general(
        left, right, (((0,), (0,)), ((), ())), preferred_element_type=jnp.float32
    )


def back_dot(left, right):
    return lax.dot_general(
        left, right, (((1,), (1,)), ((), ())), preferred_element_type=jnp.float32
    )


def norm_rows(rows, gain):
    return rows * lax.rsqrt(jnp.mean(rows * rows, axis=-1, keepdims=True) + epsilon) * gain


def norm_back(grad_normed, rows, gain):
    scale = lax.rsqrt(jnp.mean(rows * rows, axis=-1, keepdims=True) + epsilon)
    unit = rows * scale
    grad_gain = jnp.sum(grad_normed * unit, axis=0)
    grad_unit = grad_normed * gain
    grad_rows = scale * (grad_unit - unit * jnp.mean(grad_unit * unit, axis=-1, keepdims=True))
    return (grad_rows, grad_gain)


def shift_tables(delay, lengths, frame_ids):
    starts = jnp.cumsum(lengths) - lengths
    at_start = jnp.any(frame_ids[:, None] == starts[None, :], axis=1)
    after_start = jnp.any(frame_ids[:, None] - 1 == starts[None, :], axis=1)
    keep_one = jnp.logical_not(at_start)
    keep_two = jnp.logical_and(keep_one, jnp.logical_not(after_start))
    valid_rows = jnp.stack([jnp.ones_like(keep_one), keep_one, keep_two]).astype(jnp.float32)
    chosen = (delay[None, :] == jnp.arange(3, dtype=jnp.int32)[:, None]).astype(jnp.float32)
    return (chosen, valid_rows)


MESH = pl.DeviceIdType.MESH
CHUNKS = 17
FEED = 11
WIDE = 768
ROUNDS = 5
MOST = 48
SPLIT = ((0, MOST), (MOST, 64))


def mm(a, b):
    return jnp.dot(a, b, preferred_element_type=jnp.float32)


def nt(a, b):
    return lax.dot_general(a, b, (((1,), (1,)), ((), ())), preferred_element_type=jnp.float32)


def tn(a, b):
    return lax.dot_general(a, b, (((0,), (0,)), ((), ())), preferred_element_type=jnp.float32)


def either(cond, fn):
    if isinstance(cond, bool):
        if cond:
            fn()
    else:
        pl.when(cond)(fn)


def within(t, low, high):
    if isinstance(t, int):
        return low <= t < high
    return jnp.logical_and(t >= low, t < high)


def layer_kernel(
    tok_hbm,
    ctx,
    gain_one,
    gain_two,
    cot,
    ctx_own,
    qkv_own,
    out_own,
    gate_own,
    up_own,
    down_own,
    delay,
    lengths,
    mixed_hbm,
    dtok_hbm,
    dctx,
    dctxw_hbm,
    dgain_one,
    dgain_two,
    dqkv_hbm,
    dout_hbm,
    dgate_hbm,
    dup_hbm,
    ddown_hbm,
    gathered,
    w_own,
    lin,
    n1,
    n1t,
    qkv,
    mixed,
    mixt,
    aft,
    n2,
    n2t,
    oacc,
    gn,
    wbuf,
    wtail,
    part,
    hidt,
    shift,
    gacc,
    gsend,
    grecv,
    xsend,
    xrecv,
    r_c,
    r_y,
    r_zl,
    r_zh,
    t_keep,
    t_send,
    u_keep,
    u_send,
    v_keep,
    v_send,
    fin,
    ag_ss,
    ag_rs,
    rs_ss,
    rs_rs,
    x_ss,
    x_rs,
    g_ss,
    g_rs,
    own_sem,
    load_sem,
    tok_sem,
    rim_ss,
    rim_rs,
    out_sem,
):
    s = lax.axis_index("stream")
    f = lax.axis_index("frames")
    c = f % 2
    y = (f // 2) % 2
    zl = (f // 4) % 2
    zh = f // 8
    d_c = (s, f + 1 - 2 * c)
    d_y = (s, f + 2 - 4 * y)
    d_zl = (s, f + 4 - 8 * zl)
    d_zh = (s, f + 8 - 16 * zh)
    d_x = (1 - s, f)
    partners = (d_zh, d_zl, d_y, d_c)

    frames = lax.axis_size("frames")
    has_next, has_prev = f < frames - 1, f > 0
    d_next, d_prev = (s, f + 1), (s, f - 1)

    tokext = n2t
    tok_copy = pltpu.make_async_copy(tok_hbm, tokext.at[16:1040], tok_sem)
    tok_copy.start()

    barrier = pltpu.get_barrier_semaphore()

    def greet(device):
        pl.semaphore_signal(barrier, inc=1, device_id=device, device_id_type=MESH)

    for device in partners + (d_x,):
        greet(device)
    pl.when(has_next)(lambda: greet(d_next))
    pl.when(has_prev)(lambda: greet(d_prev))

    w_own[0, 0:32, 0:512] = ctx_own[:, 0:512]
    w_own[0, 32:64, 0:512] = ctx_own[:, 512:1024]
    w_own[0, :, 512:768] = out_own[:, 768:1024]
    w_own[5] = out_own[:, 0:768]
    for g in range(4):
        for part_id in range(3):
            at = part_id * 1024 + g * 256
            w_own[1 + g, :, part_id * 256 : part_id * 256 + 256] = qkv_own[:, at : at + 256]

    def own_copy(low, high, i):
        return pltpu.make_async_copy(
            w_own.at[low:high], gathered.at[low:high, zh, zl, y, c], own_sem.at[i]
        )

    own_copy(0, 6, 0).start()

    pl.semaphore_wait(barrier, 5 + has_next.astype(jnp.int32) + has_prev.astype(jnp.int32))

    def remote(src, dst, ss, rs, device):
        return pltpu.make_async_remote_copy(
            src_ref=src, dst_ref=dst, send_sem=ss, recv_sem=rs, device_id=device, device_id_type=MESH
        )

    def ag_copies(stage, k):
        if stage == 0:
            triples = [(w_own.at[k], gathered.at[k, zh, zl, y, c], d_zh)]
        elif stage == 1:
            near, side = gathered.at[k, :, zl, y, c, 0:MOST], gathered.at[k, :, zl, y, c, MOST:64]
            triples = [(near, near, d_zl), (side, side, d_y)]
        elif stage == 2:
            side, near = gathered.at[k, :, :, y, c, 0:MOST], gathered.at[k, :, zl, :, c, MOST:64]
            triples = [(side, side, d_y), (near, near, d_zl)]
        else:
            own = gathered.at[k, :, :, :, c]
            triples = [(own, own, d_c)]
        first = (0, 1, 3, 5)[stage]
        return [
            remote(src, dst, ag_ss.at[first + i, k], ag_rs.at[first + i, k], device)
            for i, (src, dst, device) in enumerate(triples)
        ]

    def start_all(copies):
        for cp in copies:
            cp.start()

    def wait_recv_all(copies):
        for cp in copies:
            cp.wait_recv()

    def wait_send_all(copies):
        for cp in copies:
            cp.wait_send()

    def load_copy(k, slot):
        return pltpu.make_async_copy(gathered.at[k], wbuf.at[slot], load_sem.at[slot])

    def ag_tick(t):
        for stage in range(4):
            def step(stage=stage):
                k = t - stage
                if stage > 0:
                    wait_recv_all(ag_copies(stage - 1, k))
                start_all(ag_copies(stage, k))
            either(within(t, stage, stage + CHUNKS), step)
        def ready():
            wait_recv_all(ag_copies(3, t - 4))
            load_copy(t - 4, t % 2).start()
        either(within(t, 4, 4 + CHUNKS), ready)

    def rs_copies(stage, r):
        two, slot = r % 2, r % ROUNDS
        if stage == 0:
            triples = [(part.at[two, :, :, :, 1 - c], r_c.at[two], d_c)]
        elif stage == 3:
            triples = [(v_send.at[two], r_zh.at[slot], d_zh)]
        else:
            src, dst = ((t_send, r_y), (u_send, r_zl))[stage - 1]
            devices = ((d_y, d_zl), (d_zl, d_y))[stage - 1]
            triples = [
                (src.at[two, :, low:high], dst.at[slot, :, low:high], device)
                for (low, high), device in zip(SPLIT, devices)
            ]
        first = (0, 1, 3, 5)[stage]
        return [
            remote(src, dst, rs_ss.at[first + i, two], rs_rs.at[first + i, slot], device)
            for i, (src, dst, device) in enumerate(triples)
        ]

    def add(a, b):
        return a.astype(jnp.float32) + b.astype(jnp.float32)

    def place_result(k, res):
        if not isinstance(k, int):
            @pl.when(k < FEED)
            def _():
                fin[k] = res
            pl.when(k == FEED)(lambda: place_result(FEED, res))
            return
        if k < FEED:
            fin[k] = res
        elif k == FEED:
            aft[384:448, 0:768] = res
        elif k < CHUNKS - 1:
            g = k - FEED - 1
            for p in range(3):
                aft[192 + 64 * p : 256 + 64 * p, g * 256 : g * 256 + 256] = res[:, p * 256 : p * 256 + 256]
        else:
            aft[384:448, 768:1024] = res[:, 512:768]
            aft[448:480, 0:512] = res[0:32, 0:512]
            aft[448:480, 512:1024] = res[32:64, 0:512]

    def out_copies():
        pairs = [(aft.at[384:448], dout_hbm), (aft.at[448:480], dctxw_hbm)]
        for p in range(3):
            pairs.append((aft.at[192 + 64 * p : 256 + 64 * p], dqkv_hbm.at[:, p * 1024 : p * 1024 + 1024]))
        return pairs

    def feed_copies():
        pairs = [(aft.at[512:688], ddown_hbm)]
        for i, hbm in enumerate((dgate_hbm, dup_hbm)):
            at = i * 768
            if i == 1:
                at = 704
            for p in range(3):
                n = 1024 if p < 2 else 768
                pairs.append((aft.at[at + 64 * p : at + 64 * p + 64, 0:n], hbm.at[:, p * 1024 : p * 1024 + n]))
        return pairs

    def out_copy(pair, i):
        return pltpu.make_async_copy(pair[0], pair[1], out_sem.at[i])

    def unpack_feed():
        for j in range(FEED):
            for q in range(4):
                aft[512 + j * 16 : 528 + j * 16, q * 256 : q * 256 + 256] = fin[j, q * 16 : q * 16 + 16, 512:768]
        for i, at in enumerate((0, 704)):
            cols = [
                fin[j, :, i * 256 + d * 16 : i * 256 + d * 16 + 16] for d in range(16) for j in range(FEED)
            ]
            for p in range(22):
                piece = jnp.concatenate(cols[p * 8 : p * 8 + 8], axis=1)
                row, col = at + 64 * (p // 8), (p % 8) * 128
                aft[row : row + 64, col : col + 128] = piece

    def rs_tick(r, static_first=False):
        def stage_y():
            k = r - 1
            wait_recv_all(rs_copies(0, k))
            either(within(k, 2, CHUNKS), lambda: wait_send_all(rs_copies(1, k - 2)))
            two, four = k % 2, k % ROUNDS

            def piece(i, _):
                a, b = i // 2, i % 2
                for (low, high), send, keep in zip(
                    SPLIT, ((b, 1 - y), (1 - zl, b)), ((b, y), (zl, b))
                ):
                    for out, (m, n) in ((t_send, send), (t_keep, keep)):
                        out[two, i, low:high] = add(
                            part[two, a, m, n, c, low:high], r_c[two, a, m, n, low:high]
                        ).astype(jnp.bfloat16)
                return 0

            lax.fori_loop(0, 4, piece, 0)
            start_all(rs_copies(1, k))
        either(within(r, 1, CHUNKS + 1), stage_y)
        either(within(r, 0, CHUNKS), lambda: start_all(rs_copies(0, r)))

        def stage_zl():
            k = r - 2
            wait_recv_all(rs_copies(1, k))
            either(within(k, 2, CHUNKS), lambda: wait_send_all(rs_copies(2, k - 2)))
            two, four = k % 2, k % ROUNDS
            for a in range(2):
                for (low, high), mine in zip(SPLIT, (zl, y)):
                    for out, at in ((u_send, a * 2 + 1 - mine), (u_keep, a * 2 + mine)):
                        out[two, a, low:high] = add(
                            t_keep[two, at, low:high], r_y[four, at, low:high]
                        ).astype(jnp.bfloat16)
            start_all(rs_copies(2, k))
        either(within(r, 2, CHUNKS + 2), stage_zl)

        def stage_zh():
            k = r - 3
            wait_recv_all(rs_copies(2, k))
            either(within(k, 2, CHUNKS), lambda: wait_send_all(rs_copies(3, k - 2)))
            two, four = k % 2, k % ROUNDS
            v_send[two] = add(u_keep[two, 1 - zh], r_zl[four, 1 - zh]).astype(jnp.bfloat16)
            v_keep[two] = add(u_keep[two, zh], r_zl[four, zh]).astype(jnp.bfloat16)
            start_all(rs_copies(3, k))
        either(within(r, 3, CHUNKS + 3), stage_zh)

        def last():
            k = r - 4
            wait_recv_all(rs_copies(3, k))
            place_result(k, add(v_keep[k % 2], r_zh[k % ROUNDS]))
        either(within(r, 4, CHUNKS + 4), last)

    def part_free(r):
        either(within(r, 2, CHUNKS), lambda: wait_send_all(rs_copies(0, r - 2)))

    rim_copy = remote(tok_hbm.at[1008:1024], tokext.at[0:16], rim_ss.at[0], rim_rs.at[0], d_next)
    halo_copy = remote(oacc.at[0:16], oacc.at[1024:1040], rim_ss.at[1], rim_rs.at[1], d_prev)
    pl.when(has_next)(lambda: rim_copy.start())

    @pl.when(jnp.logical_not(has_prev))
    def _():
        tokext[0:16, :] = jnp.zeros((16, 1024), jnp.bfloat16)

    @pl.when(jnp.logical_not(has_next))
    def _():
        oacc[1024:1040, :] = jnp.zeros((16, 1024), jnp.float32)

    gacc[...] = jnp.zeros_like(gacc)

    place = lax.broadcasted_iota(jnp.int32, (16, 8, 1), 1)
    wait = jnp.zeros((16, 8, 1), jnp.int32)
    for p in range(8):
        wait = jnp.where(place == p, delay[p], wait)

    def starts_at(frame):
        start = jnp.int32(0)
        hit = frame == start
        for i in range(lengths.shape[0] - 1):
            start = start + lengths[i]
            hit = jnp.logical_or(hit, frame == start)
        return hit

    def same_item(frame, j):
        ok = jnp.logical_not(starts_at(frame))
        if j == 2:
            ok = jnp.logical_and(ok, jnp.logical_not(starts_at(frame - 1)))
        return ok

    def frame_of(i):
        return f * 128 + i * 16 + lax.broadcasted_iota(jnp.int32, (16, 8, 1), 0)

    def pack_feed(own, at):
        for j in range(FEED):
            cols = [own[:, d * 176 + j * 16 : d * 176 + j * 16 + 16] for d in range(16)]
            w_own[6 + j, :, at : at + 256] = jnp.concatenate(cols, axis=1)

    ag_tick(0)
    own_copy(0, 6, 0).wait()
    ag_tick(1)
    for j in range(FEED):
        for q in range(4):
            w_own[6 + j, q * 16 : q * 16 + 16, 512:768] = down_own[
                j * 16 : j * 16 + 16, q * 256 : q * 256 + 256
            ]
    pack_feed(gate_own, 0)
    ag_tick(2)
    pack_feed(up_own, 256)
    own_copy(6, CHUNKS, 1).start()
    ag_tick(3)
    ag_tick(4)
    own_copy(6, CHUNKS, 1).wait()

    load_copy(0, 0).wait()
    wtail[...] = wbuf[0, :, :, :, :, :, 512:768].reshape(1024, 256)
    half = shift.shape[1] // 2
    for h in range(2):
        w_half = wbuf[0, :, :, :, :, h * 32 : h * 32 + 32, 0:512].reshape(512, 512)
        shift[:, h * half : (h + 1) * half] = mm(ctx[...], w_half)
    xsend[0] = shift[...].astype(jnp.bfloat16)

    def x_copy(i):
        return remote(xsend.at[i], xrecv.at[i], x_ss.at[i], x_rs.at[i], d_x)

    x_copy(0).start()
    ag_tick(5)
    x_copy(0).wait_recv()
    shift[...] = shift[...] + xrecv[0].astype(jnp.float32)

    def rows_of(i, size):
        return pl.ds(pl.multiple_of(i * size, size), size)

    def norm1(i, _):
        rows = rows_of(i, 128)
        sh = shift[rows_of(i, 16), :]
        near = tokext[pl.ds(pl.multiple_of(i * 128, 128), 144), :].astype(jnp.float32)
        frame = frame_of(i)
        x = jnp.zeros((16, 8, 1024), jnp.float32)
        for j in range(3):
            keep = wait == j
            if j > 0:
                keep = jnp.logical_and(keep, same_item(frame, j))
            piece = near[16 - 8 * j : 144 - 8 * j].reshape(16, 8, 1024)
            x = jnp.where(keep, piece, x)
        x = x + sh[:, None, :]
        r = lax.rsqrt(jnp.mean(x * x, axis=-1, keepdims=True) + epsilon)
        n = (x * r * gain_one[...].astype(jnp.float32)[None]).reshape(128, 1024).astype(jnp.bfloat16)
        lin[rows, :] = x.reshape(128, 1024)
        n1[rows, :] = n
        n1t[:, rows] = n.T
        return 0

    tok_copy.wait()
    pl.when(has_prev)(lambda: rim_copy.wait_recv())
    lax.fori_loop(0, 8, norm1, 0)

    lane_low = lax.broadcasted_iota(jnp.int32, (128, 128), 1) < 64
    head_scale = HEAD ** (-0.5)

    def both(v):
        zero = jnp.zeros_like(v)
        return jnp.concatenate([jnp.where(lane_low, v, zero), jnp.where(lane_low, zero, v)], axis=0)

    own_frame = [
        lax.broadcasted_iota(jnp.int32, (8, 128), 1) // 8 == fr for fr in range(16)
    ]
    key_seen = lax.broadcasted_iota(jnp.int32, (8, 128), 0) <= lax.broadcasted_iota(jnp.int32, (8, 128), 1) % 8

    def compact(full, h):
        out = full[h * 128 : h * 128 + 8]
        for fr in range(1, 16):
            at = h * 128 + fr * 8
            out = jnp.where(own_frame[fr], full[at : at + 8], out)
        return out

    def spread(pair):
        zero = jnp.zeros((8, 128), jnp.float32)
        rows = [jnp.where(own_frame[fr], x, zero) for x in pair for fr in range(16)]
        return jnp.concatenate(rows, axis=0).astype(jnp.bfloat16)

    def probabilities(q, kk):
        full = nt(kk, q)
        pair = []
        for h in range(2):
            sc = jnp.where(key_seen, compact(full, h) * head_scale, -1e30)
            e = jnp.exp(sc - jnp.max(sc, axis=0, keepdims=True))
            pair.append(e / jnp.sum(e, axis=0, keepdims=True))
        return pair

    def pair_of(g, sub, lo):
        return [qkv[g, sub, at + lo : at + lo + 128] for at in (0, 256, 512)]

    def attn_fwd(g):
        def rows_step(i, _):
            for u in range(4):
                sub = rows_of(i * 4 + u, 128)
                for lo in (0, 128):
                    q, k, v = pair_of(g, sub, lo)
                    pr = spread(probabilities(q, both(k)))
                    out = tn(pr, both(v)).astype(jnp.bfloat16)
                    mixed[sub, pl.ds(pl.multiple_of(g * 256 + lo, 128), 128)] = out
            return 0
        lax.fori_loop(0, 2, rows_step, 0)

    def attn_bwd(g):
        def rows_step(i, _):
            for u in range(4):
                sub = rows_of(i * 4 + u, 128)
                for lo in (0, 128):
                    q, k, v = pair_of(g, sub, lo)
                    do = mixed[sub, pl.ds(pl.multiple_of(g * 256 + lo, 128), 128)]
                    kk = both(k)
                    pr = probabilities(q, kk)
                    full = nt(both(v), do)
                    ds = []
                    for h in range(2):
                        d = compact(full, h)
                        ds.append(pr[h] * (d - jnp.sum(d * pr[h], axis=0, keepdims=True)))
                    ds = spread(ds)
                    dq = tn(ds, kk) * head_scale
                    dk = mm(ds, q)
                    dv = mm(spread(pr), do)
                    qkv[g, sub, lo : lo + 128] = dq.astype(jnp.bfloat16)
                    qkv[g, sub, 256 + lo : 384 + lo] = (
                        jnp.where(lane_low, dk[:128], dk[128:]) * head_scale
                    ).astype(jnp.bfloat16)
                    qkv[g, sub, 512 + lo : 640 + lo] = jnp.where(lane_low, dv[:128], dv[128:]).astype(jnp.bfloat16)
            return 0
        lax.fori_loop(0, 2, rows_step, 0)

    def qkv_group(g, _):
        slot = (1 + g) % 2
        load_copy(1 + g, slot).wait()

        def rows_step(i, _):
            rows = rows_of(i, 256)
            qkv[g, rows, :] = mm(n1[rows, :], wbuf[slot].reshape(1024, WIDE)).astype(jnp.bfloat16)
            return 0

        lax.fori_loop(0, 4, rows_step, 0)
        attn_fwd(g)
        ag_tick(6 + g)
        return 0

    lax.fori_loop(0, 4, qkv_group, 0)

    load_copy(5, 1).wait()

    def after(i, _):
        rows = rows_of(i, 256)
        m = mixed[rows, :]
        a = lin[rows, 0:WIDE] + mm(m, wbuf[1].reshape(1024, WIDE))
        b = lin[rows, WIDE:1024] + mm(m, wtail[...])
        x = jnp.concatenate([a, b], axis=1)
        aft[rows, :] = x
        oacc[rows, :] = x
        x3 = x.reshape(32, 8, 1024)
        r = lax.rsqrt(jnp.mean(x3 * x3, axis=-1, keepdims=True) + epsilon)
        n = (x3 * r * gain_two[...].astype(jnp.float32)[None]).reshape(256, 1024).astype(jnp.bfloat16)
        n2[rows, :] = n
        n2t[0:1024, rows] = n.T
        mixt[:, rows] = m.T
        return 0

    lax.fori_loop(0, 4, after, 0)
    ag_tick(10)

    def feed(j, _):
        slot = j % 2
        load_copy(6 + j, slot).wait()
        part_free(j)
        two = j % 2

        def rows_step(i, _):
            rows = rows_of(i, 512)
            w_gu = wbuf[slot, :, :, :, :, :, 0:512].reshape(1024, 512)
            pre = mm(n2[rows, :], w_gu)
            gate, up = pre[:, :256], pre[:, 256:]
            g_hid = jnp.zeros((512, 256), jnp.float32)
            for q in range(4):
                w_q = wbuf[slot, :, :, :, :, q * 16 : q * 16 + 16, 512:768].reshape(256, 256)
                g_hid = g_hid + nt(cot[rows, q * 256 : q * 256 + 256], w_q)
            sig = jax.nn.sigmoid(gate)
            silu = gate * sig
            hid = (silu * up).astype(jnp.bfloat16)
            g_gate = (g_hid * up * sig * (1.0 + gate * (1.0 - sig))).astype(jnp.bfloat16)
            g_up = (g_hid * silu).astype(jnp.bfloat16)
            for q in range(4):
                w_q = wbuf[slot, :, :, :, :, q * 16 : q * 16 + 16, 512:768].reshape(256, 256)
                oacc[rows, q * 256 : q * 256 + 256] += mm(hid, w_q)
            both_g = jnp.concatenate([g_gate, g_up], axis=1)
            n1[rows, 0:512] = both_g
            hidt[:, rows] = hid.T
            back = nt(both_g, w_gu)
            @pl.when(j == 0)
            def _():
                gn[rows, :] = back
            @pl.when(j > 0)
            def _():
                gn[rows, :] += back
            return 0

        lax.fori_loop(0, 2, rows_step, 0)

        def weight_step(m, _):
            res = mm(n2t[rows_of(m, 512), :], n1[:, 0:512]).astype(jnp.bfloat16).reshape(2, 2, 2, 64, 512)
            part[two, m, :, :, :, :, 0:512] = res
            return 0

        lax.fori_loop(0, 2, weight_step, 0)
        for q in range(4):
            res = mm(hidt[...], cot[:, q * 256 : q * 256 + 256]).astype(jnp.bfloat16)
            part[two, :, :, :, :, q * 16 : q * 16 + 16, 512:768] = res.reshape(2, 2, 2, 2, 16, 256)
        ag_tick(11 + j)
        rs_tick(j)
        return 0

    lax.fori_loop(0, FEED, feed, 0)
    load_copy(5, 1).start()
    load_copy(1, 0).start()

    def norm2_back(i, _):
        rows = rows_of(i, 128)
        n2t[rows, :] = oacc[rows, :].astype(jnp.bfloat16)
        x = aft[rows, :].reshape(16, 8, 1024)
        g = gn[rows, :].reshape(16, 8, 1024)
        r = lax.rsqrt(jnp.mean(x * x, axis=-1, keepdims=True) + epsilon)
        unit = x * r
        gacc[8:16, :] += jnp.sum(g * unit, axis=0)
        gu = g * gain_two[...].astype(jnp.float32)[None]
        back = r * (gu - unit * jnp.mean(gu * unit, axis=-1, keepdims=True))
        total = cot[rows, :].astype(jnp.float32) + back.reshape(128, 1024)
        oacc[rows, :] = total
        n2[rows, :] = total.astype(jnp.bfloat16)
        return 0

    lax.fori_loop(0, 8, norm2_back, 0)
    mixed_copy = pltpu.make_async_copy(n2t.at[0:1024], mixed_hbm, out_sem.at[0])
    mixed_copy.start()

    part_free(11)

    def out_weight_step(m, _):
        res = mm(mixt[rows_of(m, 256), :], n2[:, 0:WIDE]).astype(jnp.bfloat16)
        part[1, m // 2, m % 2] = res.reshape(2, 2, 64, WIDE)
        return 0

    lax.fori_loop(0, 4, out_weight_step, 0)
    rs_tick(11)

    def mixed_back(i, _):
        rows = rows_of(i, 256)
        g = n2[rows, :]
        res = nt(g[:, 0:WIDE], wbuf[1].reshape(1024, WIDE)) + nt(g[:, WIDE:1024], wtail[...])
        mixed[rows, :] = res.astype(jnp.bfloat16)
        return 0

    load_copy(5, 1).wait()
    lax.fori_loop(0, 4, mixed_back, 0)
    load_copy(2, 1).start()

    def qkv_back(g, _):
        slot = g % 2
        attn_bwd(g)
        part_free(12 + g)
        two = g % 2

        def weight_step(m, _):
            res = mm(n1t[rows_of(m, 256), :], qkv[g]).astype(jnp.bfloat16)
            part[two, m // 2, m % 2] = res.reshape(2, 2, 64, WIDE)
            return 0

        lax.fori_loop(0, 4, weight_step, 0)
        rs_tick(12 + g)

        def rows_step(i, _):
            rows = rows_of(i, 256)
            back = nt(qkv[g, rows, :], wbuf[slot].reshape(1024, WIDE))
            @pl.when(g == 0)
            def _():
                gn[rows, :] = back
            @pl.when(g > 0)
            def _():
                gn[rows, :] += back
            return 0

        load_copy(1 + g, slot).wait()
        lax.fori_loop(0, 4, rows_step, 0)
        pl.when(g < 2)(lambda: load_copy(3 + g, slot).start())
        pl.when(g == 2)(lambda: load_copy(0, 0).start())
        return 0

    lax.fori_loop(0, 4, qkv_back, 0)

    def norm1_back(i, _):
        rows = rows_of(i, 128)
        x = lin[rows, :].reshape(16, 8, 1024)
        g = gn[rows, :].reshape(16, 8, 1024)
        r = lax.rsqrt(jnp.mean(x * x, axis=-1, keepdims=True) + epsilon)
        unit = x * r
        gacc[0:8, :] += jnp.sum(g * unit, axis=0)
        gu = g * gain_one[...].astype(jnp.float32)[None]
        back = r * (gu - unit * jnp.mean(gu * unit, axis=-1, keepdims=True))
        total = oacc[rows, :].reshape(16, 8, 1024) + back
        oacc[rows, :] = total.reshape(128, 1024)
        shift[rows_of(i, 16), :] = jnp.sum(total, axis=1)
        return 0

    lax.fori_loop(0, 8, norm1_back, 0)
    pl.when(has_prev)(lambda: halo_copy.start())
    xsend[1] = shift[...].astype(jnp.bfloat16)
    x_copy(1).start()

    def gain_copy(i):
        return remote(gsend.at[i], grecv.at[i], g_ss.at[i], g_rs.at[i], partners[i])

    gsend[0] = gacc[...]
    gain_copy(0).start()

    load_copy(0, 0).wait()
    part_free(16)

    def out_tail_step(m, _):
        res = mm(mixt[rows_of(m, 256), :], n2[:, WIDE:1024]).astype(jnp.bfloat16)
        part[0, m // 2, m % 2, :, :, :, 512:768] = res.reshape(2, 2, 64, 256)
        return 0

    lax.fori_loop(0, 4, out_tail_step, 0)

    x_copy(1).wait_recv()
    g_low = (shift[...] + xrecv[1].astype(jnp.float32)).astype(jnp.bfloat16)
    ctx_t = ctx[...].T
    for h in range(2):
        gh = g_low[:, h * 512 : (h + 1) * 512]
        res = mm(ctx_t, gh).astype(jnp.bfloat16).reshape(2, 2, 2, 2, 32, 512)
        part[0, :, :, :, :, h * 32 : h * 32 + 32, 0:512] = res
    rs_tick(16)
    w0 = wbuf[0, :, :, :, :, 0:32, 0:512].reshape(512, 512)
    w1 = wbuf[0, :, :, :, :, 32:64, 0:512].reshape(512, 512)
    dctx[...] = nt(g_low[:, :512], w0) + nt(g_low[:, 512:], w1)

    def dtok(i, _):
        rows = rows_of(i, 128)
        near = oacc[pl.ds(pl.multiple_of(i * 128, 128), 144), :]
        frame = frame_of(i)
        x = jnp.zeros((16, 8, 1024), jnp.float32)
        for j in range(3):
            keep = wait == j
            if j > 0:
                keep = jnp.logical_and(keep, same_item(frame + j, j))
            x = jnp.where(keep, near[8 * j : 128 + 8 * j].reshape(16, 8, 1024), x)
        gn[rows, :] = x.reshape(128, 1024)
        return 0

    dtok_copy = pltpu.make_async_copy(gn, dtok_hbm, out_sem.at[1])
    feed_out = [out_copy(pair, 2 + i) for i, pair in enumerate(feed_copies())]
    for i in range(4):
        gain_copy(i).wait_recv()
        if i < 3:
            gsend[i + 1] = gsend[i] + grecv[i]
            gain_copy(i + 1).start()
        else:
            total = gsend[i] + grecv[i]
            dgain_one[...] = total[0:8]
            dgain_two[...] = total[8:16]
        rs_tick(17 + i)
        if i == 0:
            unpack_feed()
            for cp in feed_out:
                cp.start()
            pl.when(has_next)(lambda: halo_copy.wait_recv())
            lax.fori_loop(0, 8, dtok, 0)
            dtok_copy.start()

    last_out = [out_copy(pair, 9 + i) for i, pair in enumerate(out_copies())]
    for cp in last_out:
        cp.start()
    pl.when(has_next)(lambda: rim_copy.wait_send())
    pl.when(has_prev)(lambda: halo_copy.wait_send())

    for i in range(4):
        gain_copy(i).wait_send()
    for i in range(2):
        x_copy(i).wait_send()

    for stage in range(4):
        for k in (CHUNKS - 2, CHUNKS - 1):
            wait_send_all(rs_copies(stage, k))

    def drain(k, _):
        for stage in range(4):
            wait_send_all(ag_copies(stage, k))
        return 0

    lax.fori_loop(0, CHUNKS, drain, 0)
    mixed_copy.wait()
    dtok_copy.wait()
    for cp in feed_out + last_out:
        cp.wait()


def call_layer(tok, ctx, gain_one, gain_two, cot, weights, delay, lengths):
    f32, bf16 = jnp.float32, jnp.bfloat16
    vm, dma = pltpu.VMEM, pltpu.SemaphoreType.DMA
    shape = jax.ShapeDtypeStruct
    in_vmem, in_hbm, in_smem = (pl.BlockSpec(memory_space=m) for m in (pltpu.VMEM, pltpu.HBM, pltpu.SMEM))
    return pl.pallas_call(
        layer_kernel,
        name="layer",
        out_shape=(
            shape((1024, 1024), bf16),
            shape((1024, 1024), f32),
            shape((128, 512), f32),
            shape((32, 1024), f32),
            shape((8, 1024), f32),
            shape((8, 1024), f32),
            shape((64, 3072), f32),
            shape((64, 1024), f32),
            shape((64, 2816), f32),
            shape((64, 2816), f32),
            shape((176, 1024), f32),
            shape((CHUNKS, 2, 2, 2, 2, 64, WIDE), bf16),
        ),
        in_specs=[in_hbm] + [in_vmem] * 10 + [in_smem] * 2,
        out_specs=(in_hbm, in_hbm, in_vmem, in_hbm, in_vmem, in_vmem) + (in_hbm,) * 6,
        scratch_shapes=[
            vm((CHUNKS, 64, WIDE), bf16),
            vm((1024, 1024), f32),
            vm((1024, 1024), bf16),
            vm((1024, 1024), bf16),
            vm((4, 1024, WIDE), bf16),
            vm((1024, 1024), bf16),
            vm((1024, 1024), bf16),
            vm((1024, 1024), f32),
            vm((1024, 1024), bf16),
            vm((1040, 1024), bf16),
            vm((1040, 1024), f32),
            vm((1024, 1024), f32),
            vm((2, 2, 2, 2, 2, 64, WIDE), bf16),
            vm((1024, 256), bf16),
            vm((2, 2, 2, 2, 2, 64, WIDE), bf16),
            vm((256, 1024), bf16),
            vm((128, 1024), f32),
            vm((16, 1024), f32),
            vm((4, 16, 1024), f32),
            vm((4, 16, 1024), f32),
            vm((2, 128, 1024), bf16),
            vm((2, 128, 1024), bf16),
            vm((2, 2, 2, 2, 64, WIDE), bf16),
            vm((ROUNDS, 4, 64, WIDE), bf16),
            vm((ROUNDS, 2, 64, WIDE), bf16),
            vm((ROUNDS, 64, WIDE), bf16),
            vm((2, 4, 64, WIDE), bf16),
            vm((2, 4, 64, WIDE), bf16),
            vm((2, 2, 64, WIDE), bf16),
            vm((2, 2, 64, WIDE), bf16),
            vm((2, 64, WIDE), bf16),
            vm((2, 64, WIDE), bf16),
            vm((FEED, 64, WIDE), f32),
            dma((6, CHUNKS)),
            dma((6, CHUNKS)),
            dma((6, 2)),
            dma((6, ROUNDS)),
            dma((2,)),
            dma((2,)),
            dma((4,)),
            dma((4,)),
            dma((2,)),
            dma((2,)),
            dma,
            dma((2,)),
            dma((2,)),
            dma((14,)),
        ],
        compiler_params=pltpu.CompilerParams(
            collective_id=0, has_side_effects=True, vmem_limit_bytes=63 * 1024 * 1024
        ),
    )(tok, ctx, gain_one, gain_two, cot, *weights, delay, lengths)


def body_kernel(
    tokens,
    context,
    ctx_weight,
    delay,
    lengths,
    attn_gain,
    ffn_gain,
    qkv_weight,
    out_weight,
    gate_weight,
    up_weight,
    down_weight,
    cotangent,
):
    frame_count, positions, width = tokens.shape[1:]
    rows = frame_count * positions
    weights = (ctx_weight, qkv_weight[0], out_weight[0], gate_weight[0], up_weight[0], down_weight[0])
    mixed_out, d_tokens, d_context, d_ctx, d_gain_one, d_gain_two, *grads = call_layer(
        tokens.reshape(rows, width),
        context,
        attn_gain[0],
        ffn_gain[0],
        cotangent.reshape(rows, width),
        weights,
        delay,
        lengths,
    )
    d_qkv, d_out, d_gate, d_up, d_down, _ = grads
    return (
        mixed_out.reshape(tokens.shape),
        d_tokens.reshape(tokens.shape),
        d_context,
        d_ctx,
        d_gain_one[None],
        d_gain_two[None],
        d_qkv[None],
        d_out[None],
        d_gate[None],
        d_up[None],
        d_down[None],
    )


def body(
    tokens,
    context,
    ctx_weight,
    delay,
    lengths,
    attn_gain,
    ffn_gain,
    qkv_weight,
    out_weight,
    gate_weight,
    up_weight,
    down_weight,
    cotangent,
):
    frame_count = tokens.shape[1]
    positions = tokens.shape[2]
    model_width = tokens.shape[3]
    token_rows = frame_count * positions
    head_scale = HEAD ** (-0.5)
    ctx_full = lax.all_gather(context, "stream", axis=1, tiled=True)
    ctx_rows = lax.all_gather(ctx_weight, ("stream", "frames"), axis=0, tiled=True)
    shift_term = flat_dot(ctx_full, ctx_rows)
    inputs = tokens[0]
    rim_rows = shifted(inputs[frame_count - 2 :], "frames", 1)
    extended = jnp.concatenate([rim_rows, inputs], axis=0).astype(jnp.float32)
    frame_ids = lax.axis_index("frames") * frame_count + jnp.arange(frame_count, dtype=jnp.int32)
    chosen, valid_rows = shift_tables(delay, lengths, frame_ids)
    layer_in = jnp.broadcast_to(shift_term[:, None, :], (frame_count, positions, model_width))
    for offset in range(3):
        piece = extended[2 - offset : 2 - offset + frame_count]
        layer_in = (
            layer_in + chosen[offset][None, :, None] * valid_rows[offset][:, None, None] * piece
        )
    weights = (
        lax.all_gather(qkv_weight[0], "frames", axis=0, tiled=True),
        lax.all_gather(out_weight[0], "frames", axis=0, tiled=True),
        lax.all_gather(gate_weight[0], "frames", axis=0, tiled=True),
        lax.all_gather(up_weight[0], "frames", axis=0, tiled=True),
        lax.all_gather(down_weight[0], "frames", axis=0, tiled=True),
    )
    w_qkv, w_out, w_gate, w_up, w_down = weights
    gain_one = attn_gain[0].astype(jnp.float32)
    gain_two = ffn_gain[0].astype(jnp.float32)
    normed = norm_rows(layer_in, gain_one).astype(jnp.bfloat16).reshape(token_rows, model_width)
    qkv = (
        flat_dot(normed, w_qkv).astype(jnp.bfloat16).reshape(frame_count, positions, 3, HEADS, HEAD)
    )
    queries = qkv[:, :, 0]
    key_part = qkv[:, :, 1]
    values = qkv[:, :, 2]
    scores = (
        jnp.einsum("fqhd,fkhd->fhqk", queries, key_part, preferred_element_type=jnp.float32)
        * head_scale
    )
    causal = jnp.arange(positions)[:, None] >= jnp.arange(positions)[None, :]
    scores = jnp.where(causal[None, None], scores, -1e30)
    probs = jax.nn.softmax(scores, axis=-1)
    probs_low = probs.astype(jnp.bfloat16)
    mixed = jnp.einsum("fhqk,fkhd->fqhd", probs_low, values, preferred_element_type=jnp.float32)
    mixed = mixed.astype(jnp.bfloat16).reshape(token_rows, model_width)
    after_attn = layer_in + flat_dot(mixed, w_out).reshape(frame_count, positions, model_width)
    normed_two = (
        norm_rows(after_attn, gain_two).astype(jnp.bfloat16).reshape(token_rows, model_width)
    )
    gate_pre = flat_dot(normed_two, w_gate)
    up_pre = flat_dot(normed_two, w_up)
    hidden = (jax.nn.silu(gate_pre) * up_pre).astype(jnp.bfloat16)
    out_full = after_attn + flat_dot(hidden, w_down).reshape(frame_count, positions, model_width)
    b_qkv, b_out, b_gate, b_up, b_down = weights
    grad_out = cotangent[0].astype(jnp.float32)
    grad_ff = grad_out.reshape(token_rows, model_width).astype(jnp.bfloat16)
    grad_down = trans_dot(hidden, grad_ff)
    grad_hidden = back_dot(grad_ff, b_down)
    sigmoid_gate = jax.nn.sigmoid(gate_pre)
    grad_gate = (
        grad_hidden * up_pre * sigmoid_gate * (1.0 + gate_pre * (1.0 - sigmoid_gate))
    ).astype(jnp.bfloat16)
    grad_up = (grad_hidden * gate_pre * sigmoid_gate).astype(jnp.bfloat16)
    grad_gate_w = trans_dot(normed_two, grad_gate)
    grad_up_w = trans_dot(normed_two, grad_up)
    grad_normed_two = (back_dot(grad_gate, b_gate) + back_dot(grad_up, b_up)).reshape(
        frame_count, positions, model_width
    )
    grad_after_norm, grad_gain_two = norm_back(grad_normed_two, after_attn, gain_two)
    grad_after = grad_out + grad_after_norm
    grad_branch = grad_after.reshape(token_rows, model_width).astype(jnp.bfloat16)
    grad_out_w = trans_dot(mixed, grad_branch)
    grad_mixed = (
        back_dot(grad_branch, b_out)
        .astype(jnp.bfloat16)
        .reshape(frame_count, positions, HEADS, HEAD)
    )
    grad_values = jnp.einsum(
        "fhqk,fqhd->fkhd", probs_low, grad_mixed, preferred_element_type=jnp.float32
    )
    grad_probs = jnp.einsum(
        "fqhd,fkhd->fhqk", grad_mixed, values, preferred_element_type=jnp.float32
    )
    grad_scores = (
        probs * (grad_probs - jnp.sum(grad_probs * probs, axis=-1, keepdims=True))
    ).astype(jnp.bfloat16)
    grad_queries = (
        jnp.einsum("fhqk,fkhd->fqhd", grad_scores, key_part, preferred_element_type=jnp.float32)
        * head_scale
    )
    grad_keys = (
        jnp.einsum("fhqk,fqhd->fkhd", grad_scores, queries, preferred_element_type=jnp.float32)
        * head_scale
    )
    grad_qkv = jnp.stack([grad_queries, grad_keys, grad_values], axis=2).astype(jnp.bfloat16)
    grad_qkv = grad_qkv.reshape(token_rows, 3 * model_width)
    grad_qkv_w = trans_dot(normed, grad_qkv)
    all_parts = (
        lax.psum_scatter(grad_qkv_w, "frames", scatter_dimension=0, tiled=True),
        lax.psum_scatter(grad_out_w, "frames", scatter_dimension=0, tiled=True),
        lax.psum_scatter(grad_gate_w, "frames", scatter_dimension=0, tiled=True),
        lax.psum_scatter(grad_up_w, "frames", scatter_dimension=0, tiled=True),
        lax.psum_scatter(grad_down, "frames", scatter_dimension=0, tiled=True),
    )
    d_qkv_rows, d_out_rows, d_gate_rows, d_up_rows, d_down_rows = all_parts
    grad_normed = back_dot(grad_qkv, b_qkv).reshape(frame_count, positions, model_width)
    grad_in_norm, grad_gain_one = norm_back(grad_normed, layer_in, gain_one)
    grad_in = grad_after + grad_in_norm
    gain_sums = lax.psum((grad_gain_one, grad_gain_two), "frames")
    grad_shift = jnp.sum(grad_in, axis=1).astype(jnp.bfloat16)
    grad_ctx_w = trans_dot(ctx_full, grad_shift)
    ctx_w_rows = lax.psum_scatter(grad_ctx_w, ("stream", "frames"), scatter_dimension=0, tiled=True)
    grad_context = back_dot(grad_shift, ctx_rows)
    context_half = lax.psum_scatter(
        grad_context.astype(jnp.bfloat16), "stream", scatter_dimension=1, tiled=True
    ).astype(jnp.float32)
    grad_ext = jnp.zeros((frame_count + 2, positions, model_width), jnp.float32)
    for offset in range(3):
        term = chosen[offset][None, :, None] * valid_rows[offset][:, None, None] * grad_in
        grad_ext = grad_ext + jnp.pad(term, ((2 - offset, offset), (0, 0), (0, 0)))
    back_rows = shifted(grad_ext[:2].astype(jnp.bfloat16), "frames", -1).astype(jnp.float32)
    grad_tokens = grad_ext[2:].at[frame_count - 2 :].add(back_rows)
    return (
        out_full.astype(jnp.bfloat16)[None],
        grad_tokens[None],
        context_half,
        ctx_w_rows,
        gain_sums[0][None],
        gain_sums[1][None],
        d_qkv_rows[None],
        d_out_rows[None],
        d_gate_rows[None],
        d_up_rows[None],
        d_down_rows[None],
    )


def solution(mesh):
    fits = mesh.shape["frames"] == 16 and mesh.shape["stream"] == 2
    return jax.shard_map(
        body_kernel if fits else body,
        mesh=mesh,
        in_specs=(
            P("stream", "frames", None, None),
            P("frames", "stream"),
            P(("stream", "frames"), None),
            P(),
            P(),
            P("stream", None, None),
            P("stream", None, None),
            P("stream", "frames", None),
            P("stream", "frames", None),
            P("stream", "frames", None),
            P("stream", "frames", None),
            P("stream", "frames", None),
            P("stream", "frames", None, None),
        ),
        out_specs=(
            P("stream", "frames", None, None),
            P("stream", "frames", None, None),
            P("frames", "stream"),
            P(("stream", "frames"), None),
            P("stream", None, None),
            P("stream", None, None),
            P("stream", "frames", None),
            P("stream", "frames", None),
            P("stream", "frames", None),
            P("stream", "frames", None),
            P("stream", "frames", None),
        ),
        check_vma=False,
    )
```

```python
import jax
import jax.numpy as jnp
from jax import lax
from jax.experimental import pallas as pl
from jax.experimental.pallas import tpu as pltpu
from jax.sharding import PartitionSpec as P

HEADS = 16
HEAD = 64


epsilon = 1e-05


def shifted(x, axis, by):
    length = lax.axis_size(axis)
    pairs = [(i, i + by) for i in range(length) if 0 <= i + by < length]
    return lax.ppermute(x, axis, pairs)


def flat_dot(left, right):
    return jnp.dot(left, right, preferred_element_type=jnp.float32)


def trans_dot(left, right):
    return lax.dot_general(
        left, right, (((0,), (0,)), ((), ())), preferred_element_type=jnp.float32
    )


def back_dot(left, right):
    return lax.dot_general(
        left, right, (((1,), (1,)), ((), ())), preferred_element_type=jnp.float32
    )


def norm_rows(rows, gain):
    return rows * lax.rsqrt(jnp.mean(rows * rows, axis=-1, keepdims=True) + epsilon) * gain


def norm_back(grad_normed, rows, gain):
    scale = lax.rsqrt(jnp.mean(rows * rows, axis=-1, keepdims=True) + epsilon)
    unit = rows * scale
    grad_gain = jnp.sum(grad_normed * unit, axis=0)
    grad_unit = grad_normed * gain
    grad_rows = scale * (grad_unit - unit * jnp.mean(grad_unit * unit, axis=-1, keepdims=True))
    return (grad_rows, grad_gain)


def shift_tables(delay, lengths, frame_ids):
    starts = jnp.cumsum(lengths) - lengths
    at_start = jnp.any(frame_ids[:, None] == starts[None, :], axis=1)
    after_start = jnp.any(frame_ids[:, None] - 1 == starts[None, :], axis=1)
    keep_one = jnp.logical_not(at_start)
    keep_two = jnp.logical_and(keep_one, jnp.logical_not(after_start))
    valid_rows = jnp.stack([jnp.ones_like(keep_one), keep_one, keep_two]).astype(jnp.float32)
    chosen = (delay[None, :] == jnp.arange(3, dtype=jnp.int32)[:, None]).astype(jnp.float32)
    return (chosen, valid_rows)


MESH = pl.DeviceIdType.MESH
CHUNKS = 17
FEED = 11
WIDE = 768
ROUNDS = 5
MOST = 48
SPLIT = ((0, MOST), (MOST, 64))


def mm(a, b):
    return jnp.dot(a, b, preferred_element_type=jnp.float32)


def nt(a, b):
    return lax.dot_general(a, b, (((1,), (1,)), ((), ())), preferred_element_type=jnp.float32)


def tn(a, b):
    return lax.dot_general(a, b, (((0,), (0,)), ((), ())), preferred_element_type=jnp.float32)


def either(cond, fn):
    if isinstance(cond, bool):
        if cond:
            fn()
    else:
        pl.when(cond)(fn)


def within(t, low, high):
    if isinstance(t, int):
        return low <= t < high
    return jnp.logical_and(t >= low, t < high)


def layer_kernel(
    tok_hbm,
    ctx,
    gain_one,
    gain_two,
    cot_hbm,
    ctx_own,
    qkv_own,
    out_own,
    gate_hbm,
    up_hbm,
    down_hbm,
    delay,
    lengths,
    mixed_hbm,
    dtok_hbm,
    dctx,
    dctxw_hbm,
    dgain_one,
    dgain_two,
    dqkv_hbm,
    dout_hbm,
    dgate_hbm,
    dup_hbm,
    ddown_hbm,
    gathered,
    pend,
    cot,
    gate_own,
    up_own,
    down_own,
    w_own,
    lin,
    n1,
    n1t,
    qkv,
    mixed,
    aft,
    n2,
    n2t,
    oacc,
    gn,
    wbuf,
    wtail,
    part,
    part_own,
    hidt,
    shift,
    gacc,
    gsend,
    grecv,
    xsend,
    xrecv,
    r_c,
    r_y,
    r_zl,
    r_zh,
    t_keep,
    t_send,
    u_keep,
    u_send,
    v_keep,
    v_send,
    fin,
    ag_ss,
    ag_rs,
    rs_ss,
    rs_rs,
    x_ss,
    x_rs,
    g_ss,
    g_rs,
    own_sem,
    load_sem,
    pend_sem,
    half_sem,
    tok_sem,
    in_sem,
    rim_ss,
    rim_rs,
    out_sem,
):
    s = lax.axis_index("stream")
    f = lax.axis_index("frames")
    c = f % 2
    y = (f // 2) % 2
    zl = (f // 4) % 2
    zh = f // 8
    d_c = (s, f + 1 - 2 * c)
    d_y = (s, f + 2 - 4 * y)
    d_zl = (s, f + 4 - 8 * zl)
    d_zh = (s, f + 8 - 16 * zh)
    d_x = (1 - s, f)
    partners = (d_zh, d_zl, d_y, d_c)

    frames = lax.axis_size("frames")
    has_next, has_prev = f < frames - 1, f > 0
    d_next, d_prev = (s, f + 1), (s, f - 1)

    tokext = n2t
    tok_copy = pltpu.make_async_copy(tok_hbm, tokext.at[16:1040], tok_sem)
    fetches = [
        pltpu.make_async_copy(src, dst, in_sem.at[i])
        for i, (src, dst) in enumerate(
            ((down_hbm, down_own), (gate_hbm, gate_own), (up_hbm, up_own), (cot_hbm, cot))
        )
    ]
    for cp in fetches:
        cp.start()
    tok_copy.start()

    barrier = pltpu.get_barrier_semaphore()

    def greet(device):
        pl.semaphore_signal(barrier, inc=1, device_id=device, device_id_type=MESH)

    for device in partners + (d_x,):
        greet(device)
    pl.when(has_next)(lambda: greet(d_next))
    pl.when(has_prev)(lambda: greet(d_prev))

    w_own[0, 0:32, 0:512] = ctx_own[:, 0:512]
    w_own[0, 32:64, 0:512] = ctx_own[:, 512:1024]
    w_own[0, :, 512:768] = out_own[:, 768:1024]
    w_own[5] = out_own[:, 0:768]
    for g in range(4):
        for part_id in range(3):
            at = part_id * 1024 + g * 256
            w_own[1 + g, :, part_id * 256 : part_id * 256 + 256] = qkv_own[:, at : at + 256]

    def own_copy(low, high, i):
        return pltpu.make_async_copy(
            w_own.at[low:high], gathered.at[low:high, zh, zl, y, c], own_sem.at[i]
        )

    own_copy(0, 6, 0).start()

    pl.semaphore_wait(barrier, 5 + has_next.astype(jnp.int32) + has_prev.astype(jnp.int32))

    def remote(src, dst, ss, rs, device):
        return pltpu.make_async_remote_copy(
            src_ref=src, dst_ref=dst, send_sem=ss, recv_sem=rs, device_id=device, device_id_type=MESH
        )

    def ag_copies(stage, k):
        if stage == 0:
            triples = [(w_own.at[k], gathered.at[k, zh, zl, y, c], d_zh)]
        elif stage == 1:
            near, side = gathered.at[k, :, zl, y, c, 0:MOST], gathered.at[k, :, zl, y, c, MOST:64]
            triples = [(near, near, d_zl), (side, side, d_y)]
        elif stage == 2:
            side, near = gathered.at[k, :, :, y, c, 0:MOST], gathered.at[k, :, zl, :, c, MOST:64]
            triples = [(side, side, d_y), (near, near, d_zl)]
        else:
            own = gathered.at[k, :, :, :, c]
            triples = [(own, own, d_c)]
        first = (0, 1, 3, 5)[stage]
        return [
            remote(src, dst, ag_ss.at[first + i, k], ag_rs.at[first + i, k], device)
            for i, (src, dst, device) in enumerate(triples)
        ]

    def start_all(copies):
        for cp in copies:
            cp.start()

    def wait_recv_all(copies):
        for cp in copies:
            cp.wait_recv()

    def wait_send_all(copies):
        for cp in copies:
            cp.wait_send()

    class load_copy:
        def __init__(self, k, slot):
            self.parts = [
                pltpu.make_async_copy(
                    gathered.at[k, i // 2, i % 2], wbuf.at[slot, i // 2, i % 2], load_sem.at[slot, i]
                )
                for i in range(4)
            ]

        def start(self):
            for cp in self.parts:
                cp.start()

        def wait(self):
            for cp in self.parts:
                cp.wait()

    def ag_tick(t):
        for stage, lag in enumerate((0, 1, 2, 4)):
            def step(stage=stage, lag=lag):
                k = t - lag
                if stage > 0:
                    wait_recv_all(ag_copies(stage - 1, k))
                start_all(ag_copies(stage, k))
            either(within(t, lag, lag + CHUNKS), step)

    def ag_ready(k):
        def ready():
            wait_recv_all(ag_copies(3, k))
            load_copy(k, k % 2).start()
        either(within(k, 0, CHUNKS), ready)

    def rs_copies(stage, r):
        two, slot = r % (3 if stage == 1 else 2), r % ROUNDS
        if stage == 0:
            triples = [(pend.at[r, :, :, :, 1 - c], r_c.at[two], d_c)]
        elif stage == 3:
            triples = [(v_send.at[two], r_zh.at[slot], d_zh)]
        else:
            src, dst = ((t_send, r_y), (u_send, r_zl))[stage - 1]
            devices = ((d_y, d_zl), (d_zl, d_y))[stage - 1]
            triples = [
                (src.at[two, :, low:high], dst.at[slot, :, low:high], device)
                for (low, high), device in zip(SPLIT, devices)
            ]
        first = (0, 1, 3, 5)[stage]
        return [
            remote(src, dst, rs_ss.at[first + i, two], rs_rs.at[first + i, slot], device)
            for i, (src, dst, device) in enumerate(triples)
        ]

    def add(a, b):
        return a.astype(jnp.float32) + b.astype(jnp.float32)

    def place_result(k, res):
        if not isinstance(k, int):
            @pl.when(k < FEED)
            def _():
                fin[k] = res
            pl.when(k == FEED)(lambda: place_result(FEED, res))
            return
        if k < FEED:
            fin[k] = res
        elif k == FEED:
            aft[384:448, 0:768] = res
        elif k < CHUNKS - 1:
            g = k - FEED - 1
            for p in range(3):
                aft[192 + 64 * p : 256 + 64 * p, g * 256 : g * 256 + 256] = res[:, p * 256 : p * 256 + 256]
        else:
            aft[384:448, 768:1024] = res[:, 512:768]
            aft[448:480, 0:512] = res[0:32, 0:512]
            aft[448:480, 512:1024] = res[32:64, 0:512]

    def out_copies():
        pairs = [(aft.at[384:448], dout_hbm), (aft.at[448:480], dctxw_hbm)]
        for p in range(3):
            pairs.append((aft.at[192 + 64 * p : 256 + 64 * p], dqkv_hbm.at[:, p * 1024 : p * 1024 + 1024]))
        return pairs

    def feed_copies():
        pairs = [(aft.at[512:688], ddown_hbm)]
        for i, hbm in enumerate((dgate_hbm, dup_hbm)):
            at = i * 768
            if i == 1:
                at = 704
            for p in range(3):
                n = 1024 if p < 2 else 768
                pairs.append((aft.at[at + 64 * p : at + 64 * p + 64, 0:n], hbm.at[:, p * 1024 : p * 1024 + n]))
        return pairs

    def out_copy(pair, i):
        return pltpu.make_async_copy(pair[0], pair[1], out_sem.at[i])

    def unpack_feed():
        for j in range(FEED):
            for q in range(4):
                aft[512 + j * 16 : 528 + j * 16, q * 256 : q * 256 + 256] = fin[j, q * 16 : q * 16 + 16, 512:768]
        for i, at in enumerate((0, 704)):
            cols = [
                fin[j, :, i * 256 + d * 16 : i * 256 + d * 16 + 16] for d in range(16) for j in range(FEED)
            ]
            for p in range(22):
                piece = jnp.concatenate(cols[p * 8 : p * 8 + 8], axis=1)
                row, col = at + 64 * (p // 8), (p % 8) * 128
                aft[row : row + 64, col : col + 128] = piece

    def pend_copy(r):
        return pltpu.make_async_copy(part.at[r % 2], pend.at[r], pend_sem.at[r % 2])

    def half_copy(r):
        return pltpu.make_async_copy(pend.at[r, :, :, :, c], part_own.at[r % 2], half_sem.at[r % 2])

    def part_done(r):
        either(within(r, 1, CHUNKS), lambda: pend_copy(r - 1).wait())
        pend_copy(r).start()

    def send_half(r):
        either(within(r, 2, CHUNKS), lambda: wait_send_all(rs_copies(0, r - 2)))
        start_all(rs_copies(0, r))
        half_copy(r).start()

    def rs_tick(r):
        def stage_y():
            k = r - 1
            wait_recv_all(rs_copies(0, k))
            half_copy(k).wait()
            either(within(k, 3, CHUNKS), lambda: wait_send_all(rs_copies(1, k - 3)))
            two, three = k % 2, k % 3

            def piece(i, _):
                a, b = i // 2, i % 2
                for (low, high), send, keep in zip(
                    SPLIT, ((b, 1 - y), (1 - zl, b)), ((b, y), (zl, b))
                ):
                    for out, (m, n) in ((t_send, send), (t_keep, keep)):
                        out[three, i, low:high] = part_own[two, a, m, n, low:high] + r_c[two, a, m, n, low:high]
                return 0

            lax.fori_loop(0, 4, piece, 0)
            start_all(rs_copies(1, k))
        either(within(r, 1, CHUNKS + 1), stage_y)
        either(within(r, 0, CHUNKS), lambda: send_half(r))

        def stage_zl():
            k = r - 3
            wait_recv_all(rs_copies(1, k))
            either(within(k, 2, CHUNKS), lambda: wait_send_all(rs_copies(2, k - 2)))
            two, three, slot = k % 2, k % 3, k % ROUNDS
            for a in range(2):
                for (low, high), mine in zip(SPLIT, (zl, y)):
                    for out, at in ((u_send, a * 2 + 1 - mine), (u_keep, a * 2 + mine)):
                        out[two, a, low:high] = t_keep[three, at, low:high] + r_y[slot, at, low:high]
            start_all(rs_copies(2, k))
        either(within(r, 3, CHUNKS + 3), stage_zl)

        def stage_zh():
            k = r - 4
            wait_recv_all(rs_copies(2, k))
            either(within(k, 2, CHUNKS), lambda: wait_send_all(rs_copies(3, k - 2)))
            two, slot = k % 2, k % ROUNDS
            v_send[two] = u_keep[two, 1 - zh] + r_zl[slot, 1 - zh]
            v_keep[two] = u_keep[two, zh] + r_zl[slot, zh]
            start_all(rs_copies(3, k))
        either(within(r, 4, CHUNKS + 4), stage_zh)

        def last():
            k = r - 5
            wait_recv_all(rs_copies(3, k))
            place_result(k, add(v_keep[k % 2], r_zh[k % ROUNDS]))
        either(within(r, 5, CHUNKS + 5), last)

    rim_copy = remote(tok_hbm.at[1008:1024], tokext.at[0:16], rim_ss.at[0], rim_rs.at[0], d_next)
    halo_copy = remote(oacc.at[0:16], oacc.at[1024:1040], rim_ss.at[1], rim_rs.at[1], d_prev)
    pl.when(has_next)(lambda: rim_copy.start())

    @pl.when(jnp.logical_not(has_prev))
    def _():
        tokext[0:16, :] = jnp.zeros((16, 1024), jnp.bfloat16)

    @pl.when(jnp.logical_not(has_next))
    def _():
        oacc[1024:1040, :] = jnp.zeros((16, 1024), jnp.float32)

    gacc[...] = jnp.zeros_like(gacc)

    place = lax.broadcasted_iota(jnp.int32, (16, 8, 1), 1)
    wait = jnp.zeros((16, 8, 1), jnp.int32)
    for p in range(8):
        wait = jnp.where(place == p, delay[p], wait)

    def starts_at(frame):
        start = jnp.int32(0)
        hit = frame == start
        for i in range(lengths.shape[0] - 1):
            start = start + lengths[i]
            hit = jnp.logical_or(hit, frame == start)
        return hit

    def same_item(frame, j):
        ok = jnp.logical_not(starts_at(frame))
        if j == 2:
            ok = jnp.logical_and(ok, jnp.logical_not(starts_at(frame - 1)))
        return ok

    def frame_of(i):
        return f * 128 + i * 16 + lax.broadcasted_iota(jnp.int32, (16, 8, 1), 0)

    def pack_feed(own, at):
        for j in range(FEED):
            cols = [own[:, d * 176 + j * 16 : d * 176 + j * 16 + 16] for d in range(16)]
            w_own[6 + j, :, at : at + 256] = jnp.concatenate(cols, axis=1)

    ag_tick(0)
    own_copy(0, 6, 0).wait()
    ag_tick(1)
    for cp in fetches[:2]:
        cp.wait()
    for j in range(FEED):
        for q in range(4):
            w_own[6 + j, q * 16 : q * 16 + 16, 512:768] = down_own[
                j * 16 : j * 16 + 16, q * 256 : q * 256 + 256
            ]
    pack_feed(gate_own, 0)
    ag_tick(2)
    fetches[2].wait()
    pack_feed(up_own, 256)
    own_copy(6, CHUNKS, 1).start()
    ag_tick(3)
    ag_tick(4)
    ag_ready(0)
    own_copy(6, CHUNKS, 1).wait()

    load_copy(0, 0).wait()
    wtail[...] = wbuf[0, :, :, :, :, :, 512:768].reshape(1024, 256)
    half = shift.shape[1] // 2
    for h in range(2):
        w_half = wbuf[0, :, :, :, :, h * 32 : h * 32 + 32, 0:512].reshape(512, 512)
        shift[:, h * half : (h + 1) * half] = mm(ctx[...], w_half)
    xsend[0] = shift[...].astype(jnp.bfloat16)

    x_copy = remote(xsend.at[0], xrecv.at[0], x_ss.at[0], x_rs.at[0], d_x)
    x_copy.start()
    ag_tick(5)
    ag_ready(1)
    x_copy.wait_recv()
    shift[...] = shift[...] + xrecv[0].astype(jnp.float32)

    def rows_of(i, size):
        return pl.ds(pl.multiple_of(i * size, size), size)

    def norm1(i, _):
        rows = rows_of(i, 128)
        sh = shift[rows_of(i, 16), :]
        near = tokext[pl.ds(pl.multiple_of(i * 128, 128), 144), :].astype(jnp.float32)
        frame = frame_of(i)
        x = jnp.zeros((16, 8, 1024), jnp.float32)
        for j in range(3):
            keep = wait == j
            if j > 0:
                keep = jnp.logical_and(keep, same_item(frame, j))
            piece = near[16 - 8 * j : 144 - 8 * j].reshape(16, 8, 1024)
            x = jnp.where(keep, piece, x)
        x = x + sh[:, None, :]
        r = lax.rsqrt(jnp.mean(x * x, axis=-1, keepdims=True) + epsilon)
        n = (x * r * gain_one[...].astype(jnp.float32)[None]).reshape(128, 1024).astype(jnp.bfloat16)
        lin[rows, :] = x.reshape(128, 1024)
        n1[rows, :] = n
        n1t[:, rows] = n.T
        return 0

    tok_copy.wait()
    pl.when(has_prev)(lambda: rim_copy.wait_recv())
    lax.fori_loop(0, 8, norm1, 0)

    lane_low = lax.broadcasted_iota(jnp.int32, (128, 128), 1) < 64
    head_scale = HEAD ** (-0.5)

    def both(v):
        zero = jnp.zeros_like(v)
        return jnp.concatenate([jnp.where(lane_low, v, zero), jnp.where(lane_low, zero, v)], axis=0)

    own_frame = [
        lax.broadcasted_iota(jnp.int32, (8, 128), 1) // 8 == fr for fr in range(16)
    ]
    key_seen = lax.broadcasted_iota(jnp.int32, (8, 128), 0) <= lax.broadcasted_iota(jnp.int32, (8, 128), 1) % 8

    def compact(full, h):
        out = full[h * 128 : h * 128 + 8]
        for fr in range(1, 16):
            at = h * 128 + fr * 8
            out = jnp.where(own_frame[fr], full[at : at + 8], out)
        return out

    def spread(pair):
        zero = jnp.zeros((8, 128), jnp.float32)
        rows = [jnp.where(own_frame[fr], x, zero) for x in pair for fr in range(16)]
        return jnp.concatenate(rows, axis=0).astype(jnp.bfloat16)

    def probabilities(q, kk):
        full = nt(kk, q)
        pair = []
        for h in range(2):
            sc = jnp.where(key_seen, compact(full, h) * head_scale, -1e30)
            e = jnp.exp(sc - jnp.max(sc, axis=0, keepdims=True))
            pair.append(e / jnp.sum(e, axis=0, keepdims=True))
        return pair

    def pair_of(g, sub, lo):
        return [qkv[g, sub, at + lo : at + lo + 128] for at in (0, 256, 512)]

    def attn_fwd(g):
        def rows_step(i, _):
            for u in range(4):
                sub = rows_of(i * 4 + u, 128)
                for lo in (0, 128):
                    q, k, v = pair_of(g, sub, lo)
                    pr = spread(probabilities(q, both(k)))
                    out = tn(pr, both(v)).astype(jnp.bfloat16)
                    mixed[sub, pl.ds(pl.multiple_of(g * 256 + lo, 128), 128)] = out
            return 0
        lax.fori_loop(0, 2, rows_step, 0)

    def attn_bwd(g):
        def rows_step(i, _):
            for u in range(4):
                sub = rows_of(i * 4 + u, 128)
                for lo in (0, 128):
                    q, k, v = pair_of(g, sub, lo)
                    do = mixed[sub, pl.ds(pl.multiple_of(g * 256 + lo, 128), 128)]
                    kk = both(k)
                    pr = probabilities(q, kk)
                    full = nt(both(v), do)
                    ds = []
                    for h in range(2):
                        d = compact(full, h)
                        ds.append(pr[h] * (d - jnp.sum(d * pr[h], axis=0, keepdims=True)))
                    ds = spread(ds)
                    dq = tn(ds, kk) * head_scale
                    dk = mm(ds, q)
                    dv = mm(spread(pr), do)
                    qkv[g, sub, lo : lo + 128] = dq.astype(jnp.bfloat16)
                    qkv[g, sub, 256 + lo : 384 + lo] = (
                        jnp.where(lane_low, dk[:128], dk[128:]) * head_scale
                    ).astype(jnp.bfloat16)
                    qkv[g, sub, 512 + lo : 640 + lo] = jnp.where(lane_low, dv[:128], dv[128:]).astype(jnp.bfloat16)
            return 0
        lax.fori_loop(0, 2, rows_step, 0)

    def qkv_group(g, _):
        slot = (1 + g) % 2
        load_copy(1 + g, slot).wait()

        def rows_step(i, _):
            rows = rows_of(i, 256)
            qkv[g, rows, :] = mm(n1[rows, :], wbuf[slot].reshape(1024, WIDE)).astype(jnp.bfloat16)
            return 0

        lax.fori_loop(0, 4, rows_step, 0)
        ag_tick(6 + g)
        attn_fwd(g)
        ag_ready(2 + g)
        return 0

    lax.fori_loop(0, 4, qkv_group, 0)

    load_copy(5, 1).wait()

    def after(i, _):
        rows = rows_of(i, 256)
        m = mixed[rows, :]
        a = lin[rows, 0:WIDE] + mm(m, wbuf[1].reshape(1024, WIDE))
        b = lin[rows, WIDE:1024] + mm(m, wtail[...])
        x = jnp.concatenate([a, b], axis=1)
        aft[rows, :] = x
        oacc[rows, :] = x
        gn[rows, :] = jnp.zeros((256, 1024), jnp.float32)
        x3 = x.reshape(32, 8, 1024)
        r = lax.rsqrt(jnp.mean(x3 * x3, axis=-1, keepdims=True) + epsilon)
        n = (x3 * r * gain_two[...].astype(jnp.float32)[None]).reshape(256, 1024).astype(jnp.bfloat16)
        n2[rows, :] = n
        n2t[0:1024, rows] = n.T
        return 0

    lax.fori_loop(0, 2, after, 0)
    ag_tick(10)
    lax.fori_loop(2, 4, after, 0)
    ag_ready(6)
    fetches[3].wait()

    def feed(j, _):
        slot = j % 2
        load_copy(6 + j, slot).wait()
        two = j % 2

        def rows_step(i):
            rows = slice(i * 512, i * 512 + 512)
            w_gu = wbuf[slot, :, :, :, :, :, 0:512].reshape(1024, 512)
            pre = mm(n2[rows, :], w_gu)
            gate, up = pre[:, :256], pre[:, 256:]
            g_hid = jnp.zeros((512, 256), jnp.float32)
            for q in range(4):
                w_q = wbuf[slot, :, :, :, :, q * 16 : q * 16 + 16, 512:768].reshape(256, 256)
                g_hid = g_hid + nt(cot[rows, q * 256 : q * 256 + 256], w_q)
            sig = jax.nn.sigmoid(gate)
            silu = gate * sig
            hid = (silu * up).astype(jnp.bfloat16)
            g_gate = (g_hid * up * sig * (1.0 + gate * (1.0 - sig))).astype(jnp.bfloat16)
            g_up = (g_hid * silu).astype(jnp.bfloat16)
            for q in range(4):
                w_q = wbuf[slot, :, :, :, :, q * 16 : q * 16 + 16, 512:768].reshape(256, 256)
                oacc[rows, q * 256 : q * 256 + 256] += mm(hid, w_q)
            both_g = jnp.concatenate([g_gate, g_up], axis=1)
            n1[rows, 0:512] = both_g
            hidt[:, rows] = hid.T
            back = nt(both_g, w_gu)
            gn[rows, :] += back

        for i in range(2):
            rows_step(i)
        ag_tick(11 + j)

        def weight_step(m, _):
            res = mm(n2t[rows_of(m, 512), :], n1[:, 0:512]).astype(jnp.bfloat16).reshape(2, 2, 2, 64, 512)
            part[two, m, :, :, :, :, 0:512] = res
            return 0

        lax.fori_loop(0, 2, weight_step, 0)
        ag_ready(7 + j)
        for q in range(4):
            res = mm(hidt[...], cot[:, q * 256 : q * 256 + 256]).astype(jnp.bfloat16)
            part[two, :, :, :, :, q * 16 : q * 16 + 16, 512:768] = res.reshape(2, 2, 2, 2, 16, 256)
        part_done(j)
        pl.when(j % 2 == 1)(lambda: rs_tick(j // 2))
        return 0

    lax.fori_loop(0, FEED, feed, 0)
    load_copy(5, 1).start()
    load_copy(1, 0).start()

    def norm2_back(i, _):
        rows = rows_of(i, 128)
        n2t[rows, :] = oacc[rows, :].astype(jnp.bfloat16)
        n1[:, rows] = mixed[rows, :].T
        x = aft[rows, :].reshape(16, 8, 1024)
        g = gn[rows, :].reshape(16, 8, 1024)
        gn[rows, :] = jnp.zeros((128, 1024), jnp.float32)
        r = lax.rsqrt(jnp.mean(x * x, axis=-1, keepdims=True) + epsilon)
        unit = x * r
        gacc[8:16, :] += jnp.sum(g * unit, axis=0)
        gu = g * gain_two[...].astype(jnp.float32)[None]
        back = r * (gu - unit * jnp.mean(gu * unit, axis=-1, keepdims=True))
        total = cot[rows, :].astype(jnp.float32) + back.reshape(128, 1024)
        oacc[rows, :] = total
        n2[rows, :] = total.astype(jnp.bfloat16)
        return 0

    lax.fori_loop(0, 8, norm2_back, 0)
    mixed_copy = pltpu.make_async_copy(n2t.at[0:1024], mixed_hbm, out_sem.at[0])
    mixed_copy.start()
    rs_tick(5)


    def out_weight_step(m, _):
        res = mm(n1[rows_of(m, 256), :], n2[:, 0:WIDE]).astype(jnp.bfloat16)
        part[1, m // 2, m % 2] = res.reshape(2, 2, 64, WIDE)
        return 0

    lax.fori_loop(0, 4, out_weight_step, 0)
    part_done(11)

    def mixed_back(i, _):
        rows = rows_of(i, 256)
        g = n2[rows, :]
        res = nt(g[:, 0:WIDE], wbuf[1].reshape(1024, WIDE)) + nt(g[:, WIDE:1024], wtail[...])
        mixed[rows, :] = res.astype(jnp.bfloat16)
        return 0

    load_copy(5, 1).wait()
    lax.fori_loop(0, 4, mixed_back, 0)
    load_copy(2, 1).start()
    rs_tick(6)

    def qkv_back(g, _):
        slot = g % 2
        attn_bwd(g)
        rs_tick(7 + 2 * g)
        two = g % 2

        def weight_step(m, _):
            res = mm(n1t[rows_of(m, 256), :], qkv[g]).astype(jnp.bfloat16)
            part[two, m // 2, m % 2] = res.reshape(2, 2, 64, WIDE)
            return 0

        lax.fori_loop(0, 4, weight_step, 0)
        part_done(12 + g)

        def rows_step(i, _):
            rows = rows_of(i, 256)
            back = nt(qkv[g, rows, :], wbuf[slot].reshape(1024, WIDE))
            gn[rows, :] += back
            return 0

        load_copy(1 + g, slot).wait()
        lax.fori_loop(0, 4, rows_step, 0)
        rs_tick(8 + 2 * g)
        pl.when(g < 2)(lambda: load_copy(3 + g, slot).start())
        pl.when(g == 2)(lambda: load_copy(0, 0).start())
        return 0

    lax.fori_loop(0, 4, qkv_back, 0)

    def norm1_back(i, _):
        rows = rows_of(i, 128)
        x = lin[rows, :].reshape(16, 8, 1024)
        g = gn[rows, :].reshape(16, 8, 1024)
        r = lax.rsqrt(jnp.mean(x * x, axis=-1, keepdims=True) + epsilon)
        unit = x * r
        gacc[0:8, :] += jnp.sum(g * unit, axis=0)
        gu = g * gain_one[...].astype(jnp.float32)[None]
        back = r * (gu - unit * jnp.mean(gu * unit, axis=-1, keepdims=True))
        total = oacc[rows, :].reshape(16, 8, 1024) + back
        oacc[rows, :] = total.reshape(128, 1024)
        few = rows_of(i, 16)
        g_frame = jnp.sum(total, axis=1)
        shift[few, :] = g_frame
        xsend[1, few, :] = g_frame.astype(jnp.bfloat16)
        x_piece(i).start()
        return 0

    def x_piece(i):
        few = rows_of(i, 16)
        return remote(xsend.at[1, few], xrecv.at[1, few], x_ss.at[1 + i], x_rs.at[1 + i], d_x)

    lax.fori_loop(0, 8, norm1_back, 0)
    pl.when(has_prev)(lambda: halo_copy.start())
    def gain_copy(i):
        return remote(gsend.at[i], grecv.at[i], g_ss.at[i], g_rs.at[i], partners[i])

    gsend[0] = gacc[...]
    gain_copy(0).start()

    pend_copy(15).wait()
    rs_tick(15)
    load_copy(0, 0).wait()

    def out_tail_step(m, _):
        res = mm(n1[rows_of(m, 256), :], n2[:, WIDE:1024]).astype(jnp.bfloat16)
        part[0, m // 2, m % 2, :, :, :, 512:768] = res.reshape(2, 2, 64, 256)
        return 0

    lax.fori_loop(0, 4, out_tail_step, 0)

    for i in range(8):
        x_piece(i).wait_recv()
    g_low = (shift[...] + xrecv[1].astype(jnp.float32)).astype(jnp.bfloat16)
    ctx_t = ctx[...].T
    for h in range(2):
        gh = g_low[:, h * 512 : (h + 1) * 512]
        res = mm(ctx_t, gh).astype(jnp.bfloat16).reshape(2, 2, 2, 2, 32, 512)
        part[0, :, :, :, :, h * 32 : h * 32 + 32, 0:512] = res
    pend_copy(16).start()
    pend_copy(16).wait()
    w0 = wbuf[0, :, :, :, :, 0:32, 0:512].reshape(512, 512)
    w1 = wbuf[0, :, :, :, :, 32:64, 0:512].reshape(512, 512)
    dctx[...] = nt(g_low[:, :512], w0) + nt(g_low[:, 512:], w1)

    def dtok(i, _):
        rows = rows_of(i, 128)
        near = oacc[pl.ds(pl.multiple_of(i * 128, 128), 144), :]
        frame = frame_of(i)
        x = jnp.zeros((16, 8, 1024), jnp.float32)
        for j in range(3):
            keep = wait == j
            if j > 0:
                keep = jnp.logical_and(keep, same_item(frame + j, j))
            x = jnp.where(keep, near[8 * j : 128 + 8 * j].reshape(16, 8, 1024), x)
        gn[rows, :] = x.reshape(128, 1024)
        return 0

    rs_tick(16)
    dtok_copy = pltpu.make_async_copy(gn, dtok_hbm, out_sem.at[1])
    feed_out = [out_copy(pair, 2 + i) for i, pair in enumerate(feed_copies())]
    for i in range(4):
        gain_copy(i).wait_recv()
        if i < 3:
            gsend[i + 1] = gsend[i] + grecv[i]
            gain_copy(i + 1).start()
        else:
            total = gsend[i] + grecv[i]
            dgain_one[...] = total[0:8]
            dgain_two[...] = total[8:16]
        rs_tick(17 + i)
        if i == 3:
            rs_tick(21)
        if i == 0:
            unpack_feed()
            for cp in feed_out:
                cp.start()
            pl.when(has_next)(lambda: halo_copy.wait_recv())
            lax.fori_loop(0, 8, dtok, 0)
            dtok_copy.start()

    last_out = [out_copy(pair, 9 + i) for i, pair in enumerate(out_copies())]
    for cp in last_out:
        cp.start()
    pl.when(has_next)(lambda: rim_copy.wait_send())
    pl.when(has_prev)(lambda: halo_copy.wait_send())

    for i in range(4):
        gain_copy(i).wait_send()
    x_copy.wait_send()
    for i in range(8):
        x_piece(i).wait_send()

    for stage in range(4):
        for k in range(CHUNKS - (3 if stage == 1 else 2), CHUNKS):
            wait_send_all(rs_copies(stage, k))

    def drain(k, _):
        for stage in range(4):
            wait_send_all(ag_copies(stage, k))
        return 0

    lax.fori_loop(0, CHUNKS, drain, 0)
    mixed_copy.wait()
    dtok_copy.wait()
    for cp in feed_out + last_out:
        cp.wait()


def call_layer(tok, ctx, gain_one, gain_two, cot, weights, delay, lengths):
    f32, bf16 = jnp.float32, jnp.bfloat16
    vm, dma = pltpu.VMEM, pltpu.SemaphoreType.DMA
    shape = jax.ShapeDtypeStruct
    in_vmem, in_hbm, in_smem = (pl.BlockSpec(memory_space=m) for m in (pltpu.VMEM, pltpu.HBM, pltpu.SMEM))
    return pl.pallas_call(
        layer_kernel,
        name="layer",
        out_shape=(
            shape((1024, 1024), bf16),
            shape((1024, 1024), f32),
            shape((128, 512), f32),
            shape((32, 1024), f32),
            shape((8, 1024), f32),
            shape((8, 1024), f32),
            shape((64, 3072), f32),
            shape((64, 1024), f32),
            shape((64, 2816), f32),
            shape((64, 2816), f32),
            shape((176, 1024), f32),
            shape((CHUNKS, 2, 2, 2, 2, 64, WIDE), bf16),
            shape((CHUNKS, 2, 2, 2, 2, 64, WIDE), bf16),
        ),
        in_specs=[in_hbm] + [in_vmem] * 3 + [in_hbm] + [in_vmem] * 3 + [in_hbm] * 3 + [in_smem] * 2,
        out_specs=(in_hbm, in_hbm, in_vmem, in_hbm, in_vmem, in_vmem) + (in_hbm,) * 7,
        scratch_shapes=[
            vm((1024, 1024), bf16),
            vm((64, 2816), bf16),
            vm((64, 2816), bf16),
            vm((176, 1024), bf16),
            vm((CHUNKS, 64, WIDE), bf16),
            vm((1024, 1024), f32),
            vm((1024, 1024), bf16),
            vm((1024, 1024), bf16),
            vm((4, 1024, WIDE), bf16),
            vm((1024, 1024), bf16),
            vm((1024, 1024), f32),
            vm((1024, 1024), bf16),
            vm((1040, 1024), bf16),
            vm((1040, 1024), f32),
            vm((1024, 1024), f32),
            vm((2, 2, 2, 2, 2, 64, WIDE), bf16),
            vm((1024, 256), bf16),
            vm((2, 2, 2, 2, 2, 64, WIDE), bf16),
            vm((2, 2, 2, 2, 64, WIDE), bf16),
            vm((256, 1024), bf16),
            vm((128, 1024), f32),
            vm((16, 1024), f32),
            vm((4, 16, 1024), f32),
            vm((4, 16, 1024), f32),
            vm((2, 128, 1024), bf16),
            vm((2, 128, 1024), bf16),
            vm((2, 2, 2, 2, 64, WIDE), bf16),
            vm((ROUNDS, 4, 64, WIDE), bf16),
            vm((ROUNDS, 2, 64, WIDE), bf16),
            vm((ROUNDS, 64, WIDE), bf16),
            vm((3, 4, 64, WIDE), bf16),
            vm((3, 4, 64, WIDE), bf16),
            vm((2, 2, 64, WIDE), bf16),
            vm((2, 2, 64, WIDE), bf16),
            vm((2, 64, WIDE), bf16),
            vm((2, 64, WIDE), bf16),
            vm((FEED, 64, WIDE), f32),
            dma((6, CHUNKS)),
            dma((6, CHUNKS)),
            dma((6, 3)),
            dma((6, ROUNDS)),
            dma((9,)),
            dma((9,)),
            dma((4,)),
            dma((4,)),
            dma((2,)),
            dma((2, 4)),
            dma((2,)),
            dma((2,)),
            dma,
            dma((4,)),
            dma((2,)),
            dma((2,)),
            dma((14,)),
        ],
        compiler_params=pltpu.CompilerParams(
            collective_id=0, has_side_effects=True, vmem_limit_bytes=63 * 1024 * 1024
        ),
    )(tok, ctx, gain_one, gain_two, cot, *weights, delay, lengths)


def copy_kernel(*refs):
    n = (len(refs) - 2) // 3
    srcs, dsts, held, in_sem, out_sem = refs[:n], refs[n : 2 * n], refs[2 * n : 3 * n], refs[-2], refs[-1]
    ins = [pltpu.make_async_copy(srcs[i], held[i], in_sem.at[i]) for i in range(n)]
    outs = [pltpu.make_async_copy(held[i], dsts[i], out_sem.at[i]) for i in range(n)]
    for cp in ins:
        cp.start()
    for cp_in, cp_out in zip(ins, outs):
        cp_in.wait()
        cp_out.start()
    for cp in outs:
        cp.wait()


def copy_all(arrays):
    n = len(arrays)
    hbm = pl.BlockSpec(memory_space=pltpu.HBM)
    return pl.pallas_call(
        copy_kernel,
        name="outputs",
        out_shape=tuple(jax.ShapeDtypeStruct(a.shape, a.dtype) for a in arrays),
        in_specs=[hbm] * n,
        out_specs=(hbm,) * n,
        scratch_shapes=[pltpu.VMEM(a.shape, a.dtype) for a in arrays]
        + [pltpu.SemaphoreType.DMA((n,)), pltpu.SemaphoreType.DMA((n,))],
        compiler_params=pltpu.CompilerParams(vmem_limit_bytes=63 * 1024 * 1024),
    )(*arrays)


def body_kernel(
    tokens,
    context,
    ctx_weight,
    delay,
    lengths,
    attn_gain,
    ffn_gain,
    qkv_weight,
    out_weight,
    gate_weight,
    up_weight,
    down_weight,
    cotangent,
):
    frame_count, positions, width = tokens.shape[1:]
    rows = frame_count * positions
    weights = (ctx_weight, qkv_weight[0], out_weight[0], gate_weight[0], up_weight[0], down_weight[0])
    mixed_out, d_tokens, d_context, d_ctx, d_gain_one, d_gain_two, *grads = call_layer(
        tokens.reshape(rows, width),
        context,
        attn_gain[0],
        ffn_gain[0],
        cotangent.reshape(rows, width),
        weights,
        delay,
        lengths,
    )
    mixed_out, d_tokens, d_context, d_ctx, d_gain_one, d_gain_two, *grads = copy_all(
        (mixed_out, d_tokens, d_context, d_ctx, d_gain_one, d_gain_two, *grads[:-2])
    )
    d_qkv, d_out, d_gate, d_up, d_down = grads
    return (
        mixed_out.reshape(tokens.shape),
        d_tokens.reshape(tokens.shape),
        d_context,
        d_ctx,
        d_gain_one[None],
        d_gain_two[None],
        d_qkv[None],
        d_out[None],
        d_gate[None],
        d_up[None],
        d_down[None],
    )


def body(
    tokens,
    context,
    ctx_weight,
    delay,
    lengths,
    attn_gain,
    ffn_gain,
    qkv_weight,
    out_weight,
    gate_weight,
    up_weight,
    down_weight,
    cotangent,
):
    frame_count = tokens.shape[1]
    positions = tokens.shape[2]
    model_width = tokens.shape[3]
    token_rows = frame_count * positions
    head_scale = HEAD ** (-0.5)
    ctx_full = lax.all_gather(context, "stream", axis=1, tiled=True)
    ctx_rows = lax.all_gather(ctx_weight, ("stream", "frames"), axis=0, tiled=True)
    shift_term = flat_dot(ctx_full, ctx_rows)
    inputs = tokens[0]
    rim_rows = shifted(inputs[frame_count - 2 :], "frames", 1)
    extended = jnp.concatenate([rim_rows, inputs], axis=0).astype(jnp.float32)
    frame_ids = lax.axis_index("frames") * frame_count + jnp.arange(frame_count, dtype=jnp.int32)
    chosen, valid_rows = shift_tables(delay, lengths, frame_ids)
    layer_in = jnp.broadcast_to(shift_term[:, None, :], (frame_count, positions, model_width))
    for offset in range(3):
        piece = extended[2 - offset : 2 - offset + frame_count]
        layer_in = (
            layer_in + chosen[offset][None, :, None] * valid_rows[offset][:, None, None] * piece
        )
    weights = (
        lax.all_gather(qkv_weight[0], "frames", axis=0, tiled=True),
        lax.all_gather(out_weight[0], "frames", axis=0, tiled=True),
        lax.all_gather(gate_weight[0], "frames", axis=0, tiled=True),
        lax.all_gather(up_weight[0], "frames", axis=0, tiled=True),
        lax.all_gather(down_weight[0], "frames", axis=0, tiled=True),
    )
    w_qkv, w_out, w_gate, w_up, w_down = weights
    gain_one = attn_gain[0].astype(jnp.float32)
    gain_two = ffn_gain[0].astype(jnp.float32)
    normed = norm_rows(layer_in, gain_one).astype(jnp.bfloat16).reshape(token_rows, model_width)
    qkv = (
        flat_dot(normed, w_qkv).astype(jnp.bfloat16).reshape(frame_count, positions, 3, HEADS, HEAD)
    )
    queries = qkv[:, :, 0]
    key_part = qkv[:, :, 1]
    values = qkv[:, :, 2]
    scores = (
        jnp.einsum("fqhd,fkhd->fhqk", queries, key_part, preferred_element_type=jnp.float32)
        * head_scale
    )
    causal = jnp.arange(positions)[:, None] >= jnp.arange(positions)[None, :]
    scores = jnp.where(causal[None, None], scores, -1e30)
    probs = jax.nn.softmax(scores, axis=-1)
    probs_low = probs.astype(jnp.bfloat16)
    mixed = jnp.einsum("fhqk,fkhd->fqhd", probs_low, values, preferred_element_type=jnp.float32)
    mixed = mixed.astype(jnp.bfloat16).reshape(token_rows, model_width)
    after_attn = layer_in + flat_dot(mixed, w_out).reshape(frame_count, positions, model_width)
    normed_two = (
        norm_rows(after_attn, gain_two).astype(jnp.bfloat16).reshape(token_rows, model_width)
    )
    gate_pre = flat_dot(normed_two, w_gate)
    up_pre = flat_dot(normed_two, w_up)
    hidden = (jax.nn.silu(gate_pre) * up_pre).astype(jnp.bfloat16)
    out_full = after_attn + flat_dot(hidden, w_down).reshape(frame_count, positions, model_width)
    b_qkv, b_out, b_gate, b_up, b_down = weights
    grad_out = cotangent[0].astype(jnp.float32)
    grad_ff = grad_out.reshape(token_rows, model_width).astype(jnp.bfloat16)
    grad_down = trans_dot(hidden, grad_ff)
    grad_hidden = back_dot(grad_ff, b_down)
    sigmoid_gate = jax.nn.sigmoid(gate_pre)
    grad_gate = (
        grad_hidden * up_pre * sigmoid_gate * (1.0 + gate_pre * (1.0 - sigmoid_gate))
    ).astype(jnp.bfloat16)
    grad_up = (grad_hidden * gate_pre * sigmoid_gate).astype(jnp.bfloat16)
    grad_gate_w = trans_dot(normed_two, grad_gate)
    grad_up_w = trans_dot(normed_two, grad_up)
    grad_normed_two = (back_dot(grad_gate, b_gate) + back_dot(grad_up, b_up)).reshape(
        frame_count, positions, model_width
    )
    grad_after_norm, grad_gain_two = norm_back(grad_normed_two, after_attn, gain_two)
    grad_after = grad_out + grad_after_norm
    grad_branch = grad_after.reshape(token_rows, model_width).astype(jnp.bfloat16)
    grad_out_w = trans_dot(mixed, grad_branch)
    grad_mixed = (
        back_dot(grad_branch, b_out)
        .astype(jnp.bfloat16)
        .reshape(frame_count, positions, HEADS, HEAD)
    )
    grad_values = jnp.einsum(
        "fhqk,fqhd->fkhd", probs_low, grad_mixed, preferred_element_type=jnp.float32
    )
    grad_probs = jnp.einsum(
        "fqhd,fkhd->fhqk", grad_mixed, values, preferred_element_type=jnp.float32
    )
    grad_scores = (
        probs * (grad_probs - jnp.sum(grad_probs * probs, axis=-1, keepdims=True))
    ).astype(jnp.bfloat16)
    grad_queries = (
        jnp.einsum("fhqk,fkhd->fqhd", grad_scores, key_part, preferred_element_type=jnp.float32)
        * head_scale
    )
    grad_keys = (
        jnp.einsum("fhqk,fqhd->fkhd", grad_scores, queries, preferred_element_type=jnp.float32)
        * head_scale
    )
    grad_qkv = jnp.stack([grad_queries, grad_keys, grad_values], axis=2).astype(jnp.bfloat16)
    grad_qkv = grad_qkv.reshape(token_rows, 3 * model_width)
    grad_qkv_w = trans_dot(normed, grad_qkv)
    all_parts = (
        lax.psum_scatter(grad_qkv_w, "frames", scatter_dimension=0, tiled=True),
        lax.psum_scatter(grad_out_w, "frames", scatter_dimension=0, tiled=True),
        lax.psum_scatter(grad_gate_w, "frames", scatter_dimension=0, tiled=True),
        lax.psum_scatter(grad_up_w, "frames", scatter_dimension=0, tiled=True),
        lax.psum_scatter(grad_down, "frames", scatter_dimension=0, tiled=True),
    )
    d_qkv_rows, d_out_rows, d_gate_rows, d_up_rows, d_down_rows = all_parts
    grad_normed = back_dot(grad_qkv, b_qkv).reshape(frame_count, positions, model_width)
    grad_in_norm, grad_gain_one = norm_back(grad_normed, layer_in, gain_one)
    grad_in = grad_after + grad_in_norm
    gain_sums = lax.psum((grad_gain_one, grad_gain_two), "frames")
    grad_shift = jnp.sum(grad_in, axis=1).astype(jnp.bfloat16)
    grad_ctx_w = trans_dot(ctx_full, grad_shift)
    ctx_w_rows = lax.psum_scatter(grad_ctx_w, ("stream", "frames"), scatter_dimension=0, tiled=True)
    grad_context = back_dot(grad_shift, ctx_rows)
    context_half = lax.psum_scatter(
        grad_context.astype(jnp.bfloat16), "stream", scatter_dimension=1, tiled=True
    ).astype(jnp.float32)
    grad_ext = jnp.zeros((frame_count + 2, positions, model_width), jnp.float32)
    for offset in range(3):
        term = chosen[offset][None, :, None] * valid_rows[offset][:, None, None] * grad_in
        grad_ext = grad_ext + jnp.pad(term, ((2 - offset, offset), (0, 0), (0, 0)))
    back_rows = shifted(grad_ext[:2].astype(jnp.bfloat16), "frames", -1).astype(jnp.float32)
    grad_tokens = grad_ext[2:].at[frame_count - 2 :].add(back_rows)
    return (
        out_full.astype(jnp.bfloat16)[None],
        grad_tokens[None],
        context_half,
        ctx_w_rows,
        gain_sums[0][None],
        gain_sums[1][None],
        d_qkv_rows[None],
        d_out_rows[None],
        d_gate_rows[None],
        d_up_rows[None],
        d_down_rows[None],
    )


def solution(mesh):
    fits = mesh.shape["frames"] == 16 and mesh.shape["stream"] == 2
    return jax.shard_map(
        body_kernel if fits else body,
        mesh=mesh,
        in_specs=(
            P("stream", "frames", None, None),
            P("frames", "stream"),
            P(("stream", "frames"), None),
            P(),
            P(),
            P("stream", None, None),
            P("stream", None, None),
            P("stream", "frames", None),
            P("stream", "frames", None),
            P("stream", "frames", None),
            P("stream", "frames", None),
            P("stream", "frames", None),
            P("stream", "frames", None, None),
        ),
        out_specs=(
            P("stream", "frames", None, None),
            P("stream", "frames", None, None),
            P("frames", "stream"),
            P(("stream", "frames"), None),
            P("stream", None, None),
            P("stream", None, None),
            P("stream", "frames", None),
            P("stream", "frames", None),
            P("stream", "frames", None),
            P("stream", "frames", None),
            P("stream", "frames", None),
        ),
        check_vma=False,
    )
```

```python
import jax
import jax.numpy as jnp
from jax import lax
from jax.experimental import pallas as pl
from jax.experimental.pallas import tpu as pltpu
from jax.sharding import PartitionSpec as P

HEADS = 16
HEAD = 64


epsilon = 1e-05


def shifted(x, axis, by):
    length = lax.axis_size(axis)
    pairs = [(i, i + by) for i in range(length) if 0 <= i + by < length]
    return lax.ppermute(x, axis, pairs)


def flat_dot(left, right):
    return jnp.dot(left, right, preferred_element_type=jnp.float32)


def trans_dot(left, right):
    return lax.dot_general(
        left, right, (((0,), (0,)), ((), ())), preferred_element_type=jnp.float32
    )


def back_dot(left, right):
    return lax.dot_general(
        left, right, (((1,), (1,)), ((), ())), preferred_element_type=jnp.float32
    )


def norm_rows(rows, gain):
    return rows * lax.rsqrt(jnp.mean(rows * rows, axis=-1, keepdims=True) + epsilon) * gain


def norm_back(grad_normed, rows, gain):
    scale = lax.rsqrt(jnp.mean(rows * rows, axis=-1, keepdims=True) + epsilon)
    unit = rows * scale
    grad_gain = jnp.sum(grad_normed * unit, axis=0)
    grad_unit = grad_normed * gain
    grad_rows = scale * (grad_unit - unit * jnp.mean(grad_unit * unit, axis=-1, keepdims=True))
    return (grad_rows, grad_gain)


def shift_tables(delay, lengths, frame_ids):
    starts = jnp.cumsum(lengths) - lengths
    at_start = jnp.any(frame_ids[:, None] == starts[None, :], axis=1)
    after_start = jnp.any(frame_ids[:, None] - 1 == starts[None, :], axis=1)
    keep_one = jnp.logical_not(at_start)
    keep_two = jnp.logical_and(keep_one, jnp.logical_not(after_start))
    valid_rows = jnp.stack([jnp.ones_like(keep_one), keep_one, keep_two]).astype(jnp.float32)
    chosen = (delay[None, :] == jnp.arange(3, dtype=jnp.int32)[:, None]).astype(jnp.float32)
    return (chosen, valid_rows)


MESH = pl.DeviceIdType.MESH
CHUNKS = 17
FEED = 11
WIDE = 768
ROUNDS = 5
FAR_ROUNDS = 7
MOST = 48
SPLIT = ((0, MOST), (MOST, 64))


def mm(a, b):
    return jnp.dot(a, b, preferred_element_type=jnp.float32)


def nt(a, b):
    return lax.dot_general(a, b, (((1,), (1,)), ((), ())), preferred_element_type=jnp.float32)


def tn(a, b):
    return lax.dot_general(a, b, (((0,), (0,)), ((), ())), preferred_element_type=jnp.float32)


def either(cond, fn):
    if isinstance(cond, bool):
        if cond:
            fn()
    else:
        pl.when(cond)(fn)


def within(t, low, high):
    if isinstance(t, int):
        return low <= t < high
    return jnp.logical_and(t >= low, t < high)


def layer_kernel(
    tok_hbm,
    ctx,
    gain_one,
    gain_two,
    cot_hbm,
    ctx_own,
    qkv_own,
    out_own,
    gate_hbm,
    up_hbm,
    down_hbm,
    delay,
    lengths,
    mixed_hbm,
    dtok_hbm,
    dctx,
    dctxw_hbm,
    dgain_one,
    dgain_two,
    dqkv_hbm,
    dout_hbm,
    dgate_hbm,
    dup_hbm,
    ddown_hbm,
    gathered,
    pend,
    cot,
    gate_own,
    up_own,
    down_own,
    w_own,
    lin,
    n1,
    n1t,
    qkv,
    mixed,
    aft,
    n2,
    n2t,
    oacc,
    gn,
    wbuf,
    wtail,
    part,
    part_own,
    hidt,
    shift,
    gacc,
    gsend,
    grecv,
    xsend,
    xrecv,
    r_c,
    r_y,
    r_zl,
    r_zh,
    t_keep,
    t_send,
    u_keep,
    u_send,
    v_keep,
    v_send,
    fin,
    ag_ss,
    ag_rs,
    rs_ss,
    rs_rs,
    x_ss,
    x_rs,
    g_ss,
    g_rs,
    own_sem,
    load_sem,
    pend_sem,
    half_sem,
    tok_sem,
    in_sem,
    rim_ss,
    rim_rs,
    out_sem,
):
    s = lax.axis_index("stream")
    f = lax.axis_index("frames")
    c = f % 2
    y = (f // 2) % 2
    zl = (f // 4) % 2
    zh = f // 8
    d_c = (s, f + 1 - 2 * c)
    d_y = (s, f + 2 - 4 * y)
    d_zl = (s, f + 4 - 8 * zl)
    d_zh = (s, f + 8 - 16 * zh)
    d_x = (1 - s, f)
    partners = (d_zh, d_zl, d_y, d_c)

    frames = lax.axis_size("frames")
    has_next, has_prev = f < frames - 1, f > 0
    d_next, d_prev = (s, f + 1), (s, f - 1)

    tokext = n2t
    tok_copy = pltpu.make_async_copy(tok_hbm, tokext.at[16:1040], tok_sem)
    fetches = [
        pltpu.make_async_copy(src, dst, in_sem.at[i])
        for i, (src, dst) in enumerate(
            ((down_hbm, down_own), (gate_hbm, gate_own), (up_hbm, up_own), (cot_hbm, cot))
        )
    ]
    for cp in fetches:
        cp.start()
    tok_copy.start()

    barrier = pltpu.get_barrier_semaphore()

    def greet(device):
        pl.semaphore_signal(barrier, inc=1, device_id=device, device_id_type=MESH)

    for device in partners + (d_x,):
        greet(device)
    pl.when(has_next)(lambda: greet(d_next))
    pl.when(has_prev)(lambda: greet(d_prev))

    w_own[0, 0:32, 0:512] = ctx_own[:, 0:512]
    w_own[0, 32:64, 0:512] = ctx_own[:, 512:1024]
    w_own[0, :, 512:768] = out_own[:, 768:1024]
    w_own[5] = out_own[:, 0:768]
    for g in range(4):
        for part_id in range(3):
            at = part_id * 1024 + g * 256
            w_own[1 + g, :, part_id * 256 : part_id * 256 + 256] = qkv_own[:, at : at + 256]

    def own_copy(low, high, i):
        return pltpu.make_async_copy(
            w_own.at[low:high], gathered.at[low:high, zh, zl, y, c], own_sem.at[i]
        )

    own_copy(0, 6, 0).start()

    pl.semaphore_wait(barrier, 5 + has_next.astype(jnp.int32) + has_prev.astype(jnp.int32))

    def remote(src, dst, ss, rs, device):
        return pltpu.make_async_remote_copy(
            src_ref=src, dst_ref=dst, send_sem=ss, recv_sem=rs, device_id=device, device_id_type=MESH
        )

    def ag_copies(stage, k):
        if stage == 0:
            triples = [(w_own.at[k], gathered.at[k, zh, zl, y, c], d_zh)]
        elif stage == 1:
            near, side = gathered.at[k, :, zl, y, c, 0:MOST], gathered.at[k, :, zl, y, c, MOST:64]
            triples = [(near, near, d_zl), (side, side, d_y)]
        elif stage == 2:
            side, near = gathered.at[k, :, :, y, c, 0:MOST], gathered.at[k, :, zl, :, c, MOST:64]
            triples = [(side, side, d_y), (near, near, d_zl)]
        else:
            own = gathered.at[k, :, :, :, c]
            triples = [(own, own, d_c)]
        first = (0, 1, 3, 5)[stage]
        return [
            remote(src, dst, ag_ss.at[first + i, k], ag_rs.at[first + i, k], device)
            for i, (src, dst, device) in enumerate(triples)
        ]

    def start_all(copies):
        for cp in copies:
            cp.start()

    def wait_recv_all(copies):
        for cp in copies:
            cp.wait_recv()

    def wait_send_all(copies):
        for cp in copies:
            cp.wait_send()

    class load_copy:
        def __init__(self, k, slot):
            self.parts = [
                pltpu.make_async_copy(
                    gathered.at[k, i // 2, i % 2], wbuf.at[slot, i // 2, i % 2], load_sem.at[slot, i]
                )
                for i in range(4)
            ]

        def start(self):
            for cp in self.parts:
                cp.start()

        def wait(self):
            for cp in self.parts:
                cp.wait()

    def ag_step(stage, k):
        def go():
            if stage > 0:
                wait_recv_all(ag_copies(stage - 1, k))
            start_all(ag_copies(stage, k))
        either(within(k, 0, CHUNKS), go)

    def ag_tick(t, gap=1):
        for stage in range(3):
            ag_step(stage, t - gap * stage)

    def ag_ready(k):
        def ready():
            wait_recv_all(ag_copies(3, k))
            load_copy(k, k % 2).start()
        either(within(k, 0, CHUNKS), ready)

    def rs_copies(stage, r):
        two, slot = r % (2 if stage == 0 else 3), r % (FAR_ROUNDS if stage == 3 else ROUNDS)
        if stage == 0:
            triples = [(pend.at[r, :, :, :, 1 - c], r_c.at[two], d_c)]
        elif stage == 3:
            triples = [(v_send.at[two], r_zh.at[slot], d_zh)]
        else:
            src, dst = ((t_send, r_y), (u_send, r_zl))[stage - 1]
            devices = ((d_y, d_zl), (d_zl, d_y))[stage - 1]
            triples = [
                (src.at[two, :, low:high], dst.at[slot, :, low:high], device)
                for (low, high), device in zip(SPLIT, devices)
            ]
        first = (0, 1, 3, 5)[stage]
        return [
            remote(src, dst, rs_ss.at[first + i, two], rs_rs.at[first + i, slot], device)
            for i, (src, dst, device) in enumerate(triples)
        ]

    def add(a, b):
        return a.astype(jnp.float32) + b.astype(jnp.float32)

    def place_result(k, res):
        if not isinstance(k, int):
            @pl.when(k < FEED)
            def _():
                fin[k] = res
            pl.when(k == FEED)(lambda: place_result(FEED, res))
            return
        if k < FEED:
            fin[k] = res
        elif k == FEED:
            aft[384:448, 0:768] = res
        elif k < CHUNKS - 1:
            g = k - FEED - 1
            for p in range(3):
                aft[192 + 64 * p : 256 + 64 * p, g * 256 : g * 256 + 256] = res[:, p * 256 : p * 256 + 256]
        else:
            aft[384:448, 768:1024] = res[:, 512:768]
            aft[448:480, 0:512] = res[0:32, 0:512]
            aft[448:480, 512:1024] = res[32:64, 0:512]

    def out_copies():
        pairs = [(aft.at[384:448], dout_hbm), (aft.at[448:480], dctxw_hbm)]
        for p in range(3):
            pairs.append((aft.at[192 + 64 * p : 256 + 64 * p], dqkv_hbm.at[:, p * 1024 : p * 1024 + 1024]))
        return pairs

    def feed_copies():
        pairs = [(aft.at[512:688], ddown_hbm)]
        for i, hbm in enumerate((dgate_hbm, dup_hbm)):
            at = i * 768
            if i == 1:
                at = 704
            for p in range(3):
                n = 1024 if p < 2 else 768
                pairs.append((aft.at[at + 64 * p : at + 64 * p + 64, 0:n], hbm.at[:, p * 1024 : p * 1024 + n]))
        return pairs

    def out_copy(pair, i):
        return pltpu.make_async_copy(pair[0], pair[1], out_sem.at[i])

    def unpack_feed():
        for j in range(FEED):
            for q in range(4):
                aft[512 + j * 16 : 528 + j * 16, q * 256 : q * 256 + 256] = fin[j, q * 16 : q * 16 + 16, 512:768]
        for i, at in enumerate((0, 704)):
            cols = [
                fin[j, :, i * 256 + d * 16 : i * 256 + d * 16 + 16] for d in range(16) for j in range(FEED)
            ]
            for p in range(22):
                piece = jnp.concatenate(cols[p * 8 : p * 8 + 8], axis=1)
                row, col = at + 64 * (p // 8), (p % 8) * 128
                aft[row : row + 64, col : col + 128] = piece

    def pend_copy(r):
        return pltpu.make_async_copy(part.at[r % 2], pend.at[r], pend_sem.at[r % 2])

    def half_copy(r):
        return pltpu.make_async_copy(pend.at[r, :, :, :, c], part_own.at[r % 2], half_sem.at[r % 2])

    def part_done(r):
        either(within(r, 1, CHUNKS), lambda: pend_copy(r - 1).wait())
        pend_copy(r).start()

    def send_half(r):
        either(within(r, 2, CHUNKS), lambda: wait_send_all(rs_copies(0, r - 2)))
        start_all(rs_copies(0, r))
        half_copy(r).start()

    def rs_tick(r):
        def stage_y():
            k = r - 1
            wait_recv_all(rs_copies(0, k))
            half_copy(k).wait()
            either(within(k, 3, CHUNKS), lambda: wait_send_all(rs_copies(1, k - 3)))
            two, three = k % 2, k % 3

            def piece(i, _):
                a, b = i // 2, i % 2
                for (low, high), send, keep in zip(
                    SPLIT, ((b, 1 - y), (1 - zl, b)), ((b, y), (zl, b))
                ):
                    for out, (m, n) in ((t_send, send), (t_keep, keep)):
                        out[three, i, low:high] = part_own[two, a, m, n, low:high] + r_c[two, a, m, n, low:high]
                return 0

            lax.fori_loop(0, 4, piece, 0)
            start_all(rs_copies(1, k))
        either(within(r, 1, CHUNKS + 1), stage_y)
        either(within(r, 0, CHUNKS), lambda: send_half(r))

        def stage_zl():
            k = r - 3
            wait_recv_all(rs_copies(1, k))
            either(within(k, 3, CHUNKS), lambda: wait_send_all(rs_copies(2, k - 3)))
            three, slot = k % 3, k % ROUNDS
            for a in range(2):
                for (low, high), mine in zip(SPLIT, (zl, y)):
                    for out, at in ((u_send, a * 2 + 1 - mine), (u_keep, a * 2 + mine)):
                        out[three, a, low:high] = t_keep[three, at, low:high] + r_y[slot, at, low:high]
            start_all(rs_copies(2, k))
        either(within(r, 3, CHUNKS + 3), stage_zl)

        def stage_zh():
            k = r - 5
            wait_recv_all(rs_copies(2, k))
            either(within(k, 3, CHUNKS), lambda: wait_send_all(rs_copies(3, k - 3)))
            three, slot = k % 3, k % ROUNDS
            v_send[three] = u_keep[three, 1 - zh] + r_zl[slot, 1 - zh]
            v_keep[three] = u_keep[three, zh] + r_zl[slot, zh]
            start_all(rs_copies(3, k))
        either(within(r, 5, CHUNKS + 5), stage_zh)

        def last():
            k = r - 7
            wait_recv_all(rs_copies(3, k))
            place_result(k, add(v_keep[k % 3], r_zh[k % FAR_ROUNDS]))
        either(within(r, 7, CHUNKS + 7), last)

    rim_copy = remote(tok_hbm.at[1008:1024], tokext.at[0:16], rim_ss.at[0], rim_rs.at[0], d_next)
    halo_copy = remote(oacc.at[0:16], oacc.at[1024:1040], rim_ss.at[1], rim_rs.at[1], d_prev)
    pl.when(has_next)(lambda: rim_copy.start())

    @pl.when(jnp.logical_not(has_prev))
    def _():
        tokext[0:16, :] = jnp.zeros((16, 1024), jnp.bfloat16)

    @pl.when(jnp.logical_not(has_next))
    def _():
        oacc[1024:1040, :] = jnp.zeros((16, 1024), jnp.float32)

    gacc[...] = jnp.zeros_like(gacc)

    place = lax.broadcasted_iota(jnp.int32, (16, 8, 1), 1)
    wait = jnp.zeros((16, 8, 1), jnp.int32)
    for p in range(8):
        wait = jnp.where(place == p, delay[p], wait)

    def starts_at(frame):
        start = jnp.int32(0)
        hit = frame == start
        for i in range(lengths.shape[0] - 1):
            start = start + lengths[i]
            hit = jnp.logical_or(hit, frame == start)
        return hit

    def same_item(frame, j):
        ok = jnp.logical_not(starts_at(frame))
        if j == 2:
            ok = jnp.logical_and(ok, jnp.logical_not(starts_at(frame - 1)))
        return ok

    def frame_of(i):
        return f * 128 + i * 16 + lax.broadcasted_iota(jnp.int32, (16, 8, 1), 0)

    def pack_feed(own, at):
        for j in range(FEED):
            cols = [own[:, d * 176 + j * 16 : d * 176 + j * 16 + 16] for d in range(16)]
            w_own[6 + j, :, at : at + 256] = jnp.concatenate(cols, axis=1)

    ag_tick(0)
    own_copy(0, 6, 0).wait()
    ag_tick(1)
    for cp in fetches[:2]:
        cp.wait()
    for j in range(FEED):
        for q in range(4):
            w_own[6 + j, q * 16 : q * 16 + 16, 512:768] = down_own[
                j * 16 : j * 16 + 16, q * 256 : q * 256 + 256
            ]
    pack_feed(gate_own, 0)
    ag_tick(2)
    fetches[2].wait()
    pack_feed(up_own, 256)
    own_copy(6, CHUNKS, 1).start()
    ag_tick(3)
    ag_step(3, 0)
    ag_ready(0)
    own_copy(6, CHUNKS, 1).wait()
    ag_tick(4)

    load_copy(0, 0).wait()
    wtail[...] = wbuf[0, :, :, :, :, :, 512:768].reshape(1024, 256)
    half = shift.shape[1] // 2
    for h in range(2):
        w_half = wbuf[0, :, :, :, :, h * 32 : h * 32 + 32, 0:512].reshape(512, 512)
        shift[:, h * half : (h + 1) * half] = mm(ctx[...], w_half)
    xsend[0] = shift[...].astype(jnp.bfloat16)

    x_copy = remote(xsend.at[0], xrecv.at[0], x_ss.at[0], x_rs.at[0], d_x)
    x_copy.start()
    ag_tick(5)
    ag_step(3, 1)
    ag_ready(1)
    ag_tick(6)
    ag_step(0, 7)
    ag_step(0, 8)
    ag_step(1, 6)
    x_copy.wait_recv()
    shift[...] = shift[...] + xrecv[0].astype(jnp.float32)

    def rows_of(i, size):
        return pl.ds(pl.multiple_of(i * size, size), size)

    def norm1(i, _):
        rows = rows_of(i, 128)
        sh = shift[rows_of(i, 16), :]
        near = tokext[pl.ds(pl.multiple_of(i * 128, 128), 144), :].astype(jnp.float32)
        frame = frame_of(i)
        x = jnp.zeros((16, 8, 1024), jnp.float32)
        for j in range(3):
            keep = wait == j
            if j > 0:
                keep = jnp.logical_and(keep, same_item(frame, j))
            piece = near[16 - 8 * j : 144 - 8 * j].reshape(16, 8, 1024)
            x = jnp.where(keep, piece, x)
        x = x + sh[:, None, :]
        r = lax.rsqrt(jnp.mean(x * x, axis=-1, keepdims=True) + epsilon)
        n = (x * r * gain_one[...].astype(jnp.float32)[None]).reshape(128, 1024).astype(jnp.bfloat16)
        lin[rows, :] = x.reshape(128, 1024)
        n1[rows, :] = n
        n1t[:, rows] = n.T
        return 0

    tok_copy.wait()
    pl.when(has_prev)(lambda: rim_copy.wait_recv())
    lax.fori_loop(0, 8, norm1, 0)

    lane_low = lax.broadcasted_iota(jnp.int32, (128, 128), 1) < 64
    head_scale = HEAD ** (-0.5)

    def both(v):
        zero = jnp.zeros_like(v)
        return jnp.concatenate([jnp.where(lane_low, v, zero), jnp.where(lane_low, zero, v)], axis=0)

    own_frame = [
        lax.broadcasted_iota(jnp.int32, (8, 128), 1) // 8 == fr for fr in range(16)
    ]
    key_seen = lax.broadcasted_iota(jnp.int32, (8, 128), 0) <= lax.broadcasted_iota(jnp.int32, (8, 128), 1) % 8

    def compact(full, h):
        out = full[h * 128 : h * 128 + 8]
        for fr in range(1, 16):
            at = h * 128 + fr * 8
            out = jnp.where(own_frame[fr], full[at : at + 8], out)
        return out

    def spread(pair):
        zero = jnp.zeros((8, 128), jnp.float32)
        rows = [jnp.where(own_frame[fr], x, zero) for x in pair for fr in range(16)]
        return jnp.concatenate(rows, axis=0).astype(jnp.bfloat16)

    def probabilities(q, kk):
        full = nt(kk, q)
        pair = []
        for h in range(2):
            sc = jnp.where(key_seen, compact(full, h) * head_scale, -1e30)
            e = jnp.exp(sc - jnp.max(sc, axis=0, keepdims=True))
            pair.append(e / jnp.sum(e, axis=0, keepdims=True))
        return pair

    def pair_of(g, sub, lo):
        return [qkv[g, sub, at + lo : at + lo + 128] for at in (0, 256, 512)]

    def attn_fwd(g):
        def rows_step(i, _):
            for u in range(4):
                sub = rows_of(i * 4 + u, 128)
                for lo in (0, 128):
                    q, k, v = pair_of(g, sub, lo)
                    pr = spread(probabilities(q, both(k)))
                    out = tn(pr, both(v)).astype(jnp.bfloat16)
                    mixed[sub, pl.ds(pl.multiple_of(g * 256 + lo, 128), 128)] = out
            return 0
        lax.fori_loop(0, 2, rows_step, 0)

    def attn_bwd(g):
        def rows_step(i, _):
            for u in range(4):
                sub = rows_of(i * 4 + u, 128)
                for lo in (0, 128):
                    q, k, v = pair_of(g, sub, lo)
                    do = mixed[sub, pl.ds(pl.multiple_of(g * 256 + lo, 128), 128)]
                    kk = both(k)
                    pr = probabilities(q, kk)
                    full = nt(both(v), do)
                    ds = []
                    for h in range(2):
                        d = compact(full, h)
                        ds.append(pr[h] * (d - jnp.sum(d * pr[h], axis=0, keepdims=True)))
                    ds = spread(ds)
                    dq = tn(ds, kk) * head_scale
                    dk = mm(ds, q)
                    dv = mm(spread(pr), do)
                    qkv[g, sub, lo : lo + 128] = dq.astype(jnp.bfloat16)
                    qkv[g, sub, 256 + lo : 384 + lo] = (
                        jnp.where(lane_low, dk[:128], dk[128:]) * head_scale
                    ).astype(jnp.bfloat16)
                    qkv[g, sub, 512 + lo : 640 + lo] = jnp.where(lane_low, dv[:128], dv[128:]).astype(jnp.bfloat16)
            return 0
        lax.fori_loop(0, 2, rows_step, 0)

    def qkv_group(g, _):
        slot = (1 + g) % 2
        load_copy(1 + g, slot).wait()

        def rows_step(i, _):
            rows = rows_of(i, 256)
            qkv[g, rows, :] = mm(n1[rows, :], wbuf[slot].reshape(1024, WIDE)).astype(jnp.bfloat16)
            return 0

        lax.fori_loop(0, 4, rows_step, 0)
        ag_step(3, 2 + g)
        ag_tick(9 + g, 2)
        attn_fwd(g)
        ag_ready(2 + g)
        return 0

    lax.fori_loop(0, 4, qkv_group, 0)

    load_copy(5, 1).wait()

    def after(i, _):
        rows = rows_of(i, 256)
        m = mixed[rows, :]
        a = lin[rows, 0:WIDE] + mm(m, wbuf[1].reshape(1024, WIDE))
        b = lin[rows, WIDE:1024] + mm(m, wtail[...])
        x = jnp.concatenate([a, b], axis=1)
        aft[rows, :] = x
        oacc[rows, :] = x
        gn[rows, :] = jnp.zeros((256, 1024), jnp.float32)
        x3 = x.reshape(32, 8, 1024)
        r = lax.rsqrt(jnp.mean(x3 * x3, axis=-1, keepdims=True) + epsilon)
        n = (x3 * r * gain_two[...].astype(jnp.float32)[None]).reshape(256, 1024).astype(jnp.bfloat16)
        n2[rows, :] = n
        n2t[0:1024, rows] = n.T
        return 0

    lax.fori_loop(0, 2, after, 0)
    ag_step(3, 6)
    ag_tick(13, 2)
    lax.fori_loop(2, 4, after, 0)
    ag_ready(6)
    fetches[3].wait()

    def feed(j, _):
        slot = j % 2
        load_copy(6 + j, slot).wait()
        two = j % 2

        def rows_step(i):
            rows = slice(i * 512, i * 512 + 512)
            w_gu = wbuf[slot, :, :, :, :, :, 0:512].reshape(1024, 512)
            pre = mm(n2[rows, :], w_gu)
            gate, up = pre[:, :256], pre[:, 256:]
            g_hid = jnp.zeros((512, 256), jnp.float32)
            for q in range(4):
                w_q = wbuf[slot, :, :, :, :, q * 16 : q * 16 + 16, 512:768].reshape(256, 256)
                g_hid = g_hid + nt(cot[rows, q * 256 : q * 256 + 256], w_q)
            sig = jax.nn.sigmoid(gate)
            silu = gate * sig
            hid = (silu * up).astype(jnp.bfloat16)
            g_gate = (g_hid * up * sig * (1.0 + gate * (1.0 - sig))).astype(jnp.bfloat16)
            g_up = (g_hid * silu).astype(jnp.bfloat16)
            for q in range(4):
                w_q = wbuf[slot, :, :, :, :, q * 16 : q * 16 + 16, 512:768].reshape(256, 256)
                oacc[rows, q * 256 : q * 256 + 256] += mm(hid, w_q)
            both_g = jnp.concatenate([g_gate, g_up], axis=1)
            n1[rows, 0:512] = both_g
            hidt[:, rows] = hid.T
            back = nt(both_g, w_gu)
            gn[rows, :] += back

        for i in range(2):
            rows_step(i)
        ag_step(3, 7 + j)
        ag_tick(14 + j, 2)

        def weight_step(m, _):
            res = mm(n2t[rows_of(m, 512), :], n1[:, 0:512]).astype(jnp.bfloat16).reshape(2, 2, 2, 64, 512)
            part[two, m, :, :, :, :, 0:512] = res
            return 0

        lax.fori_loop(0, 2, weight_step, 0)
        ag_ready(7 + j)
        for q in range(4):
            res = mm(hidt[...], cot[:, q * 256 : q * 256 + 256]).astype(jnp.bfloat16)
            part[two, :, :, :, :, q * 16 : q * 16 + 16, 512:768] = res.reshape(2, 2, 2, 2, 16, 256)
        part_done(j)
        pl.when(jnp.logical_or(j % 2 == 1, j == FEED - 1))(lambda: rs_tick(j // 2))
        return 0

    lax.fori_loop(0, FEED, feed, 0)
    load_copy(5, 1).start()
    load_copy(1, 0).start()

    def norm2_back(i, _):
        rows = rows_of(i, 128)
        n2t[rows, :] = oacc[rows, :].astype(jnp.bfloat16)
        n1[:, rows] = mixed[rows, :].T
        x = aft[rows, :].reshape(16, 8, 1024)
        g = gn[rows, :].reshape(16, 8, 1024)
        gn[rows, :] = jnp.zeros((128, 1024), jnp.float32)
        r = lax.rsqrt(jnp.mean(x * x, axis=-1, keepdims=True) + epsilon)
        unit = x * r
        gacc[8:16, :] += jnp.sum(g * unit, axis=0)
        gu = g * gain_two[...].astype(jnp.float32)[None]
        back = r * (gu - unit * jnp.mean(gu * unit, axis=-1, keepdims=True))
        total = cot[rows, :].astype(jnp.float32) + back.reshape(128, 1024)
        oacc[rows, :] = total
        n2[rows, :] = total.astype(jnp.bfloat16)
        return 0

    lax.fori_loop(0, 8, norm2_back, 0)
    mixed_copy = pltpu.make_async_copy(n2t.at[0:1024], mixed_hbm, out_sem.at[0])
    mixed_copy.start()
    rs_tick(6)


    def out_weight_step(m, _):
        res = mm(n1[rows_of(m, 256), :], n2[:, 0:WIDE]).astype(jnp.bfloat16)
        part[1, m // 2, m % 2] = res.reshape(2, 2, 64, WIDE)
        return 0

    lax.fori_loop(0, 4, out_weight_step, 0)
    part_done(11)

    def mixed_back(i, _):
        rows = rows_of(i, 256)
        g = n2[rows, :]
        res = nt(g[:, 0:WIDE], wbuf[1].reshape(1024, WIDE)) + nt(g[:, WIDE:1024], wtail[...])
        mixed[rows, :] = res.astype(jnp.bfloat16)
        return 0

    load_copy(5, 1).wait()
    lax.fori_loop(0, 4, mixed_back, 0)
    load_copy(2, 1).start()
    rs_tick(7)

    def qkv_back(g, _):
        slot = g % 2
        attn_bwd(g)
        pend_copy(11 + g).wait()
        rs_tick(8 + 2 * g)
        two = g % 2

        def weight_step(m, _):
            res = mm(n1t[rows_of(m, 256), :], qkv[g]).astype(jnp.bfloat16)
            part[two, m // 2, m % 2] = res.reshape(2, 2, 64, WIDE)
            return 0

        lax.fori_loop(0, 4, weight_step, 0)
        pend_copy(12 + g).start()

        def rows_step(i, _):
            rows = rows_of(i, 256)
            back = nt(qkv[g, rows, :], wbuf[slot].reshape(1024, WIDE))
            gn[rows, :] += back
            return 0

        load_copy(1 + g, slot).wait()
        lax.fori_loop(0, 4, rows_step, 0)
        pl.when(g < 3)(lambda: rs_tick(9 + 2 * g))
        pl.when(g < 2)(lambda: load_copy(3 + g, slot).start())
        pl.when(g == 2)(lambda: load_copy(0, 0).start())
        return 0

    lax.fori_loop(0, 4, qkv_back, 0)

    def norm1_back(i, _):
        rows = rows_of(i, 128)
        x = lin[rows, :].reshape(16, 8, 1024)
        g = gn[rows, :].reshape(16, 8, 1024)
        r = lax.rsqrt(jnp.mean(x * x, axis=-1, keepdims=True) + epsilon)
        unit = x * r
        gacc[0:8, :] += jnp.sum(g * unit, axis=0)
        gu = g * gain_one[...].astype(jnp.float32)[None]
        back = r * (gu - unit * jnp.mean(gu * unit, axis=-1, keepdims=True))
        total = oacc[rows, :].reshape(16, 8, 1024) + back
        oacc[rows, :] = total.reshape(128, 1024)
        few = rows_of(i, 16)
        g_frame = jnp.sum(total, axis=1)
        shift[few, :] = g_frame
        xsend[1, few, :] = g_frame.astype(jnp.bfloat16)
        x_piece(i).start()
        return 0

    def x_piece(i):
        few = rows_of(i, 16)
        return remote(xsend.at[1, few], xrecv.at[1, few], x_ss.at[1 + i], x_rs.at[1 + i], d_x)

    lax.fori_loop(0, 8, norm1_back, 0)
    pl.when(has_prev)(lambda: halo_copy.start())
    def gain_copy(i):
        return remote(gsend.at[i], grecv.at[i], g_ss.at[i], g_rs.at[i], partners[i])

    gsend[0] = gacc[...]
    gain_copy(0).start()

    pend_copy(15).wait()
    rs_tick(15)
    load_copy(0, 0).wait()

    def out_tail_step(m, _):
        res = mm(n1[rows_of(m, 256), :], n2[:, WIDE:1024]).astype(jnp.bfloat16)
        part[0, m // 2, m % 2, :, :, :, 512:768] = res.reshape(2, 2, 64, 256)
        return 0

    lax.fori_loop(0, 4, out_tail_step, 0)

    for i in range(8):
        x_piece(i).wait_recv()
    g_low = (shift[...] + xrecv[1].astype(jnp.float32)).astype(jnp.bfloat16)
    ctx_t = ctx[...].T
    for h in range(2):
        gh = g_low[:, h * 512 : (h + 1) * 512]
        res = mm(ctx_t, gh).astype(jnp.bfloat16).reshape(2, 2, 2, 2, 32, 512)
        part[0, :, :, :, :, h * 32 : h * 32 + 32, 0:512] = res
    pend_copy(16).start()
    pend_copy(16).wait()
    w0 = wbuf[0, :, :, :, :, 0:32, 0:512].reshape(512, 512)
    w1 = wbuf[0, :, :, :, :, 32:64, 0:512].reshape(512, 512)
    dctx[...] = nt(g_low[:, :512], w0) + nt(g_low[:, 512:], w1)

    def dtok(i, _):
        rows = rows_of(i, 128)
        near = oacc[pl.ds(pl.multiple_of(i * 128, 128), 144), :]
        frame = frame_of(i)
        x = jnp.zeros((16, 8, 1024), jnp.float32)
        for j in range(3):
            keep = wait == j
            if j > 0:
                keep = jnp.logical_and(keep, same_item(frame + j, j))
            x = jnp.where(keep, near[8 * j : 128 + 8 * j].reshape(16, 8, 1024), x)
        gn[rows, :] = x.reshape(128, 1024)
        return 0

    rs_tick(16)
    dtok_copy = pltpu.make_async_copy(gn, dtok_hbm, out_sem.at[1])
    last_out = [out_copy(pair, 9 + i) for i, pair in enumerate(out_copies())]
    feed_out = [out_copy(pair, 2 + i) for i, pair in enumerate(feed_copies())]
    for i in range(4):
        gain_copy(i).wait_recv()
        if i < 3:
            gsend[i + 1] = gsend[i] + grecv[i]
            gain_copy(i + 1).start()
        else:
            total = gsend[i] + grecv[i]
            dgain_one[...] = total[0:8]
            dgain_two[...] = total[8:16]
        rs_tick(17 + i)
        if i == 0:
            unpack_feed()
            for cp in feed_out:
                cp.start()
            pl.when(has_next)(lambda: halo_copy.wait_recv())
            lax.fori_loop(0, 8, dtok, 0)
            dtok_copy.start()

    rs_tick(21)
    rs_tick(22)
    for cp in last_out[2:]:
        cp.start()
    rs_tick(23)

    for cp in last_out[:2]:
        cp.start()
    pl.when(has_next)(lambda: rim_copy.wait_send())
    pl.when(has_prev)(lambda: halo_copy.wait_send())

    for i in range(4):
        gain_copy(i).wait_send()
    x_copy.wait_send()
    for i in range(8):
        x_piece(i).wait_send()

    for stage in range(4):
        for k in range(CHUNKS - (2 if stage == 0 else 3), CHUNKS):
            wait_send_all(rs_copies(stage, k))

    def drain(k, _):
        for stage in range(4):
            wait_send_all(ag_copies(stage, k))
        return 0

    lax.fori_loop(0, CHUNKS, drain, 0)
    mixed_copy.wait()
    dtok_copy.wait()
    for cp in feed_out + last_out:
        cp.wait()


def call_layer(tok, ctx, gain_one, gain_two, cot, weights, delay, lengths):
    f32, bf16 = jnp.float32, jnp.bfloat16
    vm, dma = pltpu.VMEM, pltpu.SemaphoreType.DMA
    shape = jax.ShapeDtypeStruct
    in_vmem, in_hbm, in_smem = (pl.BlockSpec(memory_space=m) for m in (pltpu.VMEM, pltpu.HBM, pltpu.SMEM))
    return pl.pallas_call(
        layer_kernel,
        name="layer",
        out_shape=(
            shape((1024, 1024), bf16),
            shape((1024, 1024), f32),
            shape((128, 512), f32),
            shape((32, 1024), f32),
            shape((8, 1024), f32),
            shape((8, 1024), f32),
            shape((64, 3072), f32),
            shape((64, 1024), f32),
            shape((64, 2816), f32),
            shape((64, 2816), f32),
            shape((176, 1024), f32),
            shape((CHUNKS, 2, 2, 2, 2, 64, WIDE), bf16),
            shape((CHUNKS, 2, 2, 2, 2, 64, WIDE), bf16),
        ),
        in_specs=[in_hbm] + [in_vmem] * 3 + [in_hbm] + [in_vmem] * 3 + [in_hbm] * 3 + [in_smem] * 2,
        out_specs=(in_hbm, in_hbm, in_vmem, in_hbm, in_vmem, in_vmem) + (in_hbm,) * 7,
        scratch_shapes=[
            vm((1024, 1024), bf16),
            vm((64, 2816), bf16),
            vm((64, 2816), bf16),
            vm((176, 1024), bf16),
            vm((CHUNKS, 64, WIDE), bf16),
            vm((1024, 1024), f32),
            vm((1024, 1024), bf16),
            vm((1024, 1024), bf16),
            vm((4, 1024, WIDE), bf16),
            vm((1024, 1024), bf16),
            vm((1024, 1024), f32),
            vm((1024, 1024), bf16),
            vm((1040, 1024), bf16),
            vm((1040, 1024), f32),
            vm((1024, 1024), f32),
            vm((2, 2, 2, 2, 2, 64, WIDE), bf16),
            vm((1024, 256), bf16),
            vm((2, 2, 2, 2, 2, 64, WIDE), bf16),
            vm((2, 2, 2, 2, 64, WIDE), bf16),
            vm((256, 1024), bf16),
            vm((128, 1024), f32),
            vm((16, 1024), f32),
            vm((4, 16, 1024), f32),
            vm((4, 16, 1024), f32),
            vm((2, 128, 1024), bf16),
            vm((2, 128, 1024), bf16),
            vm((2, 2, 2, 2, 64, WIDE), bf16),
            vm((ROUNDS, 4, 64, WIDE), bf16),
            vm((ROUNDS, 2, 64, WIDE), bf16),
            vm((FAR_ROUNDS, 64, WIDE), bf16),
            vm((3, 4, 64, WIDE), bf16),
            vm((3, 4, 64, WIDE), bf16),
            vm((3, 2, 64, WIDE), bf16),
            vm((3, 2, 64, WIDE), bf16),
            vm((3, 64, WIDE), bf16),
            vm((3, 64, WIDE), bf16),
            vm((FEED, 64, WIDE), f32),
            dma((6, CHUNKS)),
            dma((6, CHUNKS)),
            dma((6, 3)),
            dma((6, FAR_ROUNDS)),
            dma((9,)),
            dma((9,)),
            dma((4,)),
            dma((4,)),
            dma((2,)),
            dma((2, 4)),
            dma((2,)),
            dma((2,)),
            dma,
            dma((4,)),
            dma((2,)),
            dma((2,)),
            dma((14,)),
        ],
        compiler_params=pltpu.CompilerParams(
            collective_id=0, has_side_effects=True, vmem_limit_bytes=63 * 1024 * 1024
        ),
    )(tok, ctx, gain_one, gain_two, cot, *weights, delay, lengths)


def copy_kernel(*refs):
    n = (len(refs) - 2) // 3
    srcs, dsts, held, in_sem, out_sem = refs[:n], refs[n : 2 * n], refs[2 * n : 3 * n], refs[-2], refs[-1]
    ins = [pltpu.make_async_copy(srcs[i], held[i], in_sem.at[i]) for i in range(n)]
    outs = [pltpu.make_async_copy(held[i], dsts[i], out_sem.at[i]) for i in range(n)]
    for cp in ins:
        cp.start()
    for cp_in, cp_out in zip(ins, outs):
        cp_in.wait()
        cp_out.start()
    for cp in outs:
        cp.wait()


def copy_all(arrays):
    n = len(arrays)
    hbm = pl.BlockSpec(memory_space=pltpu.HBM)
    return pl.pallas_call(
        copy_kernel,
        name="outputs",
        out_shape=tuple(jax.ShapeDtypeStruct(a.shape, a.dtype) for a in arrays),
        in_specs=[hbm] * n,
        out_specs=(hbm,) * n,
        scratch_shapes=[pltpu.VMEM(a.shape, a.dtype) for a in arrays]
        + [pltpu.SemaphoreType.DMA((n,)), pltpu.SemaphoreType.DMA((n,))],
        compiler_params=pltpu.CompilerParams(vmem_limit_bytes=63 * 1024 * 1024),
    )(*arrays)


def body_kernel(
    tokens,
    context,
    ctx_weight,
    delay,
    lengths,
    attn_gain,
    ffn_gain,
    qkv_weight,
    out_weight,
    gate_weight,
    up_weight,
    down_weight,
    cotangent,
):
    frame_count, positions, width = tokens.shape[1:]
    rows = frame_count * positions
    weights = (ctx_weight, qkv_weight[0], out_weight[0], gate_weight[0], up_weight[0], down_weight[0])
    mixed_out, d_tokens, d_context, d_ctx, d_gain_one, d_gain_two, *grads = call_layer(
        tokens.reshape(rows, width),
        context,
        attn_gain[0],
        ffn_gain[0],
        cotangent.reshape(rows, width),
        weights,
        delay,
        lengths,
    )
    mixed_out, d_tokens, d_context, d_ctx, d_gain_one, d_gain_two, *grads = copy_all(
        (mixed_out, d_tokens, d_context, d_ctx, d_gain_one, d_gain_two, *grads[:-2])
    )
    d_qkv, d_out, d_gate, d_up, d_down = grads
    return (
        mixed_out.reshape(tokens.shape),
        d_tokens.reshape(tokens.shape),
        d_context,
        d_ctx,
        d_gain_one[None],
        d_gain_two[None],
        d_qkv[None],
        d_out[None],
        d_gate[None],
        d_up[None],
        d_down[None],
    )


def body(
    tokens,
    context,
    ctx_weight,
    delay,
    lengths,
    attn_gain,
    ffn_gain,
    qkv_weight,
    out_weight,
    gate_weight,
    up_weight,
    down_weight,
    cotangent,
):
    frame_count = tokens.shape[1]
    positions = tokens.shape[2]
    model_width = tokens.shape[3]
    token_rows = frame_count * positions
    head_scale = HEAD ** (-0.5)
    ctx_full = lax.all_gather(context, "stream", axis=1, tiled=True)
    ctx_rows = lax.all_gather(ctx_weight, ("stream", "frames"), axis=0, tiled=True)
    shift_term = flat_dot(ctx_full, ctx_rows)
    inputs = tokens[0]
    rim_rows = shifted(inputs[frame_count - 2 :], "frames", 1)
    extended = jnp.concatenate([rim_rows, inputs], axis=0).astype(jnp.float32)
    frame_ids = lax.axis_index("frames") * frame_count + jnp.arange(frame_count, dtype=jnp.int32)
    chosen, valid_rows = shift_tables(delay, lengths, frame_ids)
    layer_in = jnp.broadcast_to(shift_term[:, None, :], (frame_count, positions, model_width))
    for offset in range(3):
        piece = extended[2 - offset : 2 - offset + frame_count]
        layer_in = (
            layer_in + chosen[offset][None, :, None] * valid_rows[offset][:, None, None] * piece
        )
    weights = (
        lax.all_gather(qkv_weight[0], "frames", axis=0, tiled=True),
        lax.all_gather(out_weight[0], "frames", axis=0, tiled=True),
        lax.all_gather(gate_weight[0], "frames", axis=0, tiled=True),
        lax.all_gather(up_weight[0], "frames", axis=0, tiled=True),
        lax.all_gather(down_weight[0], "frames", axis=0, tiled=True),
    )
    w_qkv, w_out, w_gate, w_up, w_down = weights
    gain_one = attn_gain[0].astype(jnp.float32)
    gain_two = ffn_gain[0].astype(jnp.float32)
    normed = norm_rows(layer_in, gain_one).astype(jnp.bfloat16).reshape(token_rows, model_width)
    qkv = (
        flat_dot(normed, w_qkv).astype(jnp.bfloat16).reshape(frame_count, positions, 3, HEADS, HEAD)
    )
    queries = qkv[:, :, 0]
    key_part = qkv[:, :, 1]
    values = qkv[:, :, 2]
    scores = (
        jnp.einsum("fqhd,fkhd->fhqk", queries, key_part, preferred_element_type=jnp.float32)
        * head_scale
    )
    causal = jnp.arange(positions)[:, None] >= jnp.arange(positions)[None, :]
    scores = jnp.where(causal[None, None], scores, -1e30)
    probs = jax.nn.softmax(scores, axis=-1)
    probs_low = probs.astype(jnp.bfloat16)
    mixed = jnp.einsum("fhqk,fkhd->fqhd", probs_low, values, preferred_element_type=jnp.float32)
    mixed = mixed.astype(jnp.bfloat16).reshape(token_rows, model_width)
    after_attn = layer_in + flat_dot(mixed, w_out).reshape(frame_count, positions, model_width)
    normed_two = (
        norm_rows(after_attn, gain_two).astype(jnp.bfloat16).reshape(token_rows, model_width)
    )
    gate_pre = flat_dot(normed_two, w_gate)
    up_pre = flat_dot(normed_two, w_up)
    hidden = (jax.nn.silu(gate_pre) * up_pre).astype(jnp.bfloat16)
    out_full = after_attn + flat_dot(hidden, w_down).reshape(frame_count, positions, model_width)
    b_qkv, b_out, b_gate, b_up, b_down = weights
    grad_out = cotangent[0].astype(jnp.float32)
    grad_ff = grad_out.reshape(token_rows, model_width).astype(jnp.bfloat16)
    grad_down = trans_dot(hidden, grad_ff)
    grad_hidden = back_dot(grad_ff, b_down)
    sigmoid_gate = jax.nn.sigmoid(gate_pre)
    grad_gate = (
        grad_hidden * up_pre * sigmoid_gate * (1.0 + gate_pre * (1.0 - sigmoid_gate))
    ).astype(jnp.bfloat16)
    grad_up = (grad_hidden * gate_pre * sigmoid_gate).astype(jnp.bfloat16)
    grad_gate_w = trans_dot(normed_two, grad_gate)
    grad_up_w = trans_dot(normed_two, grad_up)
    grad_normed_two = (back_dot(grad_gate, b_gate) + back_dot(grad_up, b_up)).reshape(
        frame_count, positions, model_width
    )
    grad_after_norm, grad_gain_two = norm_back(grad_normed_two, after_attn, gain_two)
    grad_after = grad_out + grad_after_norm
    grad_branch = grad_after.reshape(token_rows, model_width).astype(jnp.bfloat16)
    grad_out_w = trans_dot(mixed, grad_branch)
    grad_mixed = (
        back_dot(grad_branch, b_out)
        .astype(jnp.bfloat16)
        .reshape(frame_count, positions, HEADS, HEAD)
    )
    grad_values = jnp.einsum(
        "fhqk,fqhd->fkhd", probs_low, grad_mixed, preferred_element_type=jnp.float32
    )
    grad_probs = jnp.einsum(
        "fqhd,fkhd->fhqk", grad_mixed, values, preferred_element_type=jnp.float32
    )
    grad_scores = (
        probs * (grad_probs - jnp.sum(grad_probs * probs, axis=-1, keepdims=True))
    ).astype(jnp.bfloat16)
    grad_queries = (
        jnp.einsum("fhqk,fkhd->fqhd", grad_scores, key_part, preferred_element_type=jnp.float32)
        * head_scale
    )
    grad_keys = (
        jnp.einsum("fhqk,fqhd->fkhd", grad_scores, queries, preferred_element_type=jnp.float32)
        * head_scale
    )
    grad_qkv = jnp.stack([grad_queries, grad_keys, grad_values], axis=2).astype(jnp.bfloat16)
    grad_qkv = grad_qkv.reshape(token_rows, 3 * model_width)
    grad_qkv_w = trans_dot(normed, grad_qkv)
    all_parts = (
        lax.psum_scatter(grad_qkv_w, "frames", scatter_dimension=0, tiled=True),
        lax.psum_scatter(grad_out_w, "frames", scatter_dimension=0, tiled=True),
        lax.psum_scatter(grad_gate_w, "frames", scatter_dimension=0, tiled=True),
        lax.psum_scatter(grad_up_w, "frames", scatter_dimension=0, tiled=True),
        lax.psum_scatter(grad_down, "frames", scatter_dimension=0, tiled=True),
    )
    d_qkv_rows, d_out_rows, d_gate_rows, d_up_rows, d_down_rows = all_parts
    grad_normed = back_dot(grad_qkv, b_qkv).reshape(frame_count, positions, model_width)
    grad_in_norm, grad_gain_one = norm_back(grad_normed, layer_in, gain_one)
    grad_in = grad_after + grad_in_norm
    gain_sums = lax.psum((grad_gain_one, grad_gain_two), "frames")
    grad_shift = jnp.sum(grad_in, axis=1).astype(jnp.bfloat16)
    grad_ctx_w = trans_dot(ctx_full, grad_shift)
    ctx_w_rows = lax.psum_scatter(grad_ctx_w, ("stream", "frames"), scatter_dimension=0, tiled=True)
    grad_context = back_dot(grad_shift, ctx_rows)
    context_half = lax.psum_scatter(
        grad_context.astype(jnp.bfloat16), "stream", scatter_dimension=1, tiled=True
    ).astype(jnp.float32)
    grad_ext = jnp.zeros((frame_count + 2, positions, model_width), jnp.float32)
    for offset in range(3):
        term = chosen[offset][None, :, None] * valid_rows[offset][:, None, None] * grad_in
        grad_ext = grad_ext + jnp.pad(term, ((2 - offset, offset), (0, 0), (0, 0)))
    back_rows = shifted(grad_ext[:2].astype(jnp.bfloat16), "frames", -1).astype(jnp.float32)
    grad_tokens = grad_ext[2:].at[frame_count - 2 :].add(back_rows)
    return (
        out_full.astype(jnp.bfloat16)[None],
        grad_tokens[None],
        context_half,
        ctx_w_rows,
        gain_sums[0][None],
        gain_sums[1][None],
        d_qkv_rows[None],
        d_out_rows[None],
        d_gate_rows[None],
        d_up_rows[None],
        d_down_rows[None],
    )


def solution(mesh):
    fits = mesh.shape["frames"] == 16 and mesh.shape["stream"] == 2
    return jax.shard_map(
        body_kernel if fits else body,
        mesh=mesh,
        in_specs=(
            P("stream", "frames", None, None),
            P("frames", "stream"),
            P(("stream", "frames"), None),
            P(),
            P(),
            P("stream", None, None),
            P("stream", None, None),
            P("stream", "frames", None),
            P("stream", "frames", None),
            P("stream", "frames", None),
            P("stream", "frames", None),
            P("stream", "frames", None),
            P("stream", "frames", None, None),
        ),
        out_specs=(
            P("stream", "frames", None, None),
            P("stream", "frames", None, None),
            P("frames", "stream"),
            P(("stream", "frames"), None),
            P("stream", None, None),
            P("stream", None, None),
            P("stream", "frames", None),
            P("stream", "frames", None),
            P("stream", "frames", None),
            P("stream", "frames", None),
            P("stream", "frames", None),
        ),
        check_vma=False,
    )
```

```python
import jax
import jax.numpy as jnp
from jax import lax
from jax.experimental import pallas as pl
from jax.experimental.pallas import tpu as pltpu
from jax.sharding import PartitionSpec as P

HEADS = 16
HEAD = 64


epsilon = 1e-05


def shifted(x, axis, by):
    length = lax.axis_size(axis)
    pairs = [(i, i + by) for i in range(length) if 0 <= i + by < length]
    return lax.ppermute(x, axis, pairs)


def flat_dot(left, right):
    return jnp.dot(left, right, preferred_element_type=jnp.float32)


def trans_dot(left, right):
    return lax.dot_general(
        left, right, (((0,), (0,)), ((), ())), preferred_element_type=jnp.float32
    )


def back_dot(left, right):
    return lax.dot_general(
        left, right, (((1,), (1,)), ((), ())), preferred_element_type=jnp.float32
    )


def norm_rows(rows, gain):
    return rows * lax.rsqrt(jnp.mean(rows * rows, axis=-1, keepdims=True) + epsilon) * gain


def norm_back(grad_normed, rows, gain):
    scale = lax.rsqrt(jnp.mean(rows * rows, axis=-1, keepdims=True) + epsilon)
    unit = rows * scale
    grad_gain = jnp.sum(grad_normed * unit, axis=0)
    grad_unit = grad_normed * gain
    grad_rows = scale * (grad_unit - unit * jnp.mean(grad_unit * unit, axis=-1, keepdims=True))
    return (grad_rows, grad_gain)


def shift_tables(delay, lengths, frame_ids):
    starts = jnp.cumsum(lengths) - lengths
    at_start = jnp.any(frame_ids[:, None] == starts[None, :], axis=1)
    after_start = jnp.any(frame_ids[:, None] - 1 == starts[None, :], axis=1)
    keep_one = jnp.logical_not(at_start)
    keep_two = jnp.logical_and(keep_one, jnp.logical_not(after_start))
    valid_rows = jnp.stack([jnp.ones_like(keep_one), keep_one, keep_two]).astype(jnp.float32)
    chosen = (delay[None, :] == jnp.arange(3, dtype=jnp.int32)[:, None]).astype(jnp.float32)
    return (chosen, valid_rows)


MESH = pl.DeviceIdType.MESH
CHUNKS = 17
FEED = 11
WIDE = 768
ROUNDS = 5
FAR_ROUNDS = 7
SPLIT = ((0, 48), (48, 64))
HALVES = ((0, 32), (32, 64))
WHOLE = ((0, 64),)
GATHER_HALVES = 6
REDUCE_HALVES = 17


def mm(a, b):
    return jnp.dot(a, b, preferred_element_type=jnp.float32)


def nt(a, b):
    return lax.dot_general(a, b, (((1,), (1,)), ((), ())), preferred_element_type=jnp.float32)


def tn(a, b):
    return lax.dot_general(a, b, (((0,), (0,)), ((), ())), preferred_element_type=jnp.float32)


def either(cond, fn):
    if isinstance(cond, bool):
        if cond:
            fn()
    else:
        pl.when(cond)(fn)


def within(t, low, high):
    if isinstance(t, int):
        return low <= t < high
    return jnp.logical_and(t >= low, t < high)


def layer_kernel(
    tok_hbm,
    ctx,
    gain_one,
    gain_two,
    cot_hbm,
    ctx_own,
    qkv_own,
    out_own,
    gate_hbm,
    up_hbm,
    down_hbm,
    delay,
    lengths,
    mixed_hbm,
    dtok_hbm,
    dctx,
    dctxw_hbm,
    dgain_one,
    dgain_two,
    dqkv_hbm,
    dout_hbm,
    dgate_hbm,
    dup_hbm,
    ddown_hbm,
    gathered,
    pend,
    cot,
    gate_own,
    up_own,
    down_own,
    w_own,
    lin,
    n1,
    n1t,
    qkv,
    mixed,
    aft,
    n2,
    n2t,
    oacc,
    gn,
    wbuf,
    wtail,
    part,
    part_own,
    hidt,
    shift,
    gacc,
    gsend,
    grecv,
    xsend,
    xrecv,
    r_c,
    r_y,
    r_zl,
    r_zh,
    t_keep,
    t_send,
    u_keep,
    u_send,
    v_keep,
    v_send,
    fin,
    ag_ss,
    ag_rs,
    rs_ss,
    rs_rs,
    x_ss,
    x_rs,
    g_ss,
    g_rs,
    own_sem,
    load_sem,
    pend_sem,
    half_sem,
    tok_sem,
    in_sem,
    rim_ss,
    rim_rs,
    out_sem,
):
    s = lax.axis_index("stream")
    f = lax.axis_index("frames")
    c = f % 2
    y = (f // 2) % 2
    zl = (f // 4) % 2
    zh = f // 8
    d_c = (s, f + 1 - 2 * c)
    d_y = (s, f + 2 - 4 * y)
    d_zl = (s, f + 4 - 8 * zl)
    d_zh = (s, f + 8 - 16 * zh)
    d_x = (1 - s, f)
    partners = (d_zh, d_zl, d_y, d_c)

    frames = lax.axis_size("frames")
    has_next, has_prev = f < frames - 1, f > 0
    d_next, d_prev = (s, f + 1), (s, f - 1)

    tokext = n2t
    tok_copy = pltpu.make_async_copy(tok_hbm, tokext.at[16:1040], tok_sem)
    fetches = [
        pltpu.make_async_copy(src, dst, in_sem.at[i])
        for i, (src, dst) in enumerate(
            ((down_hbm, down_own), (gate_hbm, gate_own), (up_hbm, up_own), (cot_hbm, cot))
        )
    ]
    for cp in fetches:
        cp.start()
    tok_copy.start()

    barrier = pltpu.get_barrier_semaphore()

    def greet(device):
        pl.semaphore_signal(barrier, inc=1, device_id=device, device_id_type=MESH)

    for device in partners + (d_x,):
        greet(device)
    pl.when(has_next)(lambda: greet(d_next))
    pl.when(has_prev)(lambda: greet(d_prev))

    w_own[0, 0:32, 0:512] = ctx_own[:, 0:512]
    w_own[0, 32:64, 0:512] = ctx_own[:, 512:1024]
    w_own[0, :, 512:768] = out_own[:, 768:1024]
    w_own[5] = out_own[:, 0:768]
    for g in range(4):
        for part_id in range(3):
            at = part_id * 1024 + g * 256
            w_own[1 + g, :, part_id * 256 : part_id * 256 + 256] = qkv_own[:, at : at + 256]

    def own_copy(low, high, i):
        return pltpu.make_async_copy(
            w_own.at[low:high], gathered.at[low:high, zh, zl, y, c], own_sem.at[i]
        )

    own_copy(0, 6, 0).start()

    pl.semaphore_wait(barrier, 5 + has_next.astype(jnp.int32) + has_prev.astype(jnp.int32))

    def remote(src, dst, ss, rs, device):
        return pltpu.make_async_remote_copy(
            src_ref=src, dst_ref=dst, send_sem=ss, recv_sem=rs, device_id=device, device_id_type=MESH
        )

    def ag_copies(stage, k, split):
        low, high = (slice(*rows) for rows in split)
        if stage == 0:
            triples = [(w_own.at[k], gathered.at[k, zh, zl, y, c], d_zh)]
        elif stage == 1:
            near, side = gathered.at[k, :, zl, y, c, low], gathered.at[k, :, zl, y, c, high]
            triples = [(near, near, d_zl), (side, side, d_y)]
        elif stage == 2:
            side, near = gathered.at[k, :, :, y, c, low], gathered.at[k, :, zl, :, c, high]
            triples = [(side, side, d_y), (near, near, d_zl)]
        else:
            own = gathered.at[k, :, :, :, c]
            triples = [(own, own, d_c)]
        first = (0, 1, 3, 5)[stage]
        return [
            remote(src, dst, ag_ss.at[first + i, k], ag_rs.at[first + i, k], device)
            for i, (src, dst, device) in enumerate(triples)
        ]

    def choose(k, bound, under, above, fn):
        if isinstance(k, int):
            fn(under if k < bound else above)
        else:
            pl.when(k < bound)(lambda: fn(under))
            pl.when(k >= bound)(lambda: fn(above))

    def ag_do(act, stage, k):
        if stage in (0, 3):
            act(ag_copies(stage, k, SPLIT))
        else:
            choose(k, GATHER_HALVES, SPLIT, HALVES, lambda split: act(ag_copies(stage, k, split)))

    def by_split(r, fn):
        choose(r, REDUCE_HALVES, SPLIT, HALVES, fn)

    def start_all(copies):
        for cp in copies:
            cp.start()

    def wait_recv_all(copies):
        for cp in copies:
            cp.wait_recv()

    def wait_send_all(copies):
        for cp in copies:
            cp.wait_send()

    class load_copy:
        def __init__(self, k, slot):
            self.parts = [
                pltpu.make_async_copy(
                    gathered.at[k, i // 2, i % 2], wbuf.at[slot, i // 2, i % 2], load_sem.at[slot, i]
                )
                for i in range(4)
            ]

        def start(self):
            for cp in self.parts:
                cp.start()

        def wait(self):
            for cp in self.parts:
                cp.wait()

    def ag_step(stage, k):
        def go():
            if stage > 0:
                ag_do(wait_recv_all, stage - 1, k)
            ag_do(start_all, stage, k)
        either(within(k, 0, CHUNKS), go)

    def ag_tick(t, gap=1):
        for stage in range(3):
            ag_step(stage, t - gap * stage)

    def ag_ready(k):
        def ready():
            ag_do(wait_recv_all, 3, k)
            load_copy(k, k % 2).start()
        either(within(k, 0, CHUNKS), ready)

    def rs_copies(stage, r, split):
        two, slot = r % (2 if stage == 0 else 3), r % (FAR_ROUNDS if stage == 3 else ROUNDS)
        if stage == 0:
            triples = [(pend.at[r, :, :, :, 1 - c], r_c.at[two], d_c)]
        elif stage == 3:
            triples = [(v_send.at[two], r_zh.at[slot], d_zh)]
        else:
            src, dst = ((t_send, r_y), (u_send, r_zl))[stage - 1]
            devices = ((d_y, d_zl), (d_zl, d_y))[stage - 1]
            triples = [
                (src.at[two, :, low:high], dst.at[slot, :, low:high], device)
                for (low, high), device in zip(split, devices)
            ]
        first = (0, 1, 3, 5)[stage]
        return [
            remote(src, dst, rs_ss.at[first + i, two], rs_rs.at[first + i, slot], device)
            for i, (src, dst, device) in enumerate(triples)
        ]

    def rs_do(act, stage, r):
        if stage in (0, 3):
            act(rs_copies(stage, r, SPLIT))
        else:
            by_split(r, lambda split: act(rs_copies(stage, r, split)))

    def add(a, b):
        return a.astype(jnp.float32) + b.astype(jnp.float32)

    def place_result(k, res):
        if not isinstance(k, int):
            @pl.when(k < FEED)
            def _():
                fin[k] = res
            pl.when(k == FEED)(lambda: place_result(FEED, res))
            return
        if k < FEED:
            fin[k] = res
        elif k == FEED:
            aft[384:448, 0:768] = res
        elif k < CHUNKS - 1:
            g = k - FEED - 1
            for p in range(3):
                aft[192 + 64 * p : 256 + 64 * p, g * 256 : g * 256 + 256] = res[:, p * 256 : p * 256 + 256]
        else:
            aft[384:448, 768:1024] = res[:, 512:768]
            aft[448:480, 0:512] = res[0:32, 0:512]
            aft[448:480, 512:1024] = res[32:64, 0:512]

    def out_copies():
        pairs = [(aft.at[384:448], dout_hbm), (aft.at[448:480], dctxw_hbm)]
        for p in range(3):
            pairs.append((aft.at[192 + 64 * p : 256 + 64 * p], dqkv_hbm.at[:, p * 1024 : p * 1024 + 1024]))
        return pairs

    def feed_copies():
        pairs = [(aft.at[512:688], ddown_hbm)]
        for i, hbm in enumerate((dgate_hbm, dup_hbm)):
            at = i * 768
            if i == 1:
                at = 704
            for p in range(3):
                n = 1024 if p < 2 else 768
                pairs.append((aft.at[at + 64 * p : at + 64 * p + 64, 0:n], hbm.at[:, p * 1024 : p * 1024 + n]))
        return pairs

    def out_copy(pair, i):
        return pltpu.make_async_copy(pair[0], pair[1], out_sem.at[i])

    def unpack_feed():
        for j in range(FEED):
            for q in range(4):
                aft[512 + j * 16 : 528 + j * 16, q * 256 : q * 256 + 256] = fin[j, q * 16 : q * 16 + 16, 512:768]
        for i, at in enumerate((0, 704)):
            cols = [
                fin[j, :, i * 256 + d * 16 : i * 256 + d * 16 + 16] for d in range(16) for j in range(FEED)
            ]
            for p in range(22):
                piece = jnp.concatenate(cols[p * 8 : p * 8 + 8], axis=1)
                row, col = at + 64 * (p // 8), (p % 8) * 128
                aft[row : row + 64, col : col + 128] = piece

    def pend_copy(r):
        return pltpu.make_async_copy(part.at[r % 2], pend.at[r], pend_sem.at[r % 2])

    def half_copy(r):
        return pltpu.make_async_copy(pend.at[r, :, :, :, c], part_own.at[r % 2], half_sem.at[r % 2])

    def part_done(r):
        either(within(r, 1, CHUNKS), lambda: pend_copy(r - 1).wait())
        pend_copy(r).start()

    def send_half(r):
        either(within(r, 2, CHUNKS), lambda: rs_do(wait_send_all, 0, r - 2))
        rs_do(start_all, 0, r)
        half_copy(r).start()

    def rs_tick(r):
        def stage_y():
            k = r - 1
            rs_do(wait_recv_all, 0, k)
            half_copy(k).wait()
            either(within(k, 3, CHUNKS), lambda: rs_do(wait_send_all, 1, k - 3))
            two, three = k % 2, k % 3

            def pieces(split):
                def piece(i, _):
                    a, b = i // 2, i % 2
                    for (low, high), send, keep in zip(split, ((b, 1 - y), (1 - zl, b)), ((b, y), (zl, b))):
                        for out, (m, n) in ((t_send, send), (t_keep, keep)):
                            out[three, i, low:high] = part_own[two, a, m, n, low:high] + r_c[two, a, m, n, low:high]
                    return 0

                lax.fori_loop(0, 4, piece, 0)

            by_split(k, pieces)
            rs_do(start_all, 1, k)
        either(within(r, 1, CHUNKS + 1), stage_y)
        either(within(r, 0, CHUNKS), lambda: send_half(r))

        def stage_zl():
            k = r - 3
            rs_do(wait_recv_all, 1, k)
            either(within(k, 3, CHUNKS), lambda: rs_do(wait_send_all, 2, k - 3))
            three, slot = k % 3, k % ROUNDS

            def pieces(split):
                for a in range(2):
                    for (low, high), mine in zip(split, (zl, y)):
                        for out, at in ((u_send, a * 2 + 1 - mine), (u_keep, a * 2 + mine)):
                            out[three, a, low:high] = t_keep[three, at, low:high] + r_y[slot, at, low:high]

            by_split(k, pieces)
            rs_do(start_all, 2, k)
        either(within(r, 3, CHUNKS + 3), stage_zl)

        def stage_zh():
            k = r - 5
            rs_do(wait_recv_all, 2, k)
            either(within(k, 3, CHUNKS), lambda: rs_do(wait_send_all, 3, k - 3))
            three, slot = k % 3, k % ROUNDS
            v_send[three] = u_keep[three, 1 - zh] + r_zl[slot, 1 - zh]
            v_keep[three] = u_keep[three, zh] + r_zl[slot, zh]
            rs_do(start_all, 3, k)
        either(within(r, 5, CHUNKS + 5), stage_zh)

        def last():
            k = r - 7
            rs_do(wait_recv_all, 3, k)
            place_result(k, add(v_keep[k % 3], r_zh[k % FAR_ROUNDS]))
        either(within(r, 7, CHUNKS + 7), last)

    rim_copy = remote(tok_hbm.at[1008:1024], tokext.at[0:16], rim_ss.at[0], rim_rs.at[0], d_next)
    halo_copy = remote(oacc.at[0:16], oacc.at[1024:1040], rim_ss.at[1], rim_rs.at[1], d_prev)
    pl.when(has_next)(lambda: rim_copy.start())

    @pl.when(jnp.logical_not(has_prev))
    def _():
        tokext[0:16, :] = jnp.zeros((16, 1024), jnp.bfloat16)

    @pl.when(jnp.logical_not(has_next))
    def _():
        oacc[1024:1040, :] = jnp.zeros((16, 1024), jnp.float32)

    gacc[...] = jnp.zeros_like(gacc)

    place = lax.broadcasted_iota(jnp.int32, (16, 8, 1), 1)
    wait = jnp.zeros((16, 8, 1), jnp.int32)
    for p in range(8):
        wait = jnp.where(place == p, delay[p], wait)

    def starts_at(frame):
        start = jnp.int32(0)
        hit = frame == start
        for i in range(lengths.shape[0] - 1):
            start = start + lengths[i]
            hit = jnp.logical_or(hit, frame == start)
        return hit

    def same_item(frame, j):
        ok = jnp.logical_not(starts_at(frame))
        if j == 2:
            ok = jnp.logical_and(ok, jnp.logical_not(starts_at(frame - 1)))
        return ok

    def frame_of(i):
        return f * 128 + i * 16 + lax.broadcasted_iota(jnp.int32, (16, 8, 1), 0)

    def pack_feed(own, at):
        for j in range(FEED):
            cols = [own[:, d * 176 + j * 16 : d * 176 + j * 16 + 16] for d in range(16)]
            w_own[6 + j, :, at : at + 256] = jnp.concatenate(cols, axis=1)

    ag_tick(0)
    own_copy(0, 6, 0).wait()
    ag_tick(1)
    for cp in fetches[:2]:
        cp.wait()
    for j in range(FEED):
        for q in range(4):
            w_own[6 + j, q * 16 : q * 16 + 16, 512:768] = down_own[
                j * 16 : j * 16 + 16, q * 256 : q * 256 + 256
            ]
    pack_feed(gate_own, 0)
    ag_tick(2)
    fetches[2].wait()
    pack_feed(up_own, 256)
    own_copy(6, CHUNKS, 1).start()
    ag_tick(3)
    ag_step(3, 0)
    ag_ready(0)
    own_copy(6, CHUNKS, 1).wait()
    ag_tick(4)

    load_copy(0, 0).wait()
    wtail[...] = wbuf[0, :, :, :, :, :, 512:768].reshape(1024, 256)
    half = shift.shape[1] // 2
    for h in range(2):
        w_half = wbuf[0, :, :, :, :, h * 32 : h * 32 + 32, 0:512].reshape(512, 512)
        shift[:, h * half : (h + 1) * half] = mm(ctx[...], w_half)
    xsend[0] = shift[...].astype(jnp.bfloat16)

    x_copy = remote(xsend.at[0], xrecv.at[0], x_ss.at[0], x_rs.at[0], d_x)
    x_copy.start()
    ag_tick(5)
    ag_step(3, 1)
    ag_ready(1)
    ag_tick(6)
    ag_step(0, 7)
    ag_step(0, 8)
    ag_step(1, 6)
    x_copy.wait_recv()
    shift[...] = shift[...] + xrecv[0].astype(jnp.float32)

    def rows_of(i, size):
        return pl.ds(pl.multiple_of(i * size, size), size)

    def norm1(i, _):
        rows = rows_of(i, 128)
        sh = shift[rows_of(i, 16), :]
        near = tokext[pl.ds(pl.multiple_of(i * 128, 128), 144), :].astype(jnp.float32)
        frame = frame_of(i)
        x = jnp.zeros((16, 8, 1024), jnp.float32)
        for j in range(3):
            keep = wait == j
            if j > 0:
                keep = jnp.logical_and(keep, same_item(frame, j))
            piece = near[16 - 8 * j : 144 - 8 * j].reshape(16, 8, 1024)
            x = jnp.where(keep, piece, x)
        x = x + sh[:, None, :]
        r = lax.rsqrt(jnp.mean(x * x, axis=-1, keepdims=True) + epsilon)
        n = (x * r * gain_one[...].astype(jnp.float32)[None]).reshape(128, 1024).astype(jnp.bfloat16)
        lin[rows, :] = x.reshape(128, 1024)
        n1[rows, :] = n
        n1t[:, rows] = n.T
        return 0

    tok_copy.wait()
    pl.when(has_prev)(lambda: rim_copy.wait_recv())
    lax.fori_loop(0, 8, norm1, 0)

    lane_low = lax.broadcasted_iota(jnp.int32, (128, 128), 1) < 64
    head_scale = HEAD ** (-0.5)

    def both(v):
        zero = jnp.zeros_like(v)
        return jnp.concatenate([jnp.where(lane_low, v, zero), jnp.where(lane_low, zero, v)], axis=0)

    own_frame = [
        lax.broadcasted_iota(jnp.int32, (8, 128), 1) // 8 == fr for fr in range(16)
    ]
    key_seen = lax.broadcasted_iota(jnp.int32, (8, 128), 0) <= lax.broadcasted_iota(jnp.int32, (8, 128), 1) % 8

    def compact(full, h):
        out = full[h * 128 : h * 128 + 8]
        for fr in range(1, 16):
            at = h * 128 + fr * 8
            out = jnp.where(own_frame[fr], full[at : at + 8], out)
        return out

    def spread(pair):
        zero = jnp.zeros((8, 128), jnp.float32)
        rows = [jnp.where(own_frame[fr], x, zero) for x in pair for fr in range(16)]
        return jnp.concatenate(rows, axis=0).astype(jnp.bfloat16)

    def probabilities(q, kk):
        full = nt(kk, q)
        pair = []
        for h in range(2):
            sc = jnp.where(key_seen, compact(full, h) * head_scale, -1e30)
            e = jnp.exp(sc - jnp.max(sc, axis=0, keepdims=True))
            pair.append(e / jnp.sum(e, axis=0, keepdims=True))
        return pair

    def pair_of(g, sub, lo):
        return [qkv[g, sub, at + lo : at + lo + 128] for at in (0, 256, 512)]

    def attn_fwd(g):
        def rows_step(i, _):
            for u in range(4):
                sub = rows_of(i * 4 + u, 128)
                for lo in (0, 128):
                    q, k, v = pair_of(g, sub, lo)
                    pr = spread(probabilities(q, both(k)))
                    out = tn(pr, both(v)).astype(jnp.bfloat16)
                    mixed[sub, pl.ds(pl.multiple_of(g * 256 + lo, 128), 128)] = out
            return 0
        lax.fori_loop(0, 2, rows_step, 0)

    def attn_bwd(g):
        def rows_step(i, _):
            for u in range(4):
                sub = rows_of(i * 4 + u, 128)
                for lo in (0, 128):
                    q, k, v = pair_of(g, sub, lo)
                    do = mixed[sub, pl.ds(pl.multiple_of(g * 256 + lo, 128), 128)]
                    kk = both(k)
                    pr = probabilities(q, kk)
                    full = nt(both(v), do)
                    ds = []
                    for h in range(2):
                        d = compact(full, h)
                        ds.append(pr[h] * (d - jnp.sum(d * pr[h], axis=0, keepdims=True)))
                    ds = spread(ds)
                    dq = tn(ds, kk) * head_scale
                    dk = mm(ds, q)
                    dv = mm(spread(pr), do)
                    qkv[g, sub, lo : lo + 128] = dq.astype(jnp.bfloat16)
                    qkv[g, sub, 256 + lo : 384 + lo] = (
                        jnp.where(lane_low, dk[:128], dk[128:]) * head_scale
                    ).astype(jnp.bfloat16)
                    qkv[g, sub, 512 + lo : 640 + lo] = jnp.where(lane_low, dv[:128], dv[128:]).astype(jnp.bfloat16)
            return 0
        lax.fori_loop(0, 2, rows_step, 0)

    def qkv_group(g, _):
        slot = (1 + g) % 2
        load_copy(1 + g, slot).wait()

        def rows_step(i, _):
            rows = rows_of(i, 256)
            qkv[g, rows, :] = mm(n1[rows, :], wbuf[slot].reshape(1024, WIDE)).astype(jnp.bfloat16)
            return 0

        lax.fori_loop(0, 4, rows_step, 0)
        ag_step(3, 2 + g)
        ag_tick(9 + g, 2)
        attn_fwd(g)
        ag_ready(2 + g)
        return 0

    lax.fori_loop(0, 4, qkv_group, 0)

    load_copy(5, 1).wait()

    def after(i, _):
        rows = rows_of(i, 256)
        m = mixed[rows, :]
        a = lin[rows, 0:WIDE] + mm(m, wbuf[1].reshape(1024, WIDE))
        b = lin[rows, WIDE:1024] + mm(m, wtail[...])
        x = jnp.concatenate([a, b], axis=1)
        aft[rows, :] = x
        oacc[rows, :] = x
        gn[rows, :] = jnp.zeros((256, 1024), jnp.float32)
        x3 = x.reshape(32, 8, 1024)
        r = lax.rsqrt(jnp.mean(x3 * x3, axis=-1, keepdims=True) + epsilon)
        n = (x3 * r * gain_two[...].astype(jnp.float32)[None]).reshape(256, 1024).astype(jnp.bfloat16)
        n2[rows, :] = n
        n2t[0:1024, rows] = n.T
        return 0

    lax.fori_loop(0, 2, after, 0)
    ag_step(3, 6)
    ag_tick(13, 2)
    lax.fori_loop(2, 4, after, 0)
    ag_ready(6)
    fetches[3].wait()

    def feed(j, _):
        slot = j % 2
        load_copy(6 + j, slot).wait()
        two = j % 2

        def rows_step(i):
            rows = slice(i * 512, i * 512 + 512)
            w_gu = wbuf[slot, :, :, :, :, :, 0:512].reshape(1024, 512)
            pre = mm(n2[rows, :], w_gu)
            gate, up = pre[:, :256], pre[:, 256:]
            g_hid = jnp.zeros((512, 256), jnp.float32)
            for q in range(4):
                w_q = wbuf[slot, :, :, :, :, q * 16 : q * 16 + 16, 512:768].reshape(256, 256)
                g_hid = g_hid + nt(cot[rows, q * 256 : q * 256 + 256], w_q)
            sig = jax.nn.sigmoid(gate)
            silu = gate * sig
            hid = (silu * up).astype(jnp.bfloat16)
            g_gate = (g_hid * up * sig * (1.0 + gate * (1.0 - sig))).astype(jnp.bfloat16)
            g_up = (g_hid * silu).astype(jnp.bfloat16)
            for q in range(4):
                w_q = wbuf[slot, :, :, :, :, q * 16 : q * 16 + 16, 512:768].reshape(256, 256)
                oacc[rows, q * 256 : q * 256 + 256] += mm(hid, w_q)
            both_g = jnp.concatenate([g_gate, g_up], axis=1)
            n1[rows, 0:512] = both_g
            hidt[:, rows] = hid.T
            back = nt(both_g, w_gu)
            gn[rows, :] += back

        for i in range(2):
            rows_step(i)
        ag_step(3, 7 + j)
        ag_tick(14 + j, 2)

        def weight_step(m, _):
            res = mm(n2t[rows_of(m, 512), :], n1[:, 0:512]).astype(jnp.bfloat16).reshape(2, 2, 2, 64, 512)
            part[two, m, :, :, :, :, 0:512] = res
            return 0

        lax.fori_loop(0, 2, weight_step, 0)
        ag_ready(7 + j)
        for q in range(4):
            res = mm(hidt[...], cot[:, q * 256 : q * 256 + 256]).astype(jnp.bfloat16)
            part[two, :, :, :, :, q * 16 : q * 16 + 16, 512:768] = res.reshape(2, 2, 2, 2, 16, 256)
        part_done(j)
        pl.when(jnp.logical_and(j % 2 == 1, j < 6))(lambda: rs_tick(j // 2))
        pl.when(j >= 6)(lambda: rs_tick(j - 3))
        return 0

    lax.fori_loop(0, FEED, feed, 0)
    load_copy(5, 1).start()
    load_copy(1, 0).start()

    def norm2_back(i, _):
        rows = rows_of(i, 128)
        n2t[rows, :] = oacc[rows, :].astype(jnp.bfloat16)
        n1[:, rows] = mixed[rows, :].T
        x = aft[rows, :].reshape(16, 8, 1024)
        g = gn[rows, :].reshape(16, 8, 1024)
        gn[rows, :] = jnp.zeros((128, 1024), jnp.float32)
        r = lax.rsqrt(jnp.mean(x * x, axis=-1, keepdims=True) + epsilon)
        unit = x * r
        gacc[8:16, :] += jnp.sum(g * unit, axis=0)
        gu = g * gain_two[...].astype(jnp.float32)[None]
        back = r * (gu - unit * jnp.mean(gu * unit, axis=-1, keepdims=True))
        total = cot[rows, :].astype(jnp.float32) + back.reshape(128, 1024)
        oacc[rows, :] = total
        n2[rows, :] = total.astype(jnp.bfloat16)
        return 0

    lax.fori_loop(0, 8, norm2_back, 0)
    mixed_copy = pltpu.make_async_copy(n2t.at[0:1024], mixed_hbm, out_sem.at[0])
    mixed_copy.start()
    rs_tick(8)


    def out_weight_step(m, _):
        res = mm(n1[rows_of(m, 256), :], n2[:, 0:WIDE]).astype(jnp.bfloat16)
        part[1, m // 2, m % 2] = res.reshape(2, 2, 64, WIDE)
        return 0

    lax.fori_loop(0, 4, out_weight_step, 0)
    part_done(11)

    def mixed_back(i, _):
        rows = rows_of(i, 256)
        g = n2[rows, :]
        res = nt(g[:, 0:WIDE], wbuf[1].reshape(1024, WIDE)) + nt(g[:, WIDE:1024], wtail[...])
        mixed[rows, :] = res.astype(jnp.bfloat16)
        return 0

    load_copy(5, 1).wait()
    lax.fori_loop(0, 4, mixed_back, 0)
    load_copy(2, 1).start()
    rs_tick(9)

    def qkv_back(g, _):
        slot = g % 2
        attn_bwd(g)
        pend_copy(11 + g).wait()
        rs_tick(10 + g + g // 2)
        two = g % 2

        def weight_step(m, _):
            res = mm(n1t[rows_of(m, 256), :], qkv[g]).astype(jnp.bfloat16)
            part[two, m // 2, m % 2] = res.reshape(2, 2, 64, WIDE)
            return 0

        lax.fori_loop(0, 4, weight_step, 0)
        pend_copy(12 + g).start()

        def rows_step(i, _):
            rows = rows_of(i, 256)
            back = nt(qkv[g, rows, :], wbuf[slot].reshape(1024, WIDE))
            gn[rows, :] += back
            return 0

        load_copy(1 + g, slot).wait()
        lax.fori_loop(0, 4, rows_step, 0)
        pl.when(g == 1)(lambda: rs_tick(12))
        pl.when(g < 2)(lambda: load_copy(3 + g, slot).start())
        pl.when(g == 2)(lambda: load_copy(0, 0).start())
        return 0

    lax.fori_loop(0, 4, qkv_back, 0)

    def norm1_back(i, _):
        rows = rows_of(i, 128)
        x = lin[rows, :].reshape(16, 8, 1024)
        g = gn[rows, :].reshape(16, 8, 1024)
        r = lax.rsqrt(jnp.mean(x * x, axis=-1, keepdims=True) + epsilon)
        unit = x * r
        gacc[0:8, :] += jnp.sum(g * unit, axis=0)
        gu = g * gain_one[...].astype(jnp.float32)[None]
        back = r * (gu - unit * jnp.mean(gu * unit, axis=-1, keepdims=True))
        total = oacc[rows, :].reshape(16, 8, 1024) + back
        oacc[rows, :] = total.reshape(128, 1024)
        few = rows_of(i, 16)
        g_frame = jnp.sum(total, axis=1)
        shift[few, :] = g_frame
        xsend[1, few, :] = g_frame.astype(jnp.bfloat16)
        x_piece(i).start()
        return 0

    def x_piece(i):
        few = rows_of(i, 16)
        return remote(xsend.at[1, few], xrecv.at[1, few], x_ss.at[1 + i], x_rs.at[1 + i], d_x)

    lax.fori_loop(0, 8, norm1_back, 0)
    pl.when(has_prev)(lambda: halo_copy.start())
    def gain_copy(i):
        return remote(gsend.at[i], grecv.at[i], g_ss.at[i], g_rs.at[i], partners[i])

    gsend[0] = gacc[...]
    gain_copy(0).start()

    pend_copy(15).wait()
    rs_tick(15)
    load_copy(0, 0).wait()

    def out_tail_step(m, _):
        res = mm(n1[rows_of(m, 256), :], n2[:, WIDE:1024]).astype(jnp.bfloat16)
        part[0, m // 2, m % 2, :, :, :, 512:768] = res.reshape(2, 2, 64, 256)
        return 0

    lax.fori_loop(0, 4, out_tail_step, 0)

    for i in range(8):
        x_piece(i).wait_recv()
    g_low = (shift[...] + xrecv[1].astype(jnp.float32)).astype(jnp.bfloat16)
    ctx_t = ctx[...].T
    for h in range(2):
        gh = g_low[:, h * 512 : (h + 1) * 512]
        res = mm(ctx_t, gh).astype(jnp.bfloat16).reshape(2, 2, 2, 2, 32, 512)
        part[0, :, :, :, :, h * 32 : h * 32 + 32, 0:512] = res
    pend_copy(16).start()
    pend_copy(16).wait()
    w0 = wbuf[0, :, :, :, :, 0:32, 0:512].reshape(512, 512)
    w1 = wbuf[0, :, :, :, :, 32:64, 0:512].reshape(512, 512)
    dctx[...] = nt(g_low[:, :512], w0) + nt(g_low[:, 512:], w1)

    def dtok(i, _):
        rows = rows_of(i, 128)
        near = oacc[pl.ds(pl.multiple_of(i * 128, 128), 144), :]
        frame = frame_of(i)
        x = jnp.zeros((16, 8, 1024), jnp.float32)
        for j in range(3):
            keep = wait == j
            if j > 0:
                keep = jnp.logical_and(keep, same_item(frame + j, j))
            x = jnp.where(keep, near[8 * j : 128 + 8 * j].reshape(16, 8, 1024), x)
        gn[rows, :] = x.reshape(128, 1024)
        return 0

    rs_tick(16)
    dtok_copy = pltpu.make_async_copy(gn, dtok_hbm, out_sem.at[1])
    last_out = [out_copy(pair, 9 + i) for i, pair in enumerate(out_copies())]
    feed_out = [out_copy(pair, 2 + i) for i, pair in enumerate(feed_copies())]
    for i in range(4):
        gain_copy(i).wait_recv()
        if i < 3:
            gsend[i + 1] = gsend[i] + grecv[i]
            gain_copy(i + 1).start()
        else:
            total = gsend[i] + grecv[i]
            dgain_one[...] = total[0:8]
            dgain_two[...] = total[8:16]
        rs_tick(17 + i)
        if i == 0:
            unpack_feed()
            for cp in feed_out:
                cp.start()
            pl.when(has_next)(lambda: halo_copy.wait_recv())
            lax.fori_loop(0, 8, dtok, 0)
            dtok_copy.start()

    rs_tick(21)
    rs_tick(22)
    for cp in last_out[2:]:
        cp.start()
    rs_tick(23)

    for cp in last_out[:2]:
        cp.start()
    pl.when(has_next)(lambda: rim_copy.wait_send())
    pl.when(has_prev)(lambda: halo_copy.wait_send())

    for i in range(4):
        gain_copy(i).wait_send()
    x_copy.wait_send()
    for i in range(8):
        x_piece(i).wait_send()

    for stage in range(4):
        for k in range(CHUNKS - (2 if stage == 0 else 3), CHUNKS):
            rs_do(wait_send_all, stage, k)

    def drain(k, _):
        for stage in range(4):
            ag_do(wait_send_all, stage, k)
        return 0

    lax.fori_loop(0, CHUNKS, drain, 0)
    mixed_copy.wait()
    dtok_copy.wait()
    for cp in feed_out + last_out:
        cp.wait()


def call_layer(tok, ctx, gain_one, gain_two, cot, weights, delay, lengths):
    f32, bf16 = jnp.float32, jnp.bfloat16
    vm, dma = pltpu.VMEM, pltpu.SemaphoreType.DMA
    shape = jax.ShapeDtypeStruct
    in_vmem, in_hbm, in_smem = (pl.BlockSpec(memory_space=m) for m in (pltpu.VMEM, pltpu.HBM, pltpu.SMEM))
    return pl.pallas_call(
        layer_kernel,
        name="layer",
        out_shape=(
            shape((1024, 1024), bf16),
            shape((1024, 1024), f32),
            shape((128, 512), f32),
            shape((32, 1024), f32),
            shape((8, 1024), f32),
            shape((8, 1024), f32),
            shape((64, 3072), f32),
            shape((64, 1024), f32),
            shape((64, 2816), f32),
            shape((64, 2816), f32),
            shape((176, 1024), f32),
            shape((CHUNKS, 2, 2, 2, 2, 64, WIDE), bf16),
            shape((CHUNKS, 2, 2, 2, 2, 64, WIDE), bf16),
        ),
        in_specs=[in_hbm] + [in_vmem] * 3 + [in_hbm] + [in_vmem] * 3 + [in_hbm] * 3 + [in_smem] * 2,
        out_specs=(in_hbm, in_hbm, in_vmem, in_hbm, in_vmem, in_vmem) + (in_hbm,) * 7,
        scratch_shapes=[
            vm((1024, 1024), bf16),
            vm((64, 2816), bf16),
            vm((64, 2816), bf16),
            vm((176, 1024), bf16),
            vm((CHUNKS, 64, WIDE), bf16),
            vm((1024, 1024), f32),
            vm((1024, 1024), bf16),
            vm((1024, 1024), bf16),
            vm((4, 1024, WIDE), bf16),
            vm((1024, 1024), bf16),
            vm((1024, 1024), f32),
            vm((1024, 1024), bf16),
            vm((1040, 1024), bf16),
            vm((1040, 1024), f32),
            vm((1024, 1024), f32),
            vm((2, 2, 2, 2, 2, 64, WIDE), bf16),
            vm((1024, 256), bf16),
            vm((2, 2, 2, 2, 2, 64, WIDE), bf16),
            vm((2, 2, 2, 2, 64, WIDE), bf16),
            vm((256, 1024), bf16),
            vm((128, 1024), f32),
            vm((16, 1024), f32),
            vm((4, 16, 1024), f32),
            vm((4, 16, 1024), f32),
            vm((2, 128, 1024), bf16),
            vm((2, 128, 1024), bf16),
            vm((2, 2, 2, 2, 64, WIDE), bf16),
            vm((ROUNDS, 4, 64, WIDE), bf16),
            vm((ROUNDS, 2, 64, WIDE), bf16),
            vm((FAR_ROUNDS, 64, WIDE), bf16),
            vm((3, 4, 64, WIDE), bf16),
            vm((3, 4, 64, WIDE), bf16),
            vm((3, 2, 64, WIDE), bf16),
            vm((3, 2, 64, WIDE), bf16),
            vm((3, 64, WIDE), bf16),
            vm((3, 64, WIDE), bf16),
            vm((FEED, 64, WIDE), f32),
            dma((6, CHUNKS)),
            dma((6, CHUNKS)),
            dma((6, 3)),
            dma((6, FAR_ROUNDS)),
            dma((9,)),
            dma((9,)),
            dma((4,)),
            dma((4,)),
            dma((2,)),
            dma((2, 4)),
            dma((2,)),
            dma((2,)),
            dma,
            dma((4,)),
            dma((2,)),
            dma((2,)),
            dma((14,)),
        ],
        compiler_params=pltpu.CompilerParams(
            collective_id=0, has_side_effects=True, vmem_limit_bytes=63 * 1024 * 1024
        ),
    )(tok, ctx, gain_one, gain_two, cot, *weights, delay, lengths)


def copy_kernel(*refs):
    n = (len(refs) - 2) // 3
    srcs, dsts, held, in_sem, out_sem = refs[:n], refs[n : 2 * n], refs[2 * n : 3 * n], refs[-2], refs[-1]
    ins = [pltpu.make_async_copy(srcs[i], held[i], in_sem.at[i]) for i in range(n)]
    outs = [pltpu.make_async_copy(held[i], dsts[i], out_sem.at[i]) for i in range(n)]
    for cp in ins:
        cp.start()
    for cp_in, cp_out in zip(ins, outs):
        cp_in.wait()
        cp_out.start()
    for cp in outs:
        cp.wait()


def copy_all(arrays):
    n = len(arrays)
    hbm = pl.BlockSpec(memory_space=pltpu.HBM)
    return pl.pallas_call(
        copy_kernel,
        name="outputs",
        out_shape=tuple(jax.ShapeDtypeStruct(a.shape, a.dtype) for a in arrays),
        in_specs=[hbm] * n,
        out_specs=(hbm,) * n,
        scratch_shapes=[pltpu.VMEM(a.shape, a.dtype) for a in arrays]
        + [pltpu.SemaphoreType.DMA((n,)), pltpu.SemaphoreType.DMA((n,))],
        compiler_params=pltpu.CompilerParams(vmem_limit_bytes=63 * 1024 * 1024),
    )(*arrays)


def body_kernel(
    tokens,
    context,
    ctx_weight,
    delay,
    lengths,
    attn_gain,
    ffn_gain,
    qkv_weight,
    out_weight,
    gate_weight,
    up_weight,
    down_weight,
    cotangent,
):
    frame_count, positions, width = tokens.shape[1:]
    rows = frame_count * positions
    weights = (ctx_weight, qkv_weight[0], out_weight[0], gate_weight[0], up_weight[0], down_weight[0])
    mixed_out, d_tokens, d_context, d_ctx, d_gain_one, d_gain_two, *grads = call_layer(
        tokens.reshape(rows, width),
        context,
        attn_gain[0],
        ffn_gain[0],
        cotangent.reshape(rows, width),
        weights,
        delay,
        lengths,
    )
    mixed_out, d_tokens, d_context, d_ctx, d_gain_one, d_gain_two, *grads = copy_all(
        (mixed_out, d_tokens, d_context, d_ctx, d_gain_one, d_gain_two, *grads[:-2])
    )
    d_qkv, d_out, d_gate, d_up, d_down = grads
    return (
        mixed_out.reshape(tokens.shape),
        d_tokens.reshape(tokens.shape),
        d_context,
        d_ctx,
        d_gain_one[None],
        d_gain_two[None],
        d_qkv[None],
        d_out[None],
        d_gate[None],
        d_up[None],
        d_down[None],
    )


def body(
    tokens,
    context,
    ctx_weight,
    delay,
    lengths,
    attn_gain,
    ffn_gain,
    qkv_weight,
    out_weight,
    gate_weight,
    up_weight,
    down_weight,
    cotangent,
):
    frame_count = tokens.shape[1]
    positions = tokens.shape[2]
    model_width = tokens.shape[3]
    token_rows = frame_count * positions
    head_scale = HEAD ** (-0.5)
    ctx_full = lax.all_gather(context, "stream", axis=1, tiled=True)
    ctx_rows = lax.all_gather(ctx_weight, ("stream", "frames"), axis=0, tiled=True)
    shift_term = flat_dot(ctx_full, ctx_rows)
    inputs = tokens[0]
    rim_rows = shifted(inputs[frame_count - 2 :], "frames", 1)
    extended = jnp.concatenate([rim_rows, inputs], axis=0).astype(jnp.float32)
    frame_ids = lax.axis_index("frames") * frame_count + jnp.arange(frame_count, dtype=jnp.int32)
    chosen, valid_rows = shift_tables(delay, lengths, frame_ids)
    layer_in = jnp.broadcast_to(shift_term[:, None, :], (frame_count, positions, model_width))
    for offset in range(3):
        piece = extended[2 - offset : 2 - offset + frame_count]
        layer_in = (
            layer_in + chosen[offset][None, :, None] * valid_rows[offset][:, None, None] * piece
        )
    weights = (
        lax.all_gather(qkv_weight[0], "frames", axis=0, tiled=True),
        lax.all_gather(out_weight[0], "frames", axis=0, tiled=True),
        lax.all_gather(gate_weight[0], "frames", axis=0, tiled=True),
        lax.all_gather(up_weight[0], "frames", axis=0, tiled=True),
        lax.all_gather(down_weight[0], "frames", axis=0, tiled=True),
    )
    w_qkv, w_out, w_gate, w_up, w_down = weights
    gain_one = attn_gain[0].astype(jnp.float32)
    gain_two = ffn_gain[0].astype(jnp.float32)
    normed = norm_rows(layer_in, gain_one).astype(jnp.bfloat16).reshape(token_rows, model_width)
    qkv = (
        flat_dot(normed, w_qkv).astype(jnp.bfloat16).reshape(frame_count, positions, 3, HEADS, HEAD)
    )
    queries = qkv[:, :, 0]
    key_part = qkv[:, :, 1]
    values = qkv[:, :, 2]
    scores = (
        jnp.einsum("fqhd,fkhd->fhqk", queries, key_part, preferred_element_type=jnp.float32)
        * head_scale
    )
    causal = jnp.arange(positions)[:, None] >= jnp.arange(positions)[None, :]
    scores = jnp.where(causal[None, None], scores, -1e30)
    probs = jax.nn.softmax(scores, axis=-1)
    probs_low = probs.astype(jnp.bfloat16)
    mixed = jnp.einsum("fhqk,fkhd->fqhd", probs_low, values, preferred_element_type=jnp.float32)
    mixed = mixed.astype(jnp.bfloat16).reshape(token_rows, model_width)
    after_attn = layer_in + flat_dot(mixed, w_out).reshape(frame_count, positions, model_width)
    normed_two = (
        norm_rows(after_attn, gain_two).astype(jnp.bfloat16).reshape(token_rows, model_width)
    )
    gate_pre = flat_dot(normed_two, w_gate)
    up_pre = flat_dot(normed_two, w_up)
    hidden = (jax.nn.silu(gate_pre) * up_pre).astype(jnp.bfloat16)
    out_full = after_attn + flat_dot(hidden, w_down).reshape(frame_count, positions, model_width)
    b_qkv, b_out, b_gate, b_up, b_down = weights
    grad_out = cotangent[0].astype(jnp.float32)
    grad_ff = grad_out.reshape(token_rows, model_width).astype(jnp.bfloat16)
    grad_down = trans_dot(hidden, grad_ff)
    grad_hidden = back_dot(grad_ff, b_down)
    sigmoid_gate = jax.nn.sigmoid(gate_pre)
    grad_gate = (
        grad_hidden * up_pre * sigmoid_gate * (1.0 + gate_pre * (1.0 - sigmoid_gate))
    ).astype(jnp.bfloat16)
    grad_up = (grad_hidden * gate_pre * sigmoid_gate).astype(jnp.bfloat16)
    grad_gate_w = trans_dot(normed_two, grad_gate)
    grad_up_w = trans_dot(normed_two, grad_up)
    grad_normed_two = (back_dot(grad_gate, b_gate) + back_dot(grad_up, b_up)).reshape(
        frame_count, positions, model_width
    )
    grad_after_norm, grad_gain_two = norm_back(grad_normed_two, after_attn, gain_two)
    grad_after = grad_out + grad_after_norm
    grad_branch = grad_after.reshape(token_rows, model_width).astype(jnp.bfloat16)
    grad_out_w = trans_dot(mixed, grad_branch)
    grad_mixed = (
        back_dot(grad_branch, b_out)
        .astype(jnp.bfloat16)
        .reshape(frame_count, positions, HEADS, HEAD)
    )
    grad_values = jnp.einsum(
        "fhqk,fqhd->fkhd", probs_low, grad_mixed, preferred_element_type=jnp.float32
    )
    grad_probs = jnp.einsum(
        "fqhd,fkhd->fhqk", grad_mixed, values, preferred_element_type=jnp.float32
    )
    grad_scores = (
        probs * (grad_probs - jnp.sum(grad_probs * probs, axis=-1, keepdims=True))
    ).astype(jnp.bfloat16)
    grad_queries = (
        jnp.einsum("fhqk,fkhd->fqhd", grad_scores, key_part, preferred_element_type=jnp.float32)
        * head_scale
    )
    grad_keys = (
        jnp.einsum("fhqk,fqhd->fkhd", grad_scores, queries, preferred_element_type=jnp.float32)
        * head_scale
    )
    grad_qkv = jnp.stack([grad_queries, grad_keys, grad_values], axis=2).astype(jnp.bfloat16)
    grad_qkv = grad_qkv.reshape(token_rows, 3 * model_width)
    grad_qkv_w = trans_dot(normed, grad_qkv)
    all_parts = (
        lax.psum_scatter(grad_qkv_w, "frames", scatter_dimension=0, tiled=True),
        lax.psum_scatter(grad_out_w, "frames", scatter_dimension=0, tiled=True),
        lax.psum_scatter(grad_gate_w, "frames", scatter_dimension=0, tiled=True),
        lax.psum_scatter(grad_up_w, "frames", scatter_dimension=0, tiled=True),
        lax.psum_scatter(grad_down, "frames", scatter_dimension=0, tiled=True),
    )
    d_qkv_rows, d_out_rows, d_gate_rows, d_up_rows, d_down_rows = all_parts
    grad_normed = back_dot(grad_qkv, b_qkv).reshape(frame_count, positions, model_width)
    grad_in_norm, grad_gain_one = norm_back(grad_normed, layer_in, gain_one)
    grad_in = grad_after + grad_in_norm
    gain_sums = lax.psum((grad_gain_one, grad_gain_two), "frames")
    grad_shift = jnp.sum(grad_in, axis=1).astype(jnp.bfloat16)
    grad_ctx_w = trans_dot(ctx_full, grad_shift)
    ctx_w_rows = lax.psum_scatter(grad_ctx_w, ("stream", "frames"), scatter_dimension=0, tiled=True)
    grad_context = back_dot(grad_shift, ctx_rows)
    context_half = lax.psum_scatter(
        grad_context.astype(jnp.bfloat16), "stream", scatter_dimension=1, tiled=True
    ).astype(jnp.float32)
    grad_ext = jnp.zeros((frame_count + 2, positions, model_width), jnp.float32)
    for offset in range(3):
        term = chosen[offset][None, :, None] * valid_rows[offset][:, None, None] * grad_in
        grad_ext = grad_ext + jnp.pad(term, ((2 - offset, offset), (0, 0), (0, 0)))
    back_rows = shifted(grad_ext[:2].astype(jnp.bfloat16), "frames", -1).astype(jnp.float32)
    grad_tokens = grad_ext[2:].at[frame_count - 2 :].add(back_rows)
    return (
        out_full.astype(jnp.bfloat16)[None],
        grad_tokens[None],
        context_half,
        ctx_w_rows,
        gain_sums[0][None],
        gain_sums[1][None],
        d_qkv_rows[None],
        d_out_rows[None],
        d_gate_rows[None],
        d_up_rows[None],
        d_down_rows[None],
    )


def solution(mesh):
    fits = mesh.shape["frames"] == 16 and mesh.shape["stream"] == 2
    return jax.shard_map(
        body_kernel if fits else body,
        mesh=mesh,
        in_specs=(
            P("stream", "frames", None, None),
            P("frames", "stream"),
            P(("stream", "frames"), None),
            P(),
            P(),
            P("stream", None, None),
            P("stream", None, None),
            P("stream", "frames", None),
            P("stream", "frames", None),
            P("stream", "frames", None),
            P("stream", "frames", None),
            P("stream", "frames", None),
            P("stream", "frames", None, None),
        ),
        out_specs=(
            P("stream", "frames", None, None),
            P("stream", "frames", None, None),
            P("frames", "stream"),
            P(("stream", "frames"), None),
            P("stream", None, None),
            P("stream", None, None),
            P("stream", "frames", None),
            P("stream", "frames", None),
            P("stream", "frames", None),
            P("stream", "frames", None),
            P("stream", "frames", None),
        ),
        check_vma=False,
    )
```

```python
import jax
import jax.numpy as jnp
from jax import lax
from jax.experimental import pallas as pl
from jax.experimental.pallas import tpu as pltpu
from jax.sharding import PartitionSpec as P

HEADS = 16
HEAD = 64


epsilon = 1e-05


def shifted(x, axis, by):
    length = lax.axis_size(axis)
    pairs = [(i, i + by) for i in range(length) if 0 <= i + by < length]
    return lax.ppermute(x, axis, pairs)


def flat_dot(left, right):
    return jnp.dot(left, right, preferred_element_type=jnp.float32)


def trans_dot(left, right):
    return lax.dot_general(
        left, right, (((0,), (0,)), ((), ())), preferred_element_type=jnp.float32
    )


def back_dot(left, right):
    return lax.dot_general(
        left, right, (((1,), (1,)), ((), ())), preferred_element_type=jnp.float32
    )


def norm_rows(rows, gain):
    return rows * lax.rsqrt(jnp.mean(rows * rows, axis=-1, keepdims=True) + epsilon) * gain


def norm_back(grad_normed, rows, gain):
    scale = lax.rsqrt(jnp.mean(rows * rows, axis=-1, keepdims=True) + epsilon)
    unit = rows * scale
    grad_gain = jnp.sum(grad_normed * unit, axis=0)
    grad_unit = grad_normed * gain
    grad_rows = scale * (grad_unit - unit * jnp.mean(grad_unit * unit, axis=-1, keepdims=True))
    return (grad_rows, grad_gain)


def shift_tables(delay, lengths, frame_ids):
    starts = jnp.cumsum(lengths) - lengths
    at_start = jnp.any(frame_ids[:, None] == starts[None, :], axis=1)
    after_start = jnp.any(frame_ids[:, None] - 1 == starts[None, :], axis=1)
    keep_one = jnp.logical_not(at_start)
    keep_two = jnp.logical_and(keep_one, jnp.logical_not(after_start))
    valid_rows = jnp.stack([jnp.ones_like(keep_one), keep_one, keep_two]).astype(jnp.float32)
    chosen = (delay[None, :] == jnp.arange(3, dtype=jnp.int32)[:, None]).astype(jnp.float32)
    return (chosen, valid_rows)


MESH = pl.DeviceIdType.MESH
CHUNKS = 17
FEED = 11
WIDE = 768
ROUNDS = 5
FAR_ROUNDS = 7
SPLIT = ((0, 48), (48, 64))
HALVES = ((0, 32), (32, 64))
WHOLE = ((0, 64),)
GATHER_HALVES = 6
REDUCE_HALVES = 17


def mm(a, b):
    return jnp.dot(a, b, preferred_element_type=jnp.float32)


def nt(a, b):
    return lax.dot_general(a, b, (((1,), (1,)), ((), ())), preferred_element_type=jnp.float32)


def tn(a, b):
    return lax.dot_general(a, b, (((0,), (0,)), ((), ())), preferred_element_type=jnp.float32)


def either(cond, fn):
    if isinstance(cond, bool):
        if cond:
            fn()
    else:
        pl.when(cond)(fn)


def within(t, low, high):
    if isinstance(t, int):
        return low <= t < high
    return jnp.logical_and(t >= low, t < high)


def layer_kernel(
    tok_hbm,
    ctx,
    gain_one,
    gain_two,
    cot_hbm,
    ctx_own,
    qkv_own,
    out_own,
    gate_hbm,
    up_hbm,
    down_hbm,
    delay,
    lengths,
    mixed_hbm,
    dtok_hbm,
    dctx,
    dctxw_hbm,
    dgain_one,
    dgain_two,
    dqkv_hbm,
    dout_hbm,
    dgate_hbm,
    dup_hbm,
    ddown_hbm,
    gathered,
    pend,
    cot,
    gate_own,
    up_own,
    down_own,
    w_own,
    lin,
    n1,
    n1t,
    qkv,
    mixed,
    aft,
    n2,
    n2t,
    oacc,
    gn,
    wbuf,
    wtail,
    part,
    part_own,
    hidt,
    shift,
    gacc,
    gsend,
    grecv,
    xsend,
    xrecv,
    r_c,
    r_y,
    r_zl,
    r_zh,
    t_keep,
    t_send,
    u_keep,
    u_send,
    v_keep,
    v_send,
    fin,
    ag_ss,
    ag_rs,
    rs_ss,
    rs_rs,
    x_ss,
    x_rs,
    g_ss,
    g_rs,
    own_sem,
    load_sem,
    pend_sem,
    half_sem,
    tok_sem,
    in_sem,
    rim_ss,
    rim_rs,
    out_sem,
):
    s = lax.axis_index("stream")
    f = lax.axis_index("frames")
    c = f % 2
    y = (f // 2) % 2
    zl = (f // 4) % 2
    zh = f // 8
    d_c = (s, f + 1 - 2 * c)
    d_y = (s, f + 2 - 4 * y)
    d_zl = (s, f + 4 - 8 * zl)
    d_zh = (s, f + 8 - 16 * zh)
    d_x = (1 - s, f)
    partners = (d_zh, d_zl, d_y, d_c)

    frames = lax.axis_size("frames")
    has_next, has_prev = f < frames - 1, f > 0
    d_next, d_prev = (s, f + 1), (s, f - 1)

    tokext = n2t
    tok_copy = pltpu.make_async_copy(tok_hbm, tokext.at[16:1040], tok_sem)
    fetches = [
        pltpu.make_async_copy(src, dst, in_sem.at[i])
        for i, (src, dst) in enumerate(
            ((down_hbm, down_own), (gate_hbm, gate_own), (up_hbm, up_own), (cot_hbm, cot))
        )
    ]
    for cp in fetches:
        cp.start()
    tok_copy.start()

    barrier = pltpu.get_barrier_semaphore()

    def greet(device):
        pl.semaphore_signal(barrier, inc=1, device_id=device, device_id_type=MESH)

    for device in partners + (d_x,):
        greet(device)
    pl.when(has_next)(lambda: greet(d_next))
    pl.when(has_prev)(lambda: greet(d_prev))

    w_own[0, 0:32, 0:512] = ctx_own[:, 0:512]
    w_own[0, 32:64, 0:512] = ctx_own[:, 512:1024]
    w_own[0, :, 512:768] = out_own[:, 768:1024]
    w_own[5] = out_own[:, 0:768]
    for g in range(4):
        for part_id in range(3):
            at = part_id * 1024 + g * 256
            w_own[1 + g, :, part_id * 256 : part_id * 256 + 256] = qkv_own[:, at : at + 256]

    def own_copy(low, high, i):
        return pltpu.make_async_copy(
            w_own.at[low:high], gathered.at[low:high, zh, zl, y, c], own_sem.at[i]
        )

    own_copy(0, 6, 0).start()

    pl.semaphore_wait(barrier, 5 + has_next.astype(jnp.int32) + has_prev.astype(jnp.int32))

    def remote(src, dst, ss, rs, device):
        return pltpu.make_async_remote_copy(
            src_ref=src, dst_ref=dst, send_sem=ss, recv_sem=rs, device_id=device, device_id_type=MESH
        )

    def ag_copies(stage, k, split):
        low, high = (slice(*rows) for rows in split)
        if stage == 0:
            triples = [(w_own.at[k], gathered.at[k, zh, zl, y, c], d_zh)]
        elif stage == 1:
            near, side = gathered.at[k, :, zl, y, c, low], gathered.at[k, :, zl, y, c, high]
            triples = [(near, near, d_zl), (side, side, d_y)]
        elif stage == 2:
            side, near = gathered.at[k, :, :, y, c, low], gathered.at[k, :, zl, :, c, high]
            triples = [(side, side, d_y), (near, near, d_zl)]
        else:
            own = gathered.at[k, :, :, :, c]
            triples = [(own, own, d_c)]
        first = (0, 1, 3, 5)[stage]
        return [
            remote(src, dst, ag_ss.at[first + i, k], ag_rs.at[first + i, k], device)
            for i, (src, dst, device) in enumerate(triples)
        ]

    def choose(k, bound, under, above, fn):
        if isinstance(k, int):
            fn(under if k < bound else above)
        else:
            pl.when(k < bound)(lambda: fn(under))
            pl.when(k >= bound)(lambda: fn(above))

    def ag_do(act, stage, k):
        if stage in (0, 3):
            act(ag_copies(stage, k, SPLIT))
        else:
            choose(k, GATHER_HALVES, SPLIT, HALVES, lambda split: act(ag_copies(stage, k, split)))

    def by_split(r, fn):
        choose(r, REDUCE_HALVES, SPLIT, HALVES, fn)

    def start_all(copies):
        for cp in copies:
            cp.start()

    def wait_recv_all(copies):
        for cp in copies:
            cp.wait_recv()

    def wait_send_all(copies):
        for cp in copies:
            cp.wait_send()

    class load_copy:
        def __init__(self, k, slot):
            self.parts = [
                pltpu.make_async_copy(
                    gathered.at[k, i // 2, i % 2], wbuf.at[slot, i // 2, i % 2], load_sem.at[slot, i]
                )
                for i in range(4)
            ]

        def start(self):
            for cp in self.parts:
                cp.start()

        def wait(self):
            for cp in self.parts:
                cp.wait()

    def ag_step(stage, k):
        def go():
            if stage > 0:
                ag_do(wait_recv_all, stage - 1, k)
            ag_do(start_all, stage, k)
        either(within(k, 0, CHUNKS), go)

    def ag_tick(t, gap=1):
        for stage in range(3):
            ag_step(stage, t - gap * stage)

    def ag_ready(k):
        def ready():
            ag_do(wait_recv_all, 3, k)
            load_copy(k, k % 2).start()
        either(within(k, 0, CHUNKS), ready)

    def rs_copies(stage, r, split):
        two, slot = r % (2 if stage == 0 else 3), r % (FAR_ROUNDS if stage == 3 else ROUNDS)
        if stage == 0:
            triples = [(pend.at[r, :, :, :, 1 - c], r_c.at[two], d_c)]
        elif stage == 3:
            triples = [(v_send.at[two], r_zh.at[slot], d_zh)]
        else:
            src, dst = ((t_send, r_y), (u_send, r_zl))[stage - 1]
            devices = ((d_y, d_zl), (d_zl, d_y))[stage - 1]
            triples = [
                (src.at[two, :, low:high], dst.at[slot, :, low:high], device)
                for (low, high), device in zip(split, devices)
            ]
        first = (0, 1, 3, 5)[stage]
        return [
            remote(src, dst, rs_ss.at[first + i, two], rs_rs.at[first + i, slot], device)
            for i, (src, dst, device) in enumerate(triples)
        ]

    def rs_do(act, stage, r):
        if stage in (0, 3):
            act(rs_copies(stage, r, SPLIT))
        else:
            by_split(r, lambda split: act(rs_copies(stage, r, split)))

    def add(a, b):
        return a.astype(jnp.float32) + b.astype(jnp.float32)

    def place_result(k, res):
        if not isinstance(k, int):
            @pl.when(k < FEED)
            def _():
                fin[k] = res
            pl.when(k == FEED)(lambda: place_result(FEED, res))
            return
        if k < FEED:
            fin[k] = res
        elif k == FEED:
            aft[384:448, 0:768] = res
        elif k < CHUNKS - 1:
            g = k - FEED - 1
            for p in range(3):
                aft[192 + 64 * p : 256 + 64 * p, g * 256 : g * 256 + 256] = res[:, p * 256 : p * 256 + 256]
        else:
            aft[384:448, 768:1024] = res[:, 512:768]
            aft[448:480, 0:512] = res[0:32, 0:512]
            aft[448:480, 512:1024] = res[32:64, 0:512]

    def out_copies():
        pairs = [(aft.at[384:448], dout_hbm), (aft.at[448:480], dctxw_hbm)]
        for p in range(3):
            pairs.append((aft.at[192 + 64 * p : 256 + 64 * p], dqkv_hbm.at[:, p * 1024 : p * 1024 + 1024]))
        return pairs

    def feed_copies():
        pairs = [(aft.at[512:688], ddown_hbm)]
        for i, hbm in enumerate((dgate_hbm, dup_hbm)):
            at = i * 768
            if i == 1:
                at = 704
            for p in range(3):
                n = 1024 if p < 2 else 768
                pairs.append((aft.at[at + 64 * p : at + 64 * p + 64, 0:n], hbm.at[:, p * 1024 : p * 1024 + n]))
        return pairs

    def out_copy(pair, i):
        return pltpu.make_async_copy(pair[0], pair[1], out_sem.at[i])

    def unpack_feed():
        for j in range(FEED):
            for q in range(4):
                aft[512 + j * 16 : 528 + j * 16, q * 256 : q * 256 + 256] = fin[j, q * 16 : q * 16 + 16, 512:768]
        for i, at in enumerate((0, 704)):
            cols = [
                fin[j, :, i * 256 + d * 16 : i * 256 + d * 16 + 16] for d in range(16) for j in range(FEED)
            ]
            for p in range(22):
                piece = jnp.concatenate(cols[p * 8 : p * 8 + 8], axis=1)
                row, col = at + 64 * (p // 8), (p % 8) * 128
                aft[row : row + 64, col : col + 128] = piece

    def pend_copy(r):
        return pltpu.make_async_copy(part.at[r % 2], pend.at[r], pend_sem.at[r % 2])

    def half_copy(r):
        return pltpu.make_async_copy(pend.at[r, :, :, :, c], part_own.at[r % 2], half_sem.at[r % 2])

    def part_done(r):
        either(within(r, 1, CHUNKS), lambda: pend_copy(r - 1).wait())
        pend_copy(r).start()

    def send_half(r):
        either(within(r, 2, CHUNKS), lambda: rs_do(wait_send_all, 0, r - 2))
        rs_do(start_all, 0, r)
        half_copy(r).start()

    def rs_tick(r):
        def stage_y():
            k = r - 1
            rs_do(wait_recv_all, 0, k)
            half_copy(k).wait()
            either(within(k, 3, CHUNKS), lambda: rs_do(wait_send_all, 1, k - 3))
            two, three = k % 2, k % 3

            def pieces(split):
                def piece(i, _):
                    a, b = i // 2, i % 2
                    for (low, high), send, keep in zip(split, ((b, 1 - y), (1 - zl, b)), ((b, y), (zl, b))):
                        for out, (m, n) in ((t_send, send), (t_keep, keep)):
                            out[three, i, low:high] = part_own[two, a, m, n, low:high] + r_c[two, a, m, n, low:high]
                    return 0

                lax.fori_loop(0, 4, piece, 0)

            by_split(k, pieces)
            rs_do(start_all, 1, k)
        either(within(r, 1, CHUNKS + 1), stage_y)
        either(within(r, 0, CHUNKS), lambda: send_half(r))

        def stage_zl():
            k = r - 3
            rs_do(wait_recv_all, 1, k)
            either(within(k, 3, CHUNKS), lambda: rs_do(wait_send_all, 2, k - 3))
            three, slot = k % 3, k % ROUNDS

            def pieces(split):
                for a in range(2):
                    for (low, high), mine in zip(split, (zl, y)):
                        for out, at in ((u_send, a * 2 + 1 - mine), (u_keep, a * 2 + mine)):
                            out[three, a, low:high] = t_keep[three, at, low:high] + r_y[slot, at, low:high]

            by_split(k, pieces)
            rs_do(start_all, 2, k)
        either(within(r, 3, CHUNKS + 3), stage_zl)

        def stage_zh():
            k = r - 5
            rs_do(wait_recv_all, 2, k)
            either(within(k, 3, CHUNKS), lambda: rs_do(wait_send_all, 3, k - 3))
            three, slot = k % 3, k % ROUNDS
            v_send[three] = u_keep[three, 1 - zh] + r_zl[slot, 1 - zh]
            v_keep[three] = u_keep[three, zh] + r_zl[slot, zh]
            rs_do(start_all, 3, k)
        either(within(r, 5, CHUNKS + 5), stage_zh)

        def last():
            k = r - 7
            rs_do(wait_recv_all, 3, k)
            place_result(k, add(v_keep[k % 3], r_zh[k % FAR_ROUNDS]))
        either(within(r, 7, CHUNKS + 7), last)

    rim_copy = remote(tok_hbm.at[1008:1024], tokext.at[0:16], rim_ss.at[0], rim_rs.at[0], d_next)
    halo_copy = remote(oacc.at[0:16], oacc.at[1024:1040], rim_ss.at[1], rim_rs.at[1], d_prev)
    pl.when(has_next)(lambda: rim_copy.start())

    @pl.when(jnp.logical_not(has_prev))
    def _():
        tokext[0:16, :] = jnp.zeros((16, 1024), jnp.bfloat16)

    @pl.when(jnp.logical_not(has_next))
    def _():
        oacc[1024:1040, :] = jnp.zeros((16, 1024), jnp.float32)

    gacc[...] = jnp.zeros_like(gacc)

    place = lax.broadcasted_iota(jnp.int32, (16, 8, 1), 1)
    wait = jnp.zeros((16, 8, 1), jnp.int32)
    for p in range(8):
        wait = jnp.where(place == p, delay[p], wait)

    def starts_at(frame):
        start = jnp.int32(0)
        hit = frame == start
        for i in range(lengths.shape[0] - 1):
            start = start + lengths[i]
            hit = jnp.logical_or(hit, frame == start)
        return hit

    def same_item(frame, j):
        ok = jnp.logical_not(starts_at(frame))
        if j == 2:
            ok = jnp.logical_and(ok, jnp.logical_not(starts_at(frame - 1)))
        return ok

    def frame_of(i):
        return f * 128 + i * 16 + lax.broadcasted_iota(jnp.int32, (16, 8, 1), 0)

    def pack_feed(own, at):
        for j in range(FEED):
            cols = [own[:, d * 176 + j * 16 : d * 176 + j * 16 + 16] for d in range(16)]
            w_own[6 + j, :, at : at + 256] = jnp.concatenate(cols, axis=1)

    ag_tick(0)
    own_copy(0, 6, 0).wait()
    ag_tick(1)
    for cp in fetches[:2]:
        cp.wait()
    for j in range(FEED):
        for q in range(4):
            w_own[6 + j, q * 16 : q * 16 + 16, 512:768] = down_own[
                j * 16 : j * 16 + 16, q * 256 : q * 256 + 256
            ]
    pack_feed(gate_own, 0)
    ag_tick(2)
    fetches[2].wait()
    pack_feed(up_own, 256)
    own_copy(6, CHUNKS, 1).start()
    ag_tick(3)
    ag_step(3, 0)
    ag_ready(0)
    own_copy(6, CHUNKS, 1).wait()
    ag_tick(4)

    load_copy(0, 0).wait()
    wtail[...] = wbuf[0, :, :, :, :, :, 512:768].reshape(1024, 256)
    half = shift.shape[1] // 2
    for h in range(2):
        w_half = wbuf[0, :, :, :, :, h * 32 : h * 32 + 32, 0:512].reshape(512, 512)
        shift[:, h * half : (h + 1) * half] = mm(ctx[...], w_half)
    xsend[0] = shift[...].astype(jnp.bfloat16)

    x_copy = remote(xsend.at[0], xrecv.at[0], x_ss.at[0], x_rs.at[0], d_x)
    x_copy.start()
    ag_tick(5)
    for k in (6, 7, 8):
        ag_step(0, k)
    ag_step(3, 1)
    ag_ready(1)
    x_copy.wait_recv()
    shift[...] = shift[...] + xrecv[0].astype(jnp.float32)

    def rows_of(i, size):
        return pl.ds(pl.multiple_of(i * size, size), size)

    def norm1(i, _):
        rows = rows_of(i, 128)
        sh = shift[rows_of(i, 16), :]
        near = tokext[pl.ds(pl.multiple_of(i * 128, 128), 144), :].astype(jnp.float32)
        frame = frame_of(i)
        x = jnp.zeros((16, 8, 1024), jnp.float32)
        for j in range(3):
            keep = wait == j
            if j > 0:
                keep = jnp.logical_and(keep, same_item(frame, j))
            piece = near[16 - 8 * j : 144 - 8 * j].reshape(16, 8, 1024)
            x = jnp.where(keep, piece, x)
        x = x + sh[:, None, :]
        r = lax.rsqrt(jnp.mean(x * x, axis=-1, keepdims=True) + epsilon)
        n = (x * r * gain_one[...].astype(jnp.float32)[None]).reshape(128, 1024).astype(jnp.bfloat16)
        lin[rows, :] = x.reshape(128, 1024)
        n1[rows, :] = n
        n1t[:, rows] = n.T
        return 0

    tok_copy.wait()
    pl.when(has_prev)(lambda: rim_copy.wait_recv())
    lax.fori_loop(0, 4, norm1, 0)
    ag_step(1, 5)
    ag_step(2, 4)
    lax.fori_loop(4, 8, norm1, 0)
    ag_step(1, 6)

    lane_low = lax.broadcasted_iota(jnp.int32, (128, 128), 1) < 64
    head_scale = HEAD ** (-0.5)

    def both(v):
        zero = jnp.zeros_like(v)
        return jnp.concatenate([jnp.where(lane_low, v, zero), jnp.where(lane_low, zero, v)], axis=0)

    own_frame = [
        lax.broadcasted_iota(jnp.int32, (8, 128), 1) // 8 == fr for fr in range(16)
    ]
    key_seen = lax.broadcasted_iota(jnp.int32, (8, 128), 0) <= lax.broadcasted_iota(jnp.int32, (8, 128), 1) % 8

    def compact(full, h):
        out = full[h * 128 : h * 128 + 8]
        for fr in range(1, 16):
            at = h * 128 + fr * 8
            out = jnp.where(own_frame[fr], full[at : at + 8], out)
        return out

    def spread(pair):
        zero = jnp.zeros((8, 128), jnp.float32)
        rows = [jnp.where(own_frame[fr], x, zero) for x in pair for fr in range(16)]
        return jnp.concatenate(rows, axis=0).astype(jnp.bfloat16)

    def probabilities(q, kk):
        full = nt(kk, q)
        pair = []
        for h in range(2):
            sc = jnp.where(key_seen, compact(full, h) * head_scale, -1e30)
            e = jnp.exp(sc - jnp.max(sc, axis=0, keepdims=True))
            pair.append(e / jnp.sum(e, axis=0, keepdims=True))
        return pair

    def pair_of(g, sub, lo):
        return [qkv[g, sub, at + lo : at + lo + 128] for at in (0, 256, 512)]

    def attn_fwd(g):
        def rows_step(i, _):
            for u in range(4):
                sub = rows_of(i * 4 + u, 128)
                for lo in (0, 128):
                    q, k, v = pair_of(g, sub, lo)
                    pr = spread(probabilities(q, both(k)))
                    out = tn(pr, both(v)).astype(jnp.bfloat16)
                    mixed[sub, pl.ds(pl.multiple_of(g * 256 + lo, 128), 128)] = out
            return 0
        lax.fori_loop(0, 2, rows_step, 0)

    def attn_bwd(g):
        def rows_step(i, _):
            for u in range(4):
                sub = rows_of(i * 4 + u, 128)
                for lo in (0, 128):
                    q, k, v = pair_of(g, sub, lo)
                    do = mixed[sub, pl.ds(pl.multiple_of(g * 256 + lo, 128), 128)]
                    kk = both(k)
                    pr = probabilities(q, kk)
                    full = nt(both(v), do)
                    ds = []
                    for h in range(2):
                        d = compact(full, h)
                        ds.append(pr[h] * (d - jnp.sum(d * pr[h], axis=0, keepdims=True)))
                    ds = spread(ds)
                    dq = tn(ds, kk) * head_scale
                    dk = mm(ds, q)
                    dv = mm(spread(pr), do)
                    qkv[g, sub, lo : lo + 128] = dq.astype(jnp.bfloat16)
                    qkv[g, sub, 256 + lo : 384 + lo] = (
                        jnp.where(lane_low, dk[:128], dk[128:]) * head_scale
                    ).astype(jnp.bfloat16)
                    qkv[g, sub, 512 + lo : 640 + lo] = jnp.where(lane_low, dv[:128], dv[128:]).astype(jnp.bfloat16)
            return 0
        lax.fori_loop(0, 2, rows_step, 0)

    def qkv_group(g, _):
        slot = (1 + g) % 2
        load_copy(1 + g, slot).wait()

        def rows_step(i, _):
            rows = rows_of(i, 256)
            qkv[g, rows, :] = mm(n1[rows, :], wbuf[slot].reshape(1024, WIDE)).astype(jnp.bfloat16)
            return 0

        lax.fori_loop(0, 4, rows_step, 0)
        ag_step(3, 2 + g)
        ag_tick(9 + g, 2)
        attn_fwd(g)
        ag_ready(2 + g)
        return 0

    lax.fori_loop(0, 4, qkv_group, 0)

    load_copy(5, 1).wait()

    def after(i, _):
        rows = rows_of(i, 256)
        m = mixed[rows, :]
        a = lin[rows, 0:WIDE] + mm(m, wbuf[1].reshape(1024, WIDE))
        b = lin[rows, WIDE:1024] + mm(m, wtail[...])
        x = jnp.concatenate([a, b], axis=1)
        aft[rows, :] = x
        oacc[rows, :] = x
        gn[rows, :] = jnp.zeros((256, 1024), jnp.float32)
        x3 = x.reshape(32, 8, 1024)
        r = lax.rsqrt(jnp.mean(x3 * x3, axis=-1, keepdims=True) + epsilon)
        n = (x3 * r * gain_two[...].astype(jnp.float32)[None]).reshape(256, 1024).astype(jnp.bfloat16)
        n2[rows, :] = n
        n2t[0:1024, rows] = n.T
        return 0

    lax.fori_loop(0, 2, after, 0)
    ag_step(3, 6)
    ag_tick(13, 2)
    lax.fori_loop(2, 4, after, 0)
    ag_ready(6)
    fetches[3].wait()

    def feed(j, _):
        slot = j % 2
        load_copy(6 + j, slot).wait()
        two = j % 2

        def rows_step(i):
            rows = slice(i * 512, i * 512 + 512)
            w_gu = wbuf[slot, :, :, :, :, :, 0:512].reshape(1024, 512)
            pre = mm(n2[rows, :], w_gu)
            gate, up = pre[:, :256], pre[:, 256:]
            g_hid = jnp.zeros((512, 256), jnp.float32)
            for q in range(4):
                w_q = wbuf[slot, :, :, :, :, q * 16 : q * 16 + 16, 512:768].reshape(256, 256)
                g_hid = g_hid + nt(cot[rows, q * 256 : q * 256 + 256], w_q)
            sig = jax.nn.sigmoid(gate)
            silu = gate * sig
            hid = (silu * up).astype(jnp.bfloat16)
            g_gate = (g_hid * up * sig * (1.0 + gate * (1.0 - sig))).astype(jnp.bfloat16)
            g_up = (g_hid * silu).astype(jnp.bfloat16)
            for q in range(4):
                w_q = wbuf[slot, :, :, :, :, q * 16 : q * 16 + 16, 512:768].reshape(256, 256)
                oacc[rows, q * 256 : q * 256 + 256] += mm(hid, w_q)
            both_g = jnp.concatenate([g_gate, g_up], axis=1)
            n1[rows, 0:512] = both_g
            hidt[:, rows] = hid.T
            back = nt(both_g, w_gu)
            gn[rows, :] += back

        for i in range(2):
            rows_step(i)
        ag_step(3, 7 + j)
        ag_tick(14 + j, 2)

        def weight_step(m, _):
            res = mm(n2t[rows_of(m, 512), :], n1[:, 0:512]).astype(jnp.bfloat16).reshape(2, 2, 2, 64, 512)
            part[two, m, :, :, :, :, 0:512] = res
            return 0

        lax.fori_loop(0, 2, weight_step, 0)
        ag_ready(7 + j)
        for q in range(4):
            res = mm(hidt[...], cot[:, q * 256 : q * 256 + 256]).astype(jnp.bfloat16)
            part[two, :, :, :, :, q * 16 : q * 16 + 16, 512:768] = res.reshape(2, 2, 2, 2, 16, 256)
        part_done(j)
        pl.when(jnp.logical_and(j % 2 == 1, j < 6))(lambda: rs_tick(j // 2))
        pl.when(j >= 6)(lambda: rs_tick(j - 3))
        return 0

    lax.fori_loop(0, FEED, feed, 0)
    load_copy(5, 1).start()
    load_copy(1, 0).start()

    def norm2_back(i, _):
        rows = rows_of(i, 128)
        n2t[rows, :] = oacc[rows, :].astype(jnp.bfloat16)
        n1[:, rows] = mixed[rows, :].T
        x = aft[rows, :].reshape(16, 8, 1024)
        g = gn[rows, :].reshape(16, 8, 1024)
        gn[rows, :] = jnp.zeros((128, 1024), jnp.float32)
        r = lax.rsqrt(jnp.mean(x * x, axis=-1, keepdims=True) + epsilon)
        unit = x * r
        gacc[8:16, :] += jnp.sum(g * unit, axis=0)
        gu = g * gain_two[...].astype(jnp.float32)[None]
        back = r * (gu - unit * jnp.mean(gu * unit, axis=-1, keepdims=True))
        total = cot[rows, :].astype(jnp.float32) + back.reshape(128, 1024)
        oacc[rows, :] = total
        n2[rows, :] = total.astype(jnp.bfloat16)
        return 0

    lax.fori_loop(0, 8, norm2_back, 0)
    mixed_copy = pltpu.make_async_copy(n2t.at[0:1024], mixed_hbm, out_sem.at[0])
    mixed_copy.start()
    rs_tick(8)


    def out_weight_step(m, _):
        res = mm(n1[rows_of(m, 256), :], n2[:, 0:WIDE]).astype(jnp.bfloat16)
        part[1, m // 2, m % 2] = res.reshape(2, 2, 64, WIDE)
        return 0

    lax.fori_loop(0, 4, out_weight_step, 0)
    part_done(11)

    def mixed_back(i, _):
        rows = rows_of(i, 256)
        g = n2[rows, :]
        res = nt(g[:, 0:WIDE], wbuf[1].reshape(1024, WIDE)) + nt(g[:, WIDE:1024], wtail[...])
        mixed[rows, :] = res.astype(jnp.bfloat16)
        return 0

    load_copy(5, 1).wait()
    lax.fori_loop(0, 4, mixed_back, 0)
    load_copy(2, 1).start()
    rs_tick(9)

    def qkv_back(g, _):
        slot = g % 2
        attn_bwd(g)
        pend_copy(11 + g).wait()
        rs_tick(10 + g + g // 2)
        two = g % 2

        def weight_step(m, _):
            res = mm(n1t[rows_of(m, 256), :], qkv[g]).astype(jnp.bfloat16)
            part[two, m // 2, m % 2] = res.reshape(2, 2, 64, WIDE)
            return 0

        lax.fori_loop(0, 4, weight_step, 0)
        pend_copy(12 + g).start()

        def rows_step(i, _):
            rows = rows_of(i, 256)
            back = nt(qkv[g, rows, :], wbuf[slot].reshape(1024, WIDE))
            gn[rows, :] += back
            return 0

        load_copy(1 + g, slot).wait()
        lax.fori_loop(0, 4, rows_step, 0)
        pl.when(g == 1)(lambda: rs_tick(12))
        pl.when(g < 2)(lambda: load_copy(3 + g, slot).start())
        pl.when(g == 2)(lambda: load_copy(0, 0).start())
        return 0

    lax.fori_loop(0, 4, qkv_back, 0)

    def norm1_back(i, _):
        rows = rows_of(i, 128)
        x = lin[rows, :].reshape(16, 8, 1024)
        g = gn[rows, :].reshape(16, 8, 1024)
        r = lax.rsqrt(jnp.mean(x * x, axis=-1, keepdims=True) + epsilon)
        unit = x * r
        gacc[0:8, :] += jnp.sum(g * unit, axis=0)
        gu = g * gain_one[...].astype(jnp.float32)[None]
        back = r * (gu - unit * jnp.mean(gu * unit, axis=-1, keepdims=True))
        total = oacc[rows, :].reshape(16, 8, 1024) + back
        oacc[rows, :] = total.reshape(128, 1024)
        few = rows_of(i, 16)
        g_frame = jnp.sum(total, axis=1)
        shift[few, :] = g_frame
        xsend[1, few, :] = g_frame.astype(jnp.bfloat16)
        x_piece(i).start()
        return 0

    def x_piece(i):
        few = rows_of(i, 16)
        return remote(xsend.at[1, few], xrecv.at[1, few], x_ss.at[1 + i], x_rs.at[1 + i], d_x)

    lax.fori_loop(0, 8, norm1_back, 0)
    pl.when(has_prev)(lambda: halo_copy.start())
    def gain_copy(i):
        return remote(gsend.at[i], grecv.at[i], g_ss.at[i], g_rs.at[i], partners[i])

    gsend[0] = gacc[...]
    gain_copy(0).start()

    pend_copy(15).wait()
    rs_tick(15)
    load_copy(0, 0).wait()

    def out_tail_step(m, _):
        res = mm(n1[rows_of(m, 256), :], n2[:, WIDE:1024]).astype(jnp.bfloat16)
        part[0, m // 2, m % 2, :, :, :, 512:768] = res.reshape(2, 2, 64, 256)
        return 0

    lax.fori_loop(0, 4, out_tail_step, 0)

    for i in range(8):
        x_piece(i).wait_recv()
    g_low = (shift[...] + xrecv[1].astype(jnp.float32)).astype(jnp.bfloat16)
    ctx_t = ctx[...].T
    for h in range(2):
        gh = g_low[:, h * 512 : (h + 1) * 512]
        res = mm(ctx_t, gh).astype(jnp.bfloat16).reshape(2, 2, 2, 2, 32, 512)
        part[0, :, :, :, :, h * 32 : h * 32 + 32, 0:512] = res
    pend_copy(16).start()
    pend_copy(16).wait()
    w0 = wbuf[0, :, :, :, :, 0:32, 0:512].reshape(512, 512)
    w1 = wbuf[0, :, :, :, :, 32:64, 0:512].reshape(512, 512)
    dctx[...] = nt(g_low[:, :512], w0) + nt(g_low[:, 512:], w1)

    def dtok(i, _):
        rows = rows_of(i, 128)
        near = oacc[pl.ds(pl.multiple_of(i * 128, 128), 144), :]
        frame = frame_of(i)
        x = jnp.zeros((16, 8, 1024), jnp.float32)
        for j in range(3):
            keep = wait == j
            if j > 0:
                keep = jnp.logical_and(keep, same_item(frame + j, j))
            x = jnp.where(keep, near[8 * j : 128 + 8 * j].reshape(16, 8, 1024), x)
        gn[rows, :] = x.reshape(128, 1024)
        return 0

    rs_tick(16)
    dtok_copy = pltpu.make_async_copy(gn, dtok_hbm, out_sem.at[1])
    last_out = [out_copy(pair, 9 + i) for i, pair in enumerate(out_copies())]
    feed_out = [out_copy(pair, 2 + i) for i, pair in enumerate(feed_copies())]
    for i in range(4):
        gain_copy(i).wait_recv()
        if i < 3:
            gsend[i + 1] = gsend[i] + grecv[i]
            gain_copy(i + 1).start()
        else:
            total = gsend[i] + grecv[i]
            dgain_one[...] = total[0:8]
            dgain_two[...] = total[8:16]
        rs_tick(17 + i)
        if i == 0:
            unpack_feed()
            for cp in feed_out:
                cp.start()
            pl.when(has_next)(lambda: halo_copy.wait_recv())
            lax.fori_loop(0, 8, dtok, 0)
            dtok_copy.start()

    rs_tick(21)
    rs_tick(22)
    for cp in last_out[2:]:
        cp.start()
    rs_tick(23)

    for cp in last_out[:2]:
        cp.start()
    pl.when(has_next)(lambda: rim_copy.wait_send())
    pl.when(has_prev)(lambda: halo_copy.wait_send())

    for i in range(4):
        gain_copy(i).wait_send()
    x_copy.wait_send()
    for i in range(8):
        x_piece(i).wait_send()

    for stage in range(4):
        for k in range(CHUNKS - (2 if stage == 0 else 3), CHUNKS):
            rs_do(wait_send_all, stage, k)

    def drain(k, _):
        for stage in range(4):
            ag_do(wait_send_all, stage, k)
        return 0

    lax.fori_loop(0, CHUNKS, drain, 0)
    mixed_copy.wait()
    dtok_copy.wait()
    for cp in feed_out + last_out:
        cp.wait()


def call_layer(tok, ctx, gain_one, gain_two, cot, weights, delay, lengths):
    f32, bf16 = jnp.float32, jnp.bfloat16
    vm, dma = pltpu.VMEM, pltpu.SemaphoreType.DMA
    shape = jax.ShapeDtypeStruct
    in_vmem, in_hbm, in_smem = (pl.BlockSpec(memory_space=m) for m in (pltpu.VMEM, pltpu.HBM, pltpu.SMEM))
    return pl.pallas_call(
        layer_kernel,
        name="layer",
        out_shape=(
            shape((1024, 1024), bf16),
            shape((1024, 1024), f32),
            shape((128, 512), f32),
            shape((32, 1024), f32),
            shape((8, 1024), f32),
            shape((8, 1024), f32),
            shape((64, 3072), f32),
            shape((64, 1024), f32),
            shape((64, 2816), f32),
            shape((64, 2816), f32),
            shape((176, 1024), f32),
            shape((CHUNKS, 2, 2, 2, 2, 64, WIDE), bf16),
            shape((CHUNKS, 2, 2, 2, 2, 64, WIDE), bf16),
        ),
        in_specs=[in_hbm] + [in_vmem] * 3 + [in_hbm] + [in_vmem] * 3 + [in_hbm] * 3 + [in_smem] * 2,
        out_specs=(in_hbm, in_hbm, in_vmem, in_hbm, in_vmem, in_vmem) + (in_hbm,) * 7,
        scratch_shapes=[
            vm((1024, 1024), bf16),
            vm((64, 2816), bf16),
            vm((64, 2816), bf16),
            vm((176, 1024), bf16),
            vm((CHUNKS, 64, WIDE), bf16),
            vm((1024, 1024), f32),
            vm((1024, 1024), bf16),
            vm((1024, 1024), bf16),
            vm((4, 1024, WIDE), bf16),
            vm((1024, 1024), bf16),
            vm((1024, 1024), f32),
            vm((1024, 1024), bf16),
            vm((1040, 1024), bf16),
            vm((1040, 1024), f32),
            vm((1024, 1024), f32),
            vm((2, 2, 2, 2, 2, 64, WIDE), bf16),
            vm((1024, 256), bf16),
            vm((2, 2, 2, 2, 2, 64, WIDE), bf16),
            vm((2, 2, 2, 2, 64, WIDE), bf16),
            vm((256, 1024), bf16),
            vm((128, 1024), f32),
            vm((16, 1024), f32),
            vm((4, 16, 1024), f32),
            vm((4, 16, 1024), f32),
            vm((2, 128, 1024), bf16),
            vm((2, 128, 1024), bf16),
            vm((2, 2, 2, 2, 64, WIDE), bf16),
            vm((ROUNDS, 4, 64, WIDE), bf16),
            vm((ROUNDS, 2, 64, WIDE), bf16),
            vm((FAR_ROUNDS, 64, WIDE), bf16),
            vm((3, 4, 64, WIDE), bf16),
            vm((3, 4, 64, WIDE), bf16),
            vm((3, 2, 64, WIDE), bf16),
            vm((3, 2, 64, WIDE), bf16),
            vm((3, 64, WIDE), bf16),
            vm((3, 64, WIDE), bf16),
            vm((FEED, 64, WIDE), f32),
            dma((6, CHUNKS)),
            dma((6, CHUNKS)),
            dma((6, 3)),
            dma((6, FAR_ROUNDS)),
            dma((9,)),
            dma((9,)),
            dma((4,)),
            dma((4,)),
            dma((2,)),
            dma((2, 4)),
            dma((2,)),
            dma((2,)),
            dma,
            dma((4,)),
            dma((2,)),
            dma((2,)),
            dma((14,)),
        ],
        compiler_params=pltpu.CompilerParams(
            collective_id=0, has_side_effects=True, vmem_limit_bytes=63 * 1024 * 1024
        ),
    )(tok, ctx, gain_one, gain_two, cot, *weights, delay, lengths)


def copy_kernel(*refs):
    n = (len(refs) - 2) // 3
    srcs, dsts, held, in_sem, out_sem = refs[:n], refs[n : 2 * n], refs[2 * n : 3 * n], refs[-2], refs[-1]
    ins = [pltpu.make_async_copy(srcs[i], held[i], in_sem.at[i]) for i in range(n)]
    outs = [pltpu.make_async_copy(held[i], dsts[i], out_sem.at[i]) for i in range(n)]
    for cp in ins:
        cp.start()
    for cp_in, cp_out in zip(ins, outs):
        cp_in.wait()
        cp_out.start()
    for cp in outs:
        cp.wait()


def copy_all(arrays):
    n = len(arrays)
    hbm = pl.BlockSpec(memory_space=pltpu.HBM)
    return pl.pallas_call(
        copy_kernel,
        name="outputs",
        out_shape=tuple(jax.ShapeDtypeStruct(a.shape, a.dtype) for a in arrays),
        in_specs=[hbm] * n,
        out_specs=(hbm,) * n,
        scratch_shapes=[pltpu.VMEM(a.shape, a.dtype) for a in arrays]
        + [pltpu.SemaphoreType.DMA((n,)), pltpu.SemaphoreType.DMA((n,))],
        compiler_params=pltpu.CompilerParams(vmem_limit_bytes=63 * 1024 * 1024),
    )(*arrays)


def body_kernel(
    tokens,
    context,
    ctx_weight,
    delay,
    lengths,
    attn_gain,
    ffn_gain,
    qkv_weight,
    out_weight,
    gate_weight,
    up_weight,
    down_weight,
    cotangent,
):
    frame_count, positions, width = tokens.shape[1:]
    rows = frame_count * positions
    weights = (ctx_weight, qkv_weight[0], out_weight[0], gate_weight[0], up_weight[0], down_weight[0])
    mixed_out, d_tokens, d_context, d_ctx, d_gain_one, d_gain_two, *grads = call_layer(
        tokens.reshape(rows, width),
        context,
        attn_gain[0],
        ffn_gain[0],
        cotangent.reshape(rows, width),
        weights,
        delay,
        lengths,
    )
    mixed_out, d_tokens, d_context, d_ctx, d_gain_one, d_gain_two, *grads = copy_all(
        (mixed_out, d_tokens, d_context, d_ctx, d_gain_one, d_gain_two, *grads[:-2])
    )
    d_qkv, d_out, d_gate, d_up, d_down = grads
    return (
        mixed_out.reshape(tokens.shape),
        d_tokens.reshape(tokens.shape),
        d_context,
        d_ctx,
        d_gain_one[None],
        d_gain_two[None],
        d_qkv[None],
        d_out[None],
        d_gate[None],
        d_up[None],
        d_down[None],
    )


def body(
    tokens,
    context,
    ctx_weight,
    delay,
    lengths,
    attn_gain,
    ffn_gain,
    qkv_weight,
    out_weight,
    gate_weight,
    up_weight,
    down_weight,
    cotangent,
):
    frame_count = tokens.shape[1]
    positions = tokens.shape[2]
    model_width = tokens.shape[3]
    token_rows = frame_count * positions
    head_scale = HEAD ** (-0.5)
    ctx_full = lax.all_gather(context, "stream", axis=1, tiled=True)
    ctx_rows = lax.all_gather(ctx_weight, ("stream", "frames"), axis=0, tiled=True)
    shift_term = flat_dot(ctx_full, ctx_rows)
    inputs = tokens[0]
    rim_rows = shifted(inputs[frame_count - 2 :], "frames", 1)
    extended = jnp.concatenate([rim_rows, inputs], axis=0).astype(jnp.float32)
    frame_ids = lax.axis_index("frames") * frame_count + jnp.arange(frame_count, dtype=jnp.int32)
    chosen, valid_rows = shift_tables(delay, lengths, frame_ids)
    layer_in = jnp.broadcast_to(shift_term[:, None, :], (frame_count, positions, model_width))
    for offset in range(3):
        piece = extended[2 - offset : 2 - offset + frame_count]
        layer_in = (
            layer_in + chosen[offset][None, :, None] * valid_rows[offset][:, None, None] * piece
        )
    weights = (
        lax.all_gather(qkv_weight[0], "frames", axis=0, tiled=True),
        lax.all_gather(out_weight[0], "frames", axis=0, tiled=True),
        lax.all_gather(gate_weight[0], "frames", axis=0, tiled=True),
        lax.all_gather(up_weight[0], "frames", axis=0, tiled=True),
        lax.all_gather(down_weight[0], "frames", axis=0, tiled=True),
    )
    w_qkv, w_out, w_gate, w_up, w_down = weights
    gain_one = attn_gain[0].astype(jnp.float32)
    gain_two = ffn_gain[0].astype(jnp.float32)
    normed = norm_rows(layer_in, gain_one).astype(jnp.bfloat16).reshape(token_rows, model_width)
    qkv = (
        flat_dot(normed, w_qkv).astype(jnp.bfloat16).reshape(frame_count, positions, 3, HEADS, HEAD)
    )
    queries = qkv[:, :, 0]
    key_part = qkv[:, :, 1]
    values = qkv[:, :, 2]
    scores = (
        jnp.einsum("fqhd,fkhd->fhqk", queries, key_part, preferred_element_type=jnp.float32)
        * head_scale
    )
    causal = jnp.arange(positions)[:, None] >= jnp.arange(positions)[None, :]
    scores = jnp.where(causal[None, None], scores, -1e30)
    probs = jax.nn.softmax(scores, axis=-1)
    probs_low = probs.astype(jnp.bfloat16)
    mixed = jnp.einsum("fhqk,fkhd->fqhd", probs_low, values, preferred_element_type=jnp.float32)
    mixed = mixed.astype(jnp.bfloat16).reshape(token_rows, model_width)
    after_attn = layer_in + flat_dot(mixed, w_out).reshape(frame_count, positions, model_width)
    normed_two = (
        norm_rows(after_attn, gain_two).astype(jnp.bfloat16).reshape(token_rows, model_width)
    )
    gate_pre = flat_dot(normed_two, w_gate)
    up_pre = flat_dot(normed_two, w_up)
    hidden = (jax.nn.silu(gate_pre) * up_pre).astype(jnp.bfloat16)
    out_full = after_attn + flat_dot(hidden, w_down).reshape(frame_count, positions, model_width)
    b_qkv, b_out, b_gate, b_up, b_down = weights
    grad_out = cotangent[0].astype(jnp.float32)
    grad_ff = grad_out.reshape(token_rows, model_width).astype(jnp.bfloat16)
    grad_down = trans_dot(hidden, grad_ff)
    grad_hidden = back_dot(grad_ff, b_down)
    sigmoid_gate = jax.nn.sigmoid(gate_pre)
    grad_gate = (
        grad_hidden * up_pre * sigmoid_gate * (1.0 + gate_pre * (1.0 - sigmoid_gate))
    ).astype(jnp.bfloat16)
    grad_up = (grad_hidden * gate_pre * sigmoid_gate).astype(jnp.bfloat16)
    grad_gate_w = trans_dot(normed_two, grad_gate)
    grad_up_w = trans_dot(normed_two, grad_up)
    grad_normed_two = (back_dot(grad_gate, b_gate) + back_dot(grad_up, b_up)).reshape(
        frame_count, positions, model_width
    )
    grad_after_norm, grad_gain_two = norm_back(grad_normed_two, after_attn, gain_two)
    grad_after = grad_out + grad_after_norm
    grad_branch = grad_after.reshape(token_rows, model_width).astype(jnp.bfloat16)
    grad_out_w = trans_dot(mixed, grad_branch)
    grad_mixed = (
        back_dot(grad_branch, b_out)
        .astype(jnp.bfloat16)
        .reshape(frame_count, positions, HEADS, HEAD)
    )
    grad_values = jnp.einsum(
        "fhqk,fqhd->fkhd", probs_low, grad_mixed, preferred_element_type=jnp.float32
    )
    grad_probs = jnp.einsum(
        "fqhd,fkhd->fhqk", grad_mixed, values, preferred_element_type=jnp.float32
    )
    grad_scores = (
        probs * (grad_probs - jnp.sum(grad_probs * probs, axis=-1, keepdims=True))
    ).astype(jnp.bfloat16)
    grad_queries = (
        jnp.einsum("fhqk,fkhd->fqhd", grad_scores, key_part, preferred_element_type=jnp.float32)
        * head_scale
    )
    grad_keys = (
        jnp.einsum("fhqk,fqhd->fkhd", grad_scores, queries, preferred_element_type=jnp.float32)
        * head_scale
    )
    grad_qkv = jnp.stack([grad_queries, grad_keys, grad_values], axis=2).astype(jnp.bfloat16)
    grad_qkv = grad_qkv.reshape(token_rows, 3 * model_width)
    grad_qkv_w = trans_dot(normed, grad_qkv)
    all_parts = (
        lax.psum_scatter(grad_qkv_w, "frames", scatter_dimension=0, tiled=True),
        lax.psum_scatter(grad_out_w, "frames", scatter_dimension=0, tiled=True),
        lax.psum_scatter(grad_gate_w, "frames", scatter_dimension=0, tiled=True),
        lax.psum_scatter(grad_up_w, "frames", scatter_dimension=0, tiled=True),
        lax.psum_scatter(grad_down, "frames", scatter_dimension=0, tiled=True),
    )
    d_qkv_rows, d_out_rows, d_gate_rows, d_up_rows, d_down_rows = all_parts
    grad_normed = back_dot(grad_qkv, b_qkv).reshape(frame_count, positions, model_width)
    grad_in_norm, grad_gain_one = norm_back(grad_normed, layer_in, gain_one)
    grad_in = grad_after + grad_in_norm
    gain_sums = lax.psum((grad_gain_one, grad_gain_two), "frames")
    grad_shift = jnp.sum(grad_in, axis=1).astype(jnp.bfloat16)
    grad_ctx_w = trans_dot(ctx_full, grad_shift)
    ctx_w_rows = lax.psum_scatter(grad_ctx_w, ("stream", "frames"), scatter_dimension=0, tiled=True)
    grad_context = back_dot(grad_shift, ctx_rows)
    context_half = lax.psum_scatter(
        grad_context.astype(jnp.bfloat16), "stream", scatter_dimension=1, tiled=True
    ).astype(jnp.float32)
    grad_ext = jnp.zeros((frame_count + 2, positions, model_width), jnp.float32)
    for offset in range(3):
        term = chosen[offset][None, :, None] * valid_rows[offset][:, None, None] * grad_in
        grad_ext = grad_ext + jnp.pad(term, ((2 - offset, offset), (0, 0), (0, 0)))
    back_rows = shifted(grad_ext[:2].astype(jnp.bfloat16), "frames", -1).astype(jnp.float32)
    grad_tokens = grad_ext[2:].at[frame_count - 2 :].add(back_rows)
    return (
        out_full.astype(jnp.bfloat16)[None],
        grad_tokens[None],
        context_half,
        ctx_w_rows,
        gain_sums[0][None],
        gain_sums[1][None],
        d_qkv_rows[None],
        d_out_rows[None],
        d_gate_rows[None],
        d_up_rows[None],
        d_down_rows[None],
    )


def solution(mesh):
    fits = mesh.shape["frames"] == 16 and mesh.shape["stream"] == 2
    return jax.shard_map(
        body_kernel if fits else body,
        mesh=mesh,
        in_specs=(
            P("stream", "frames", None, None),
            P("frames", "stream"),
            P(("stream", "frames"), None),
            P(),
            P(),
            P("stream", None, None),
            P("stream", None, None),
            P("stream", "frames", None),
            P("stream", "frames", None),
            P("stream", "frames", None),
            P("stream", "frames", None),
            P("stream", "frames", None),
            P("stream", "frames", None, None),
        ),
        out_specs=(
            P("stream", "frames", None, None),
            P("stream", "frames", None, None),
            P("frames", "stream"),
            P(("stream", "frames"), None),
            P("stream", None, None),
            P("stream", None, None),
            P("stream", "frames", None),
            P("stream", "frames", None),
            P("stream", "frames", None),
            P("stream", "frames", None),
            P("stream", "frames", None),
        ),
        check_vma=False,
    )
```

```python
import jax
import jax.numpy as jnp
from jax import lax
from jax.experimental import pallas as pl
from jax.experimental.pallas import tpu as pltpu
from jax.sharding import PartitionSpec as P

HEADS = 16
HEAD = 64


epsilon = 1e-05


def shifted(x, axis, by):
    length = lax.axis_size(axis)
    pairs = [(i, i + by) for i in range(length) if 0 <= i + by < length]
    return lax.ppermute(x, axis, pairs)


def flat_dot(left, right):
    return jnp.dot(left, right, preferred_element_type=jnp.float32)


def trans_dot(left, right):
    return lax.dot_general(
        left, right, (((0,), (0,)), ((), ())), preferred_element_type=jnp.float32
    )


def back_dot(left, right):
    return lax.dot_general(
        left, right, (((1,), (1,)), ((), ())), preferred_element_type=jnp.float32
    )


def norm_rows(rows, gain):
    return rows * lax.rsqrt(jnp.mean(rows * rows, axis=-1, keepdims=True) + epsilon) * gain


def norm_back(grad_normed, rows, gain):
    scale = lax.rsqrt(jnp.mean(rows * rows, axis=-1, keepdims=True) + epsilon)
    unit = rows * scale
    grad_gain = jnp.sum(grad_normed * unit, axis=0)
    grad_unit = grad_normed * gain
    grad_rows = scale * (grad_unit - unit * jnp.mean(grad_unit * unit, axis=-1, keepdims=True))
    return (grad_rows, grad_gain)


def shift_tables(delay, lengths, frame_ids):
    starts = jnp.cumsum(lengths) - lengths
    at_start = jnp.any(frame_ids[:, None] == starts[None, :], axis=1)
    after_start = jnp.any(frame_ids[:, None] - 1 == starts[None, :], axis=1)
    keep_one = jnp.logical_not(at_start)
    keep_two = jnp.logical_and(keep_one, jnp.logical_not(after_start))
    valid_rows = jnp.stack([jnp.ones_like(keep_one), keep_one, keep_two]).astype(jnp.float32)
    chosen = (delay[None, :] == jnp.arange(3, dtype=jnp.int32)[:, None]).astype(jnp.float32)
    return (chosen, valid_rows)


MESH = pl.DeviceIdType.MESH
CHUNKS = 17
FEED = 11
WIDE = 768
ROUNDS = 5
FAR_ROUNDS = 7
SPLIT = ((0, 48), (48, 64))
HALVES = ((0, 32), (32, 64))
WHOLE = ((0, 64),)
GATHER_HALVES = 6
REDUCE_HALVES = 17


def mm(a, b):
    return jnp.dot(a, b, preferred_element_type=jnp.float32)


def nt(a, b):
    return lax.dot_general(a, b, (((1,), (1,)), ((), ())), preferred_element_type=jnp.float32)


def tn(a, b):
    return lax.dot_general(a, b, (((0,), (0,)), ((), ())), preferred_element_type=jnp.float32)


def either(cond, fn):
    if isinstance(cond, bool):
        if cond:
            fn()
    else:
        pl.when(cond)(fn)


def within(t, low, high):
    if isinstance(t, int):
        return low <= t < high
    return jnp.logical_and(t >= low, t < high)


def layer_kernel(
    tok_hbm,
    ctx,
    gain_one,
    gain_two,
    cot_hbm,
    ctx_own,
    qkv_own,
    out_own,
    gate_hbm,
    up_hbm,
    down_hbm,
    delay,
    lengths,
    mixed_hbm,
    dtok_hbm,
    dctx,
    dctxw_hbm,
    dgain_one,
    dgain_two,
    dqkv_hbm,
    dout_hbm,
    dgate_hbm,
    dup_hbm,
    ddown_hbm,
    gathered,
    pend,
    cot,
    gate_own,
    up_own,
    down_own,
    w_own,
    lin,
    n1,
    n1t,
    qkv,
    mixed,
    aft,
    n2,
    n2t,
    oacc,
    gn,
    wbuf,
    wtail,
    part,
    part_own,
    hidt,
    shift,
    gacc,
    gsend,
    grecv,
    xsend,
    xrecv,
    r_c,
    r_y,
    r_zl,
    r_zh,
    t_keep,
    t_send,
    u_keep,
    u_send,
    v_keep,
    v_send,
    fin,
    ag_ss,
    ag_rs,
    rs_ss,
    rs_rs,
    x_ss,
    x_rs,
    g_ss,
    g_rs,
    own_sem,
    load_sem,
    pend_sem,
    half_sem,
    tok_sem,
    in_sem,
    rim_ss,
    rim_rs,
    out_sem,
):
    s = lax.axis_index("stream")
    f = lax.axis_index("frames")
    c = f % 2
    y = (f // 2) % 2
    zl = (f // 4) % 2
    zh = f // 8
    d_c = (s, f + 1 - 2 * c)
    d_y = (s, f + 2 - 4 * y)
    d_zl = (s, f + 4 - 8 * zl)
    d_zh = (s, f + 8 - 16 * zh)
    d_x = (1 - s, f)
    partners = (d_zh, d_zl, d_y, d_c)

    frames = lax.axis_size("frames")
    has_next, has_prev = f < frames - 1, f > 0
    d_next, d_prev = (s, f + 1), (s, f - 1)

    tokext = n2t
    tok_copy = pltpu.make_async_copy(tok_hbm, tokext.at[16:1040], tok_sem)
    fetches = [
        pltpu.make_async_copy(src, dst, in_sem.at[i])
        for i, (src, dst) in enumerate(
            ((down_hbm, down_own), (gate_hbm, gate_own), (up_hbm, up_own), (cot_hbm, cot))
        )
    ]
    for cp in fetches:
        cp.start()
    tok_copy.start()

    barrier = pltpu.get_barrier_semaphore()

    def greet(device):
        pl.semaphore_signal(barrier, inc=1, device_id=device, device_id_type=MESH)

    for device in partners + (d_x,):
        greet(device)
    pl.when(has_next)(lambda: greet(d_next))
    pl.when(has_prev)(lambda: greet(d_prev))

    w_own[0, 0:32, 0:512] = ctx_own[:, 0:512]
    w_own[0, 32:64, 0:512] = ctx_own[:, 512:1024]
    w_own[0, :, 512:768] = out_own[:, 768:1024]
    w_own[5] = out_own[:, 0:768]
    for g in range(4):
        for part_id in range(3):
            at = part_id * 1024 + g * 256
            w_own[1 + g, :, part_id * 256 : part_id * 256 + 256] = qkv_own[:, at : at + 256]

    def own_copy(low, high, i):
        return pltpu.make_async_copy(
            w_own.at[low:high], gathered.at[low:high, zh, zl, y, c], own_sem.at[i]
        )

    own_copy(0, 6, 0).start()

    pl.semaphore_wait(barrier, 5 + has_next.astype(jnp.int32) + has_prev.astype(jnp.int32))

    def remote(src, dst, ss, rs, device):
        return pltpu.make_async_remote_copy(
            src_ref=src, dst_ref=dst, send_sem=ss, recv_sem=rs, device_id=device, device_id_type=MESH
        )

    def ag_copies(stage, k, split):
        low, high = (slice(*rows) for rows in split)
        if stage == 0:
            triples = [(w_own.at[k], gathered.at[k, zh, zl, y, c], d_zh)]
        elif stage == 1:
            near, side = gathered.at[k, :, zl, y, c, low], gathered.at[k, :, zl, y, c, high]
            triples = [(near, near, d_zl), (side, side, d_y)]
        elif stage == 2:
            side, near = gathered.at[k, :, :, y, c, low], gathered.at[k, :, zl, :, c, high]
            triples = [(side, side, d_y), (near, near, d_zl)]
        else:
            own = gathered.at[k, :, :, :, c]
            triples = [(own, own, d_c)]
        first = (0, 1, 3, 5)[stage]
        return [
            remote(src, dst, ag_ss.at[first + i, k], ag_rs.at[first + i, k], device)
            for i, (src, dst, device) in enumerate(triples)
        ]

    def choose(k, bound, under, above, fn):
        if isinstance(k, int):
            fn(under if k < bound else above)
        else:
            pl.when(k < bound)(lambda: fn(under))
            pl.when(k >= bound)(lambda: fn(above))

    def ag_do(act, stage, k):
        if stage in (0, 3):
            act(ag_copies(stage, k, SPLIT))
        else:
            choose(k, GATHER_HALVES, SPLIT, HALVES, lambda split: act(ag_copies(stage, k, split)))

    def by_split(r, fn):
        choose(r, REDUCE_HALVES, SPLIT, HALVES, fn)

    def start_all(copies):
        for cp in copies:
            cp.start()

    def wait_recv_all(copies):
        for cp in copies:
            cp.wait_recv()

    def wait_send_all(copies):
        for cp in copies:
            cp.wait_send()

    class load_copy:
        def __init__(self, k, slot):
            self.parts = [
                pltpu.make_async_copy(
                    gathered.at[k, i // 2, i % 2], wbuf.at[slot, i // 2, i % 2], load_sem.at[slot, i]
                )
                for i in range(4)
            ]

        def start(self):
            for cp in self.parts:
                cp.start()

        def wait(self):
            for cp in self.parts:
                cp.wait()

    def ag_step(stage, k):
        def go():
            if stage > 0:
                ag_do(wait_recv_all, stage - 1, k)
            ag_do(start_all, stage, k)
        either(within(k, 0, CHUNKS), go)

    def ag_tick(t, gap=1):
        for stage in range(3):
            ag_step(stage, t - gap * stage)

    def ag_ready(k):
        def ready():
            ag_do(wait_recv_all, 3, k)
            load_copy(k, k % 2).start()
        either(within(k, 0, CHUNKS), ready)

    def rs_copies(stage, r, split):
        two, slot = r % (2 if stage == 0 else 3), r % (FAR_ROUNDS if stage == 3 else ROUNDS)
        if stage == 0:
            triples = [(pend.at[r, :, :, :, 1 - c], r_c.at[two], d_c)]
        elif stage == 3:
            triples = [(v_send.at[two], r_zh.at[slot], d_zh)]
        else:
            src, dst = ((t_send, r_y), (u_send, r_zl))[stage - 1]
            devices = ((d_y, d_zl), (d_zl, d_y))[stage - 1]
            triples = [
                (src.at[two, :, low:high], dst.at[slot, :, low:high], device)
                for (low, high), device in zip(split, devices)
            ]
        first = (0, 1, 3, 5)[stage]
        return [
            remote(src, dst, rs_ss.at[first + i, two], rs_rs.at[first + i, slot], device)
            for i, (src, dst, device) in enumerate(triples)
        ]

    def rs_do(act, stage, r):
        if stage in (0, 3):
            act(rs_copies(stage, r, SPLIT))
        else:
            by_split(r, lambda split: act(rs_copies(stage, r, split)))

    def add(a, b):
        return a.astype(jnp.float32) + b.astype(jnp.float32)

    def place_result(k, res):
        if not isinstance(k, int):
            @pl.when(k < FEED)
            def _():
                fin[k] = res
            pl.when(k == FEED)(lambda: place_result(FEED, res))
            return
        if k < FEED:
            fin[k] = res
        elif k == FEED:
            aft[384:448, 0:768] = res
        elif k < CHUNKS - 1:
            g = k - FEED - 1
            for p in range(3):
                aft[192 + 64 * p : 256 + 64 * p, g * 256 : g * 256 + 256] = res[:, p * 256 : p * 256 + 256]
        else:
            aft[384:448, 768:1024] = res[:, 512:768]
            aft[448:480, 0:512] = res[0:32, 0:512]
            aft[448:480, 512:1024] = res[32:64, 0:512]

    def out_copies():
        pairs = [(aft.at[384:448], dout_hbm), (aft.at[448:480], dctxw_hbm)]
        for p in range(3):
            pairs.append((aft.at[192 + 64 * p : 256 + 64 * p], dqkv_hbm.at[:, p * 1024 : p * 1024 + 1024]))
        return pairs

    def feed_copies():
        pairs = [(aft.at[512:688], ddown_hbm)]
        for i, hbm in enumerate((dgate_hbm, dup_hbm)):
            at = i * 768
            if i == 1:
                at = 704
            for p in range(3):
                n = 1024 if p < 2 else 768
                pairs.append((aft.at[at + 64 * p : at + 64 * p + 64, 0:n], hbm.at[:, p * 1024 : p * 1024 + n]))
        return pairs

    def out_copy(pair, i):
        return pltpu.make_async_copy(pair[0], pair[1], out_sem.at[i])

    def unpack_feed():
        for j in range(FEED):
            for q in range(4):
                aft[512 + j * 16 : 528 + j * 16, q * 256 : q * 256 + 256] = fin[j, q * 16 : q * 16 + 16, 512:768]
        for i, at in enumerate((0, 704)):
            cols = [
                fin[j, :, i * 256 + d * 16 : i * 256 + d * 16 + 16] for d in range(16) for j in range(FEED)
            ]
            for p in range(22):
                piece = jnp.concatenate(cols[p * 8 : p * 8 + 8], axis=1)
                row, col = at + 64 * (p // 8), (p % 8) * 128
                aft[row : row + 64, col : col + 128] = piece

    def pend_copy(r):
        return pltpu.make_async_copy(part.at[r % 2], pend.at[r], pend_sem.at[r % 2])

    def half_copy(r):
        return pltpu.make_async_copy(pend.at[r, :, :, :, c], part_own.at[r % 2], half_sem.at[r % 2])

    def part_done(r):
        either(within(r, 1, CHUNKS), lambda: pend_copy(r - 1).wait())
        pend_copy(r).start()

    def send_half(r):
        either(within(r, 2, CHUNKS), lambda: rs_do(wait_send_all, 0, r - 2))
        rs_do(start_all, 0, r)
        half_copy(r).start()

    def rs_tick(r):
        def stage_y():
            k = r - 1
            rs_do(wait_recv_all, 0, k)
            half_copy(k).wait()
            either(within(k, 3, CHUNKS), lambda: rs_do(wait_send_all, 1, k - 3))
            two, three = k % 2, k % 3

            def pieces(split):
                def piece(i, _):
                    a, b = i // 2, i % 2
                    for (low, high), send, keep in zip(split, ((b, 1 - y), (1 - zl, b)), ((b, y), (zl, b))):
                        for out, (m, n) in ((t_send, send), (t_keep, keep)):
                            out[three, i, low:high] = part_own[two, a, m, n, low:high] + r_c[two, a, m, n, low:high]
                    return 0

                lax.fori_loop(0, 4, piece, 0)

            by_split(k, pieces)
            rs_do(start_all, 1, k)
        either(within(r, 1, CHUNKS + 1), stage_y)
        either(within(r, 0, CHUNKS), lambda: send_half(r))

        def stage_zl():
            k = r - 3
            rs_do(wait_recv_all, 1, k)
            either(within(k, 3, CHUNKS), lambda: rs_do(wait_send_all, 2, k - 3))
            three, slot = k % 3, k % ROUNDS

            def pieces(split):
                for a in range(2):
                    for (low, high), mine in zip(split, (zl, y)):
                        for out, at in ((u_send, a * 2 + 1 - mine), (u_keep, a * 2 + mine)):
                            out[three, a, low:high] = t_keep[three, at, low:high] + r_y[slot, at, low:high]

            by_split(k, pieces)
            rs_do(start_all, 2, k)
        either(within(r, 3, CHUNKS + 3), stage_zl)

        def stage_zh():
            k = r - 5
            rs_do(wait_recv_all, 2, k)
            either(within(k, 3, CHUNKS), lambda: rs_do(wait_send_all, 3, k - 3))
            three, slot = k % 3, k % ROUNDS
            v_send[three] = u_keep[three, 1 - zh] + r_zl[slot, 1 - zh]
            v_keep[three] = u_keep[three, zh] + r_zl[slot, zh]
            rs_do(start_all, 3, k)
        either(within(r, 5, CHUNKS + 5), stage_zh)

        def last():
            k = r - 7
            rs_do(wait_recv_all, 3, k)
            place_result(k, add(v_keep[k % 3], r_zh[k % FAR_ROUNDS]))
        either(within(r, 7, CHUNKS + 7), last)

    rim_copy = remote(tok_hbm.at[1008:1024], tokext.at[0:16], rim_ss.at[0], rim_rs.at[0], d_next)
    halo_copy = remote(oacc.at[0:16], oacc.at[1024:1040], rim_ss.at[1], rim_rs.at[1], d_prev)
    pl.when(has_next)(lambda: rim_copy.start())

    @pl.when(jnp.logical_not(has_prev))
    def _():
        tokext[0:16, :] = jnp.zeros((16, 1024), jnp.bfloat16)

    @pl.when(jnp.logical_not(has_next))
    def _():
        oacc[1024:1040, :] = jnp.zeros((16, 1024), jnp.float32)

    gacc[...] = jnp.zeros_like(gacc)

    place = lax.broadcasted_iota(jnp.int32, (16, 8, 1), 1)
    wait = jnp.zeros((16, 8, 1), jnp.int32)
    for p in range(8):
        wait = jnp.where(place == p, delay[p], wait)

    def starts_at(frame):
        start = jnp.int32(0)
        hit = frame == start
        for i in range(lengths.shape[0] - 1):
            start = start + lengths[i]
            hit = jnp.logical_or(hit, frame == start)
        return hit

    def same_item(frame, j):
        ok = jnp.logical_not(starts_at(frame))
        if j == 2:
            ok = jnp.logical_and(ok, jnp.logical_not(starts_at(frame - 1)))
        return ok

    def frame_of(i):
        return f * 128 + i * 16 + lax.broadcasted_iota(jnp.int32, (16, 8, 1), 0)

    def pack_feed(own, at):
        for j in range(FEED):
            cols = [own[:, d * 176 + j * 16 : d * 176 + j * 16 + 16] for d in range(16)]
            w_own[6 + j, :, at : at + 256] = jnp.concatenate(cols, axis=1)

    ag_tick(0)
    own_copy(0, 6, 0).wait()
    ag_tick(1)
    for cp in fetches[:2]:
        cp.wait()
    for j in range(FEED):
        for q in range(4):
            w_own[6 + j, q * 16 : q * 16 + 16, 512:768] = down_own[
                j * 16 : j * 16 + 16, q * 256 : q * 256 + 256
            ]
    pack_feed(gate_own, 0)
    ag_tick(2)
    fetches[2].wait()
    pack_feed(up_own, 256)
    own_copy(6, CHUNKS, 1).start()
    ag_tick(3)
    ag_step(3, 0)
    ag_ready(0)
    own_copy(6, CHUNKS, 1).wait()
    ag_tick(4)

    load_copy(0, 0).wait()
    wtail[...] = wbuf[0, :, :, :, :, :, 512:768].reshape(1024, 256)
    half = shift.shape[1] // 2
    for h in range(2):
        w_half = wbuf[0, :, :, :, :, h * 32 : h * 32 + 32, 0:512].reshape(512, 512)
        shift[:, h * half : (h + 1) * half] = mm(ctx[...], w_half)
    xsend[0] = shift[...].astype(jnp.bfloat16)

    x_copy = remote(xsend.at[0], xrecv.at[0], x_ss.at[0], x_rs.at[0], d_x)
    x_copy.start()
    ag_tick(5)
    for k in (6, 7, 8):
        ag_step(0, k)
    ag_step(3, 1)
    ag_ready(1)
    x_copy.wait_recv()
    shift[...] = shift[...] + xrecv[0].astype(jnp.float32)

    def rows_of(i, size):
        return pl.ds(pl.multiple_of(i * size, size), size)

    def norm1(i, _):
        rows = rows_of(i, 128)
        sh = shift[rows_of(i, 16), :]
        near = tokext[pl.ds(pl.multiple_of(i * 128, 128), 144), :].astype(jnp.float32)
        frame = frame_of(i)
        x = jnp.zeros((16, 8, 1024), jnp.float32)
        for j in range(3):
            keep = wait == j
            if j > 0:
                keep = jnp.logical_and(keep, same_item(frame, j))
            piece = near[16 - 8 * j : 144 - 8 * j].reshape(16, 8, 1024)
            x = jnp.where(keep, piece, x)
        x = x + sh[:, None, :]
        r = lax.rsqrt(jnp.mean(x * x, axis=-1, keepdims=True) + epsilon)
        n = (x * r * gain_one[...].astype(jnp.float32)[None]).reshape(128, 1024).astype(jnp.bfloat16)
        lin[rows, :] = x.reshape(128, 1024)
        n1[rows, :] = n
        n1t[:, rows] = n.T
        return 0

    tok_copy.wait()
    pl.when(has_prev)(lambda: rim_copy.wait_recv())
    lax.fori_loop(0, 4, norm1, 0)
    ag_step(1, 5)
    ag_step(2, 4)
    lax.fori_loop(4, 8, norm1, 0)
    ag_step(1, 6)

    lane_low = lax.broadcasted_iota(jnp.int32, (128, 128), 1) < 64
    head_scale = HEAD ** (-0.5)

    def both(v):
        zero = jnp.zeros_like(v)
        return jnp.concatenate([jnp.where(lane_low, v, zero), jnp.where(lane_low, zero, v)], axis=0)

    own_frame = [
        lax.broadcasted_iota(jnp.int32, (8, 128), 1) // 8 == fr for fr in range(16)
    ]
    key_seen = lax.broadcasted_iota(jnp.int32, (8, 128), 0) <= lax.broadcasted_iota(jnp.int32, (8, 128), 1) % 8

    def compact(full, h):
        out = full[h * 128 : h * 128 + 8]
        for fr in range(1, 16):
            at = h * 128 + fr * 8
            out = jnp.where(own_frame[fr], full[at : at + 8], out)
        return out

    def spread(pair):
        zero = jnp.zeros((8, 128), jnp.float32)
        rows = [jnp.where(own_frame[fr], x, zero) for x in pair for fr in range(16)]
        return jnp.concatenate(rows, axis=0).astype(jnp.bfloat16)

    def probabilities(q, kk):
        full = nt(kk, q)
        pair = []
        for h in range(2):
            sc = jnp.where(key_seen, compact(full, h) * head_scale, -1e30)
            e = jnp.exp(sc - jnp.max(sc, axis=0, keepdims=True))
            pair.append(e / jnp.sum(e, axis=0, keepdims=True))
        return pair

    def pair_of(g, sub, lo):
        return [qkv[g, sub, at + lo : at + lo + 128] for at in (0, 256, 512)]

    def attn_fwd(g):
        def rows_step(i, _):
            for u in range(4):
                sub = rows_of(i * 4 + u, 128)
                for lo in (0, 128):
                    q, k, v = pair_of(g, sub, lo)
                    pr = spread(probabilities(q, both(k)))
                    out = tn(pr, both(v)).astype(jnp.bfloat16)
                    mixed[sub, pl.ds(pl.multiple_of(g * 256 + lo, 128), 128)] = out
            return 0
        lax.fori_loop(0, 2, rows_step, 0)

    def attn_bwd(g):
        def rows_step(i, _):
            for u in range(4):
                sub = rows_of(i * 4 + u, 128)
                for lo in (0, 128):
                    q, k, v = pair_of(g, sub, lo)
                    do = mixed[sub, pl.ds(pl.multiple_of(g * 256 + lo, 128), 128)]
                    kk = both(k)
                    pr = probabilities(q, kk)
                    full = nt(both(v), do)
                    ds = []
                    for h in range(2):
                        d = compact(full, h)
                        ds.append(pr[h] * (d - jnp.sum(d * pr[h], axis=0, keepdims=True)))
                    ds = spread(ds)
                    dq = tn(ds, kk) * head_scale
                    dk = mm(ds, q)
                    dv = mm(spread(pr), do)
                    qkv[g, sub, lo : lo + 128] = dq.astype(jnp.bfloat16)
                    qkv[g, sub, 256 + lo : 384 + lo] = (
                        jnp.where(lane_low, dk[:128], dk[128:]) * head_scale
                    ).astype(jnp.bfloat16)
                    qkv[g, sub, 512 + lo : 640 + lo] = jnp.where(lane_low, dv[:128], dv[128:]).astype(jnp.bfloat16)
            return 0
        lax.fori_loop(0, 2, rows_step, 0)

    def qkv_group(g, _):
        slot = (1 + g) % 2
        load_copy(1 + g, slot).wait()

        def rows_step(i, _):
            rows = rows_of(i, 256)
            qkv[g, rows, :] = mm(n1[rows, :], wbuf[slot].reshape(1024, WIDE)).astype(jnp.bfloat16)
            return 0

        lax.fori_loop(0, 4, rows_step, 0)
        ag_step(3, 2 + g)
        ag_tick(9 + g, 2)
        attn_fwd(g)
        ag_ready(2 + g)
        return 0

    lax.fori_loop(0, 4, qkv_group, 0)

    load_copy(5, 1).wait()

    def after(i, _):
        rows = rows_of(i, 256)
        m = mixed[rows, :]
        a = lin[rows, 0:WIDE] + mm(m, wbuf[1].reshape(1024, WIDE))
        b = lin[rows, WIDE:1024] + mm(m, wtail[...])
        x = jnp.concatenate([a, b], axis=1)
        aft[rows, :] = x
        oacc[rows, :] = x
        gn[rows, :] = jnp.zeros((256, 1024), jnp.float32)
        x3 = x.reshape(32, 8, 1024)
        r = lax.rsqrt(jnp.mean(x3 * x3, axis=-1, keepdims=True) + epsilon)
        n = (x3 * r * gain_two[...].astype(jnp.float32)[None]).reshape(256, 1024).astype(jnp.bfloat16)
        n2[rows, :] = n
        n2t[0:1024, rows] = n.T
        return 0

    lax.fori_loop(0, 2, after, 0)
    ag_step(3, 6)
    ag_tick(13, 2)
    lax.fori_loop(2, 4, after, 0)
    ag_ready(6)
    fetches[3].wait()

    def feed(j, _):
        slot = j % 2
        load_copy(6 + j, slot).wait()
        two = j % 2

        def rows_step(i):
            rows = slice(i * 512, i * 512 + 512)
            w_gu = wbuf[slot, :, :, :, :, :, 0:512].reshape(1024, 512)
            pre = mm(n2[rows, :], w_gu)
            gate, up = pre[:, :256], pre[:, 256:]
            g_hid = jnp.zeros((512, 256), jnp.float32)
            for q in range(4):
                w_q = wbuf[slot, :, :, :, :, q * 16 : q * 16 + 16, 512:768].reshape(256, 256)
                g_hid = g_hid + nt(cot[rows, q * 256 : q * 256 + 256], w_q)
            sig = jax.nn.sigmoid(gate)
            silu = gate * sig
            hid = (silu * up).astype(jnp.bfloat16)
            g_gate = (g_hid * up * sig * (1.0 + gate * (1.0 - sig))).astype(jnp.bfloat16)
            g_up = (g_hid * silu).astype(jnp.bfloat16)
            for q in range(4):
                w_q = wbuf[slot, :, :, :, :, q * 16 : q * 16 + 16, 512:768].reshape(256, 256)
                oacc[rows, q * 256 : q * 256 + 256] += mm(hid, w_q)
            both_g = jnp.concatenate([g_gate, g_up], axis=1)
            n1[rows, 0:512] = both_g
            hidt[:, rows] = hid.T
            back = nt(both_g, w_gu)
            gn[rows, :] += back

        for i in range(2):
            rows_step(i)
        ag_step(3, 7 + j)
        ag_tick(14 + j, 2)

        def weight_step(m, _):
            res = mm(n2t[rows_of(m, 512), :], n1[:, 0:512]).astype(jnp.bfloat16).reshape(2, 2, 2, 64, 512)
            part[two, m, :, :, :, :, 0:512] = res
            return 0

        lax.fori_loop(0, 2, weight_step, 0)
        ag_ready(7 + j)
        for q in range(4):
            res = mm(hidt[...], cot[:, q * 256 : q * 256 + 256]).astype(jnp.bfloat16)
            part[two, :, :, :, :, q * 16 : q * 16 + 16, 512:768] = res.reshape(2, 2, 2, 2, 16, 256)
        part_done(j)
        pl.when(jnp.logical_and(j % 2 == 1, j < 6))(lambda: rs_tick(j // 2))
        pl.when(j >= 6)(lambda: rs_tick(j - 3))
        return 0

    lax.fori_loop(0, FEED, feed, 0)
    load_copy(5, 1).start()
    load_copy(1, 0).start()

    def norm2_back(i, _):
        rows = rows_of(i, 128)
        n2t[rows, :] = oacc[rows, :].astype(jnp.bfloat16)
        n1[:, rows] = mixed[rows, :].T
        x = aft[rows, :].reshape(16, 8, 1024)
        g = gn[rows, :].reshape(16, 8, 1024)
        gn[rows, :] = jnp.zeros((128, 1024), jnp.float32)
        r = lax.rsqrt(jnp.mean(x * x, axis=-1, keepdims=True) + epsilon)
        unit = x * r
        gacc[8:16, :] += jnp.sum(g * unit, axis=0)
        gu = g * gain_two[...].astype(jnp.float32)[None]
        back = r * (gu - unit * jnp.mean(gu * unit, axis=-1, keepdims=True))
        total = cot[rows, :].astype(jnp.float32) + back.reshape(128, 1024)
        oacc[rows, :] = total
        n2[rows, :] = total.astype(jnp.bfloat16)
        return 0

    lax.fori_loop(0, 8, norm2_back, 0)
    mixed_copy = pltpu.make_async_copy(n2t.at[0:1024], mixed_hbm, out_sem.at[0])
    mixed_copy.start()
    rs_tick(8)


    def out_weight_step(m, _):
        res = mm(n1[rows_of(m, 256), :], n2[:, 0:WIDE]).astype(jnp.bfloat16)
        part[1, m // 2, m % 2] = res.reshape(2, 2, 64, WIDE)
        return 0

    lax.fori_loop(0, 4, out_weight_step, 0)
    part_done(11)

    def mixed_back(i, _):
        rows = rows_of(i, 256)
        g = n2[rows, :]
        res = nt(g[:, 0:WIDE], wbuf[1].reshape(1024, WIDE)) + nt(g[:, WIDE:1024], wtail[...])
        mixed[rows, :] = res.astype(jnp.bfloat16)
        return 0

    load_copy(5, 1).wait()
    lax.fori_loop(0, 4, mixed_back, 0)
    load_copy(2, 1).start()
    rs_tick(9)

    def qkv_back(g, _):
        slot = g % 2
        attn_bwd(g)
        pend_copy(11 + g).wait()
        rs_tick(10 + g + g // 2)
        two = g % 2

        def weight_step(m, _):
            res = mm(n1t[rows_of(m, 256), :], qkv[g]).astype(jnp.bfloat16)
            part[two, m // 2, m % 2] = res.reshape(2, 2, 64, WIDE)
            return 0

        lax.fori_loop(0, 4, weight_step, 0)
        pend_copy(12 + g).start()

        def rows_step(i, _):
            rows = rows_of(i, 256)
            back = nt(qkv[g, rows, :], wbuf[slot].reshape(1024, WIDE))
            gn[rows, :] += back
            return 0

        load_copy(1 + g, slot).wait()
        lax.fori_loop(0, 4, rows_step, 0)
        pl.when(g == 1)(lambda: rs_tick(12))
        pl.when(g < 2)(lambda: load_copy(3 + g, slot).start())
        pl.when(g == 2)(lambda: load_copy(0, 0).start())
        return 0

    lax.fori_loop(0, 4, qkv_back, 0)

    def norm1_back(i, _):
        rows = rows_of(i, 128)
        x = lin[rows, :].reshape(16, 8, 1024)
        g = gn[rows, :].reshape(16, 8, 1024)
        r = lax.rsqrt(jnp.mean(x * x, axis=-1, keepdims=True) + epsilon)
        unit = x * r
        gacc[0:8, :] += jnp.sum(g * unit, axis=0)
        gu = g * gain_one[...].astype(jnp.float32)[None]
        back = r * (gu - unit * jnp.mean(gu * unit, axis=-1, keepdims=True))
        total = oacc[rows, :].reshape(16, 8, 1024) + back
        oacc[rows, :] = total.reshape(128, 1024)
        few = rows_of(i, 16)
        g_frame = jnp.sum(total, axis=1)
        shift[few, :] = g_frame
        xsend[1, few, :] = g_frame.astype(jnp.bfloat16)
        x_piece(i).start()
        return 0

    def x_piece(i):
        few = rows_of(i, 16)
        return remote(xsend.at[1, few], xrecv.at[1, few], x_ss.at[1 + i], x_rs.at[1 + i], d_x)

    lax.fori_loop(0, 8, norm1_back, 0)
    pl.when(has_prev)(lambda: halo_copy.start())
    def gain_copy(i):
        return remote(gsend.at[i], grecv.at[i], g_ss.at[i], g_rs.at[i], partners[i])

    def gain_step(i):
        gain_copy(i).wait_recv()
        total = gsend[i] + grecv[i]
        if i < 3:
            gsend[i + 1] = total
            gain_copy(i + 1).start()
        else:
            dgain_one[...] = total[0:8]
            dgain_two[...] = total[8:16]

    gsend[0] = gacc[...]
    gain_copy(0).start()

    pend_copy(15).wait()
    rs_tick(15)
    load_copy(0, 0).wait()

    def out_tail_step(m, _):
        res = mm(n1[rows_of(m, 256), :], n2[:, WIDE:1024]).astype(jnp.bfloat16)
        part[0, m // 2, m % 2, :, :, :, 512:768] = res.reshape(2, 2, 64, 256)
        return 0

    lax.fori_loop(0, 4, out_tail_step, 0)
    gain_step(0)

    for i in range(8):
        x_piece(i).wait_recv()
    g_low = (shift[...] + xrecv[1].astype(jnp.float32)).astype(jnp.bfloat16)
    ctx_t = ctx[...].T
    for h in range(2):
        gh = g_low[:, h * 512 : (h + 1) * 512]
        res = mm(ctx_t, gh).astype(jnp.bfloat16).reshape(2, 2, 2, 2, 32, 512)
        part[0, :, :, :, :, h * 32 : h * 32 + 32, 0:512] = res
    pend_copy(16).start()
    pend_copy(16).wait()
    w0 = wbuf[0, :, :, :, :, 0:32, 0:512].reshape(512, 512)
    w1 = wbuf[0, :, :, :, :, 32:64, 0:512].reshape(512, 512)
    dctx[...] = nt(g_low[:, :512], w0) + nt(g_low[:, 512:], w1)

    def dtok(i, _):
        rows = rows_of(i, 128)
        near = oacc[pl.ds(pl.multiple_of(i * 128, 128), 144), :]
        frame = frame_of(i)
        x = jnp.zeros((16, 8, 1024), jnp.float32)
        for j in range(3):
            keep = wait == j
            if j > 0:
                keep = jnp.logical_and(keep, same_item(frame + j, j))
            x = jnp.where(keep, near[8 * j : 128 + 8 * j].reshape(16, 8, 1024), x)
        gn[rows, :] = x.reshape(128, 1024)
        return 0

    rs_tick(16)
    dtok_copy = pltpu.make_async_copy(gn, dtok_hbm, out_sem.at[1])
    last_out = [out_copy(pair, 9 + i) for i, pair in enumerate(out_copies())]
    feed_out = [out_copy(pair, 2 + i) for i, pair in enumerate(feed_copies())]
    pl.when(has_next)(lambda: halo_copy.wait_recv())
    lax.fori_loop(0, 8, dtok, 0)
    dtok_copy.start()
    gain_step(1)
    rs_tick(17)
    gain_step(2)
    unpack_feed()
    for cp in feed_out:
        cp.start()
    gain_step(3)
    rs_tick(18)
    rs_tick(19)
    rs_tick(20)
    rs_tick(21)
    rs_tick(22)
    for cp in last_out[2:]:
        cp.start()
    rs_tick(23)

    for cp in last_out[:2]:
        cp.start()
    pl.when(has_next)(lambda: rim_copy.wait_send())
    pl.when(has_prev)(lambda: halo_copy.wait_send())

    for i in range(4):
        gain_copy(i).wait_send()
    x_copy.wait_send()
    for i in range(8):
        x_piece(i).wait_send()

    for stage in range(4):
        for k in range(CHUNKS - (2 if stage == 0 else 3), CHUNKS):
            rs_do(wait_send_all, stage, k)

    def drain(k, _):
        for stage in range(4):
            ag_do(wait_send_all, stage, k)
        return 0

    lax.fori_loop(0, CHUNKS, drain, 0)
    mixed_copy.wait()
    dtok_copy.wait()
    for cp in feed_out + last_out:
        cp.wait()


def call_layer(tok, ctx, gain_one, gain_two, cot, weights, delay, lengths):
    f32, bf16 = jnp.float32, jnp.bfloat16
    vm, dma = pltpu.VMEM, pltpu.SemaphoreType.DMA
    shape = jax.ShapeDtypeStruct
    in_vmem, in_hbm, in_smem = (pl.BlockSpec(memory_space=m) for m in (pltpu.VMEM, pltpu.HBM, pltpu.SMEM))
    return pl.pallas_call(
        layer_kernel,
        name="layer",
        out_shape=(
            shape((1024, 1024), bf16),
            shape((1024, 1024), f32),
            shape((128, 512), f32),
            shape((32, 1024), f32),
            shape((8, 1024), f32),
            shape((8, 1024), f32),
            shape((64, 3072), f32),
            shape((64, 1024), f32),
            shape((64, 2816), f32),
            shape((64, 2816), f32),
            shape((176, 1024), f32),
            shape((CHUNKS, 2, 2, 2, 2, 64, WIDE), bf16),
            shape((CHUNKS, 2, 2, 2, 2, 64, WIDE), bf16),
        ),
        in_specs=[in_hbm] + [in_vmem] * 3 + [in_hbm] + [in_vmem] * 3 + [in_hbm] * 3 + [in_smem] * 2,
        out_specs=(in_hbm, in_hbm, in_vmem, in_hbm, in_vmem, in_vmem) + (in_hbm,) * 7,
        scratch_shapes=[
            vm((1024, 1024), bf16),
            vm((64, 2816), bf16),
            vm((64, 2816), bf16),
            vm((176, 1024), bf16),
            vm((CHUNKS, 64, WIDE), bf16),
            vm((1024, 1024), f32),
            vm((1024, 1024), bf16),
            vm((1024, 1024), bf16),
            vm((4, 1024, WIDE), bf16),
            vm((1024, 1024), bf16),
            vm((1024, 1024), f32),
            vm((1024, 1024), bf16),
            vm((1040, 1024), bf16),
            vm((1040, 1024), f32),
            vm((1024, 1024), f32),
            vm((2, 2, 2, 2, 2, 64, WIDE), bf16),
            vm((1024, 256), bf16),
            vm((2, 2, 2, 2, 2, 64, WIDE), bf16),
            vm((2, 2, 2, 2, 64, WIDE), bf16),
            vm((256, 1024), bf16),
            vm((128, 1024), f32),
            vm((16, 1024), f32),
            vm((4, 16, 1024), f32),
            vm((4, 16, 1024), f32),
            vm((2, 128, 1024), bf16),
            vm((2, 128, 1024), bf16),
            vm((2, 2, 2, 2, 64, WIDE), bf16),
            vm((ROUNDS, 4, 64, WIDE), bf16),
            vm((ROUNDS, 2, 64, WIDE), bf16),
            vm((FAR_ROUNDS, 64, WIDE), bf16),
            vm((3, 4, 64, WIDE), bf16),
            vm((3, 4, 64, WIDE), bf16),
            vm((3, 2, 64, WIDE), bf16),
            vm((3, 2, 64, WIDE), bf16),
            vm((3, 64, WIDE), bf16),
            vm((3, 64, WIDE), bf16),
            vm((FEED, 64, WIDE), f32),
            dma((6, CHUNKS)),
            dma((6, CHUNKS)),
            dma((6, 3)),
            dma((6, FAR_ROUNDS)),
            dma((9,)),
            dma((9,)),
            dma((4,)),
            dma((4,)),
            dma((2,)),
            dma((2, 4)),
            dma((2,)),
            dma((2,)),
            dma,
            dma((4,)),
            dma((2,)),
            dma((2,)),
            dma((14,)),
        ],
        compiler_params=pltpu.CompilerParams(
            collective_id=0, has_side_effects=True, vmem_limit_bytes=63 * 1024 * 1024
        ),
    )(tok, ctx, gain_one, gain_two, cot, *weights, delay, lengths)


def copy_kernel(*refs):
    n = (len(refs) - 2) // 3
    srcs, dsts, held, in_sem, out_sem = refs[:n], refs[n : 2 * n], refs[2 * n : 3 * n], refs[-2], refs[-1]
    ins = [pltpu.make_async_copy(srcs[i], held[i], in_sem.at[i]) for i in range(n)]
    outs = [pltpu.make_async_copy(held[i], dsts[i], out_sem.at[i]) for i in range(n)]
    for cp in ins:
        cp.start()
    for cp_in, cp_out in zip(ins, outs):
        cp_in.wait()
        cp_out.start()
    for cp in outs:
        cp.wait()


def copy_all(arrays):
    n = len(arrays)
    hbm = pl.BlockSpec(memory_space=pltpu.HBM)
    return pl.pallas_call(
        copy_kernel,
        name="outputs",
        out_shape=tuple(jax.ShapeDtypeStruct(a.shape, a.dtype) for a in arrays),
        in_specs=[hbm] * n,
        out_specs=(hbm,) * n,
        scratch_shapes=[pltpu.VMEM(a.shape, a.dtype) for a in arrays]
        + [pltpu.SemaphoreType.DMA((n,)), pltpu.SemaphoreType.DMA((n,))],
        compiler_params=pltpu.CompilerParams(vmem_limit_bytes=63 * 1024 * 1024),
    )(*arrays)


def body_kernel(
    tokens,
    context,
    ctx_weight,
    delay,
    lengths,
    attn_gain,
    ffn_gain,
    qkv_weight,
    out_weight,
    gate_weight,
    up_weight,
    down_weight,
    cotangent,
):
    frame_count, positions, width = tokens.shape[1:]
    rows = frame_count * positions
    weights = (ctx_weight, qkv_weight[0], out_weight[0], gate_weight[0], up_weight[0], down_weight[0])
    mixed_out, d_tokens, d_context, d_ctx, d_gain_one, d_gain_two, *grads = call_layer(
        tokens.reshape(rows, width),
        context,
        attn_gain[0],
        ffn_gain[0],
        cotangent.reshape(rows, width),
        weights,
        delay,
        lengths,
    )
    mixed_out, d_tokens, d_context, d_ctx, d_gain_one, d_gain_two, *grads = copy_all(
        (mixed_out, d_tokens, d_context, d_ctx, d_gain_one, d_gain_two, *grads[:-2])
    )
    d_qkv, d_out, d_gate, d_up, d_down = grads
    return (
        mixed_out.reshape(tokens.shape),
        d_tokens.reshape(tokens.shape),
        d_context,
        d_ctx,
        d_gain_one[None],
        d_gain_two[None],
        d_qkv[None],
        d_out[None],
        d_gate[None],
        d_up[None],
        d_down[None],
    )


def body(
    tokens,
    context,
    ctx_weight,
    delay,
    lengths,
    attn_gain,
    ffn_gain,
    qkv_weight,
    out_weight,
    gate_weight,
    up_weight,
    down_weight,
    cotangent,
):
    frame_count = tokens.shape[1]
    positions = tokens.shape[2]
    model_width = tokens.shape[3]
    token_rows = frame_count * positions
    head_scale = HEAD ** (-0.5)
    ctx_full = lax.all_gather(context, "stream", axis=1, tiled=True)
    ctx_rows = lax.all_gather(ctx_weight, ("stream", "frames"), axis=0, tiled=True)
    shift_term = flat_dot(ctx_full, ctx_rows)
    inputs = tokens[0]
    rim_rows = shifted(inputs[frame_count - 2 :], "frames", 1)
    extended = jnp.concatenate([rim_rows, inputs], axis=0).astype(jnp.float32)
    frame_ids = lax.axis_index("frames") * frame_count + jnp.arange(frame_count, dtype=jnp.int32)
    chosen, valid_rows = shift_tables(delay, lengths, frame_ids)
    layer_in = jnp.broadcast_to(shift_term[:, None, :], (frame_count, positions, model_width))
    for offset in range(3):
        piece = extended[2 - offset : 2 - offset + frame_count]
        layer_in = (
            layer_in + chosen[offset][None, :, None] * valid_rows[offset][:, None, None] * piece
        )
    weights = (
        lax.all_gather(qkv_weight[0], "frames", axis=0, tiled=True),
        lax.all_gather(out_weight[0], "frames", axis=0, tiled=True),
        lax.all_gather(gate_weight[0], "frames", axis=0, tiled=True),
        lax.all_gather(up_weight[0], "frames", axis=0, tiled=True),
        lax.all_gather(down_weight[0], "frames", axis=0, tiled=True),
    )
    w_qkv, w_out, w_gate, w_up, w_down = weights
    gain_one = attn_gain[0].astype(jnp.float32)
    gain_two = ffn_gain[0].astype(jnp.float32)
    normed = norm_rows(layer_in, gain_one).astype(jnp.bfloat16).reshape(token_rows, model_width)
    qkv = (
        flat_dot(normed, w_qkv).astype(jnp.bfloat16).reshape(frame_count, positions, 3, HEADS, HEAD)
    )
    queries = qkv[:, :, 0]
    key_part = qkv[:, :, 1]
    values = qkv[:, :, 2]
    scores = (
        jnp.einsum("fqhd,fkhd->fhqk", queries, key_part, preferred_element_type=jnp.float32)
        * head_scale
    )
    causal = jnp.arange(positions)[:, None] >= jnp.arange(positions)[None, :]
    scores = jnp.where(causal[None, None], scores, -1e30)
    probs = jax.nn.softmax(scores, axis=-1)
    probs_low = probs.astype(jnp.bfloat16)
    mixed = jnp.einsum("fhqk,fkhd->fqhd", probs_low, values, preferred_element_type=jnp.float32)
    mixed = mixed.astype(jnp.bfloat16).reshape(token_rows, model_width)
    after_attn = layer_in + flat_dot(mixed, w_out).reshape(frame_count, positions, model_width)
    normed_two = (
        norm_rows(after_attn, gain_two).astype(jnp.bfloat16).reshape(token_rows, model_width)
    )
    gate_pre = flat_dot(normed_two, w_gate)
    up_pre = flat_dot(normed_two, w_up)
    hidden = (jax.nn.silu(gate_pre) * up_pre).astype(jnp.bfloat16)
    out_full = after_attn + flat_dot(hidden, w_down).reshape(frame_count, positions, model_width)
    b_qkv, b_out, b_gate, b_up, b_down = weights
    grad_out = cotangent[0].astype(jnp.float32)
    grad_ff = grad_out.reshape(token_rows, model_width).astype(jnp.bfloat16)
    grad_down = trans_dot(hidden, grad_ff)
    grad_hidden = back_dot(grad_ff, b_down)
    sigmoid_gate = jax.nn.sigmoid(gate_pre)
    grad_gate = (
        grad_hidden * up_pre * sigmoid_gate * (1.0 + gate_pre * (1.0 - sigmoid_gate))
    ).astype(jnp.bfloat16)
    grad_up = (grad_hidden * gate_pre * sigmoid_gate).astype(jnp.bfloat16)
    grad_gate_w = trans_dot(normed_two, grad_gate)
    grad_up_w = trans_dot(normed_two, grad_up)
    grad_normed_two = (back_dot(grad_gate, b_gate) + back_dot(grad_up, b_up)).reshape(
        frame_count, positions, model_width
    )
    grad_after_norm, grad_gain_two = norm_back(grad_normed_two, after_attn, gain_two)
    grad_after = grad_out + grad_after_norm
    grad_branch = grad_after.reshape(token_rows, model_width).astype(jnp.bfloat16)
    grad_out_w = trans_dot(mixed, grad_branch)
    grad_mixed = (
        back_dot(grad_branch, b_out)
        .astype(jnp.bfloat16)
        .reshape(frame_count, positions, HEADS, HEAD)
    )
    grad_values = jnp.einsum(
        "fhqk,fqhd->fkhd", probs_low, grad_mixed, preferred_element_type=jnp.float32
    )
    grad_probs = jnp.einsum(
        "fqhd,fkhd->fhqk", grad_mixed, values, preferred_element_type=jnp.float32
    )
    grad_scores = (
        probs * (grad_probs - jnp.sum(grad_probs * probs, axis=-1, keepdims=True))
    ).astype(jnp.bfloat16)
    grad_queries = (
        jnp.einsum("fhqk,fkhd->fqhd", grad_scores, key_part, preferred_element_type=jnp.float32)
        * head_scale
    )
    grad_keys = (
        jnp.einsum("fhqk,fqhd->fkhd", grad_scores, queries, preferred_element_type=jnp.float32)
        * head_scale
    )
    grad_qkv = jnp.stack([grad_queries, grad_keys, grad_values], axis=2).astype(jnp.bfloat16)
    grad_qkv = grad_qkv.reshape(token_rows, 3 * model_width)
    grad_qkv_w = trans_dot(normed, grad_qkv)
    all_parts = (
        lax.psum_scatter(grad_qkv_w, "frames", scatter_dimension=0, tiled=True),
        lax.psum_scatter(grad_out_w, "frames", scatter_dimension=0, tiled=True),
        lax.psum_scatter(grad_gate_w, "frames", scatter_dimension=0, tiled=True),
        lax.psum_scatter(grad_up_w, "frames", scatter_dimension=0, tiled=True),
        lax.psum_scatter(grad_down, "frames", scatter_dimension=0, tiled=True),
    )
    d_qkv_rows, d_out_rows, d_gate_rows, d_up_rows, d_down_rows = all_parts
    grad_normed = back_dot(grad_qkv, b_qkv).reshape(frame_count, positions, model_width)
    grad_in_norm, grad_gain_one = norm_back(grad_normed, layer_in, gain_one)
    grad_in = grad_after + grad_in_norm
    gain_sums = lax.psum((grad_gain_one, grad_gain_two), "frames")
    grad_shift = jnp.sum(grad_in, axis=1).astype(jnp.bfloat16)
    grad_ctx_w = trans_dot(ctx_full, grad_shift)
    ctx_w_rows = lax.psum_scatter(grad_ctx_w, ("stream", "frames"), scatter_dimension=0, tiled=True)
    grad_context = back_dot(grad_shift, ctx_rows)
    context_half = lax.psum_scatter(
        grad_context.astype(jnp.bfloat16), "stream", scatter_dimension=1, tiled=True
    ).astype(jnp.float32)
    grad_ext = jnp.zeros((frame_count + 2, positions, model_width), jnp.float32)
    for offset in range(3):
        term = chosen[offset][None, :, None] * valid_rows[offset][:, None, None] * grad_in
        grad_ext = grad_ext + jnp.pad(term, ((2 - offset, offset), (0, 0), (0, 0)))
    back_rows = shifted(grad_ext[:2].astype(jnp.bfloat16), "frames", -1).astype(jnp.float32)
    grad_tokens = grad_ext[2:].at[frame_count - 2 :].add(back_rows)
    return (
        out_full.astype(jnp.bfloat16)[None],
        grad_tokens[None],
        context_half,
        ctx_w_rows,
        gain_sums[0][None],
        gain_sums[1][None],
        d_qkv_rows[None],
        d_out_rows[None],
        d_gate_rows[None],
        d_up_rows[None],
        d_down_rows[None],
    )


def solution(mesh):
    fits = mesh.shape["frames"] == 16 and mesh.shape["stream"] == 2
    return jax.shard_map(
        body_kernel if fits else body,
        mesh=mesh,
        in_specs=(
            P("stream", "frames", None, None),
            P("frames", "stream"),
            P(("stream", "frames"), None),
            P(),
            P(),
            P("stream", None, None),
            P("stream", None, None),
            P("stream", "frames", None),
            P("stream", "frames", None),
            P("stream", "frames", None),
            P("stream", "frames", None),
            P("stream", "frames", None),
            P("stream", "frames", None, None),
        ),
        out_specs=(
            P("stream", "frames", None, None),
            P("stream", "frames", None, None),
            P("frames", "stream"),
            P(("stream", "frames"), None),
            P("stream", None, None),
            P("stream", None, None),
            P("stream", "frames", None),
            P("stream", "frames", None),
            P("stream", "frames", None),
            P("stream", "frames", None),
            P("stream", "frames", None),
        ),
        check_vma=False,
    )
```
